32 devices in a mesh: grp: 8 (over z, y), tp: 4 (over x, core).
Axes of the slice: x: 2, y: 2, z: 4, core: 2. Of those that a mesh axis runs over, the one named last changes fastest.
Arguments:
- tokens: bfloat16 [8, 3136, 512], P(None, 'grp'), may hold values from -6 to 6
- grad_out: bfloat16 [8, 3136, 512], P(None, 'grp'), may hold values from -6 to 6
- ln1_gain: bfloat16 [512], P('grp'), may hold values from 0.5 to 1.5
- ln1_shift: bfloat16 [512], P('grp'), may hold values from -3 to 3
- w_qkv: bfloat16 [512, 3, 512], P('grp', None, 'tp'), may hold values from -0.25 to 0.25
- qkv_bias: bfloat16 [2, 512], P(None, 'tp'), may hold values from -3 to 3
- rel_table: bfloat16 [2535, 16], P(None, 'tp'), may hold values from -4 to 4
- w_proj: bfloat16 [512, 512], P('grp', 'tp'), may hold values from -2 to 2
- proj_bias: bfloat16 [512], P('grp'), may hold values from -3 to 3
- ln2_gain: bfloat16 [512], P('grp'), may hold values from 0.5 to 1.5
- ln2_shift: bfloat16 [512], P('grp'), may hold values from -3 to 3
- w_in: bfloat16 [512, 2048], P('grp', 'tp'), may hold values from -0.25 to 0.25
- in_bias: bfloat16 [2048], P('tp'), may hold values from -3 to 3
- w_out: bfloat16 [512, 2048], P('grp', 'tp'), may hold values from -0.125 to 0.125
- out_bias: bfloat16 [512], P('grp'), may hold values from -3 to 3
Outputs:
- output: bfloat16 [8, 3136, 512], P(None, 'grp')
- grad_tokens: float32 [8, 3136, 512], P(None, 'grp')
- grad_ln1_gain: float32 [512], P('grp')
- grad_ln1_shift: float32 [512], P('grp')
- grad_w_qkv: float32 [512, 3, 512], P('grp', None, 'tp')
- grad_qkv_bias: float32 [2, 512], P(None, 'tp')
- grad_rel_table: float32 [2535, 16], P(None, 'tp')
- grad_w_proj: float32 [512, 512], P('grp', 'tp')
- grad_proj_bias: float32 [512], P('grp')
- grad_ln2_gain: float32 [512], P('grp')
- grad_ln2_shift: float32 [512], P('grp')
- grad_w_in: float32 [512, 2048], P('grp', 'tp')
- grad_in_bias: float32 [2048], P('tp')
- grad_w_out: float32 [512, 2048], P('grp', 'tp')
- grad_out_bias: float32 [512], P('grp')
The draws below stay inside these ranges and needn't reach their ends.
All inputs are finite; a program needn't handle non-finite values.
Results may differ from the reference program's by a relative error of at most 0.011.
Values may be sent and summed in bfloat16 or wider, within the bound.
No kernel may reach another device: no remote copies, remote signals or barrier semaphores. Data moves between devices by JAX's collectives and lax.ppermute only.
A program may use at most 256 MiB of HBM per device.

```python
import jax
import jax.numpy as jnp
from jax import lax

D = 512
HEADS = 16
HD = 32
FF = 2048
CT = 16
CH = 14
CW = 14
WT = 8
WH = 7
WW = 7
ST = 4
SH = 3
SW = 3
POS = 3136
WIN = 392
NWIN = 8
RB = 2535
CLIPS = 8


def block_levels(stream_key, shape, shards, low, high):
    loudness, own = 1.0, jax.random.fold_in(stream_key, 6)
    for dim, parts in shards:
        draws = jnp.exp(jax.random.uniform(jax.random.fold_in(own, dim), (parts,), jnp.float32, low / len(shards), high / len(shards)))
        loudness = loudness * jnp.repeat(draws, shape[dim] // parts).reshape([-1 if axis == dim else 1 for axis in range(len(shape))])
    return loudness


def scatter_about(own_key, shape, scale, bound, pieces=(), held_as=jnp.bfloat16):
    loudness = block_levels(own_key, shape, pieces, -0.22, 0.18) if pieces else 1.0
    entries = jax.random.normal(own_key, shape, jnp.float32) * scale * loudness
    return jnp.minimum(jnp.maximum(entries, -bound), bound).astype(held_as)


def setup_inputs(seed: int = 0) -> dict:
    key_of = jax.random.split(jax.random.key(seed), 16)
    tokens = scatter_about(key_of[0], (CLIPS, POS, D), 1.0, 6.0, ((1, 8),))
    grad_out = scatter_about(key_of[1], (CLIPS, POS, D), 1.0, 6.0, ((1, 8),))
    ln1_gain = jnp.clip(1.0 + 0.1 * jax.random.normal(key_of[2], (D,), jnp.float32), 0.5, 1.5).astype(jnp.bfloat16)
    ln1_shift = scatter_about(key_of[3], (D,), 0.5, 3.0, ((0, 8),))
    w_qkv = scatter_about(key_of[4], (D, 3, D), D ** -0.5, 0.25, ((0, 8), (2, 4)))
    qkv_bias = scatter_about(key_of[5], (2, D), 0.5, 3.0, ((1, 4),))
    rel_table = scatter_about(key_of[6], (RB, HEADS), 1.0, 4.0, ((1, 4),))
    w_proj = scatter_about(key_of[7], (D, D), (max(D // 64, 4)) ** -0.5, 2.0, ((0, 8), (1, 4)))
    proj_bias = scatter_about(key_of[8], (D,), 0.5, 3.0, ((0, 8),))
    ln2_gain = jnp.clip(1.0 + 0.1 * jax.random.normal(key_of[9], (D,), jnp.float32), 0.5, 1.5).astype(jnp.bfloat16)
    ln2_shift = scatter_about(key_of[10], (D,), 0.5, 3.0, ((0, 8),))
    w_in = scatter_about(key_of[11], (D, FF), D ** -0.5, 0.25, ((0, 8), (1, 4)))
    in_bias = scatter_about(key_of[12], (FF,), 0.5, 3.0, ((0, 4),))
    w_out = scatter_about(key_of[13], (D, FF), FF ** -0.5, 0.125, ((0, 8), (1, 4)))
    out_bias = scatter_about(key_of[14], (D,), 0.5, 3.0, ((0, 8),))
    return {"tokens": tokens, "grad_out": grad_out, "ln1_gain": ln1_gain, "ln1_shift": ln1_shift, "w_qkv": w_qkv, "qkv_bias": qkv_bias, "rel_table": rel_table, "w_proj": w_proj, "proj_bias": proj_bias, "ln2_gain": ln2_gain, "ln2_shift": ln2_shift, "w_in": w_in, "in_bias": in_bias, "w_out": w_out, "out_bias": out_bias}


@jax.custom_vjp
def low(v):
    return lax.optimization_barrier(v.astype(jnp.bfloat16)).astype(jnp.float32)

@jax.custom_vjp
def low_back(v):
    return v

def low_keep(v):
    return (low(v), None)

def low_pass(kept, grad):
    return (grad,)

def back_keep(v):
    return (v, None)

def back_low(kept, grad):
    return (low(grad),)
low.defvjp(low_keep, low_pass)
low_back.defvjp(back_keep, back_low)

def normalize(token_rows, gain, offset):
    row_mean = lax.optimization_barrier(jnp.mean(token_rows, axis=-1, keepdims=True))
    centered = token_rows - row_mean
    variance = lax.optimization_barrier(jnp.mean(centered * centered, axis=-1, keepdims=True))
    return centered * lax.rsqrt(variance + 1e-05) * gain + offset

def to_windows(field):
    clip_count = field.shape[0]
    features = field.shape[-1]
    grid_cells = field.reshape(clip_count, CT, CH, CW, features)
    grid_cells = jnp.roll(grid_cells, (-ST, -SH, -SW), axis=(1, 2, 3))
    grid_cells = grid_cells.reshape(clip_count, CT // WT, WT, CH // WH, WH, CW // WW, WW, features)
    grid_cells = grid_cells.transpose(0, 1, 3, 5, 2, 4, 6, 7)
    return grid_cells.reshape(clip_count * NWIN, WIN, features)

def from_windows(windows, clip_count):
    features = windows.shape[-1]
    grid_cells = windows.reshape(clip_count, CT // WT, CH // WH, CW // WW, WT, WH, WW, features)
    grid_cells = grid_cells.transpose(0, 1, 4, 2, 5, 3, 6, 7).reshape(clip_count, CT, CH, CW, features)
    grid_cells = jnp.roll(grid_cells, (ST, SH, SW), axis=(1, 2, 3))
    return grid_cells.reshape(clip_count, CT * CH * CW, features)

def region_part(extent, window, offset):
    places = jnp.arange(extent)
    return jnp.where(places < extent - window, 0, jnp.where(places < extent - offset, 1, 2)).astype(jnp.int32)

def window_mask():
    regions = region_part(CT, WT, ST)[:, None, None] * 9 + region_part(CH, WH, SH)[None, :, None] * 3 + region_part(CW, WW, SW)[None, None, :]
    grid_cells = regions.reshape(CT // WT, WT, CH // WH, WH, CW // WW, WW).transpose(0, 2, 4, 1, 3, 5)
    grid_cells = grid_cells.reshape(NWIN, WIN)
    return grid_cells[:, :, None] == grid_cells[:, None, :]

def relative_index():
    places = jnp.arange(WIN)
    frames = places // (WH * WW)
    rows_of = places // WW % WH
    column = places % WW
    return (((frames[:, None] - frames[None, :] + WT - 1) * (2 * WH - 1) + rows_of[:, None] - rows_of[None, :] + WH - 1) * (2 * WW - 1) + column[:, None] - column[None, :] + WW - 1).astype(jnp.int32)

def clip_layer(params, clip_rows):
    ln1_gain, ln1_shift, w_qkv, qkv_bias, rel_table, w_proj, proj_bias, ln2_gain, ln2_shift, w_in, in_bias, w_out, out_bias = params
    normed = low(normalize(clip_rows, ln1_gain, ln1_shift))
    projected = jnp.einsum('pd,dkf->pkf', normed, w_qkv, precision=lax.Precision.HIGHEST)
    query_rows = low(low_back(projected[:, 0] + qkv_bias[0]))
    key_rows = low(low_back(projected[:, 1]))
    value_rows = low(low_back(projected[:, 2] + qkv_bias[1]))

    def split_heads(field):
        return to_windows(field[None]).reshape(NWIN, WIN, HEADS, HD)
    query_w = split_heads(query_rows)
    key_w = split_heads(key_rows)
    value_w = split_heads(value_rows)
    pos_bias = jnp.take(rel_table, relative_index().reshape(-1), axis=0).reshape(WIN, WIN, HEADS).transpose(2, 0, 1)
    scores = jnp.einsum('wqhd,wkhd->whqk', query_w, key_w, precision=lax.Precision.HIGHEST) * HD ** (-0.5) + pos_bias[None]
    scores = low_back(jnp.where(window_mask()[:, None], scores, -1000000000.0))
    weights = low(jax.nn.softmax(scores, axis=-1))
    attended = jnp.einsum('whqk,wkhd->wqhd', weights, value_w, precision=lax.Precision.HIGHEST).reshape(NWIN, WIN, D)
    attended = low(low_back(from_windows(attended, 1)[0]))
    branch = low_back(jnp.dot(attended, w_proj.T, precision=lax.Precision.HIGHEST) + proj_bias)
    hidden_one = clip_rows + branch
    normed_two = low(normalize(hidden_one, ln2_gain, ln2_shift))
    inner_act = low_back(jnp.dot(normed_two, w_in, precision=lax.Precision.HIGHEST) + in_bias)
    activated = low(jax.nn.gelu(inner_act, approximate=False))
    return hidden_one + jnp.dot(activated, w_out.T, precision=lax.Precision.HIGHEST) + out_bias

def reference(tokens, grad_out, ln1_gain, ln1_shift, w_qkv, qkv_bias, rel_table, w_proj, proj_bias, ln2_gain, ln2_shift, w_in, in_bias, w_out, out_bias):
    params = tuple((item.astype(jnp.float32) for item in (ln1_gain, ln1_shift, w_qkv, qkv_bias, rel_table, w_proj, proj_bias, ln2_gain, ln2_shift, w_in, in_bias, w_out, out_bias)))

    def full_layer(params, field):

        def one_clip(clip_rows):
            return clip_layer(params, clip_rows)
        return lax.map(jax.checkpoint(one_clip), field)
    output, pullback = jax.vjp(full_layer, params, tokens.astype(jnp.float32))
    param_grads, token_grad = pullback(grad_out.astype(jnp.float32))
    return (output.astype(jnp.bfloat16), token_grad, param_grads[0], param_grads[1], param_grads[2], param_grads[3], param_grads[4], param_grads[5], param_grads[6], param_grads[7], param_grads[8], param_grads[9], param_grads[10], param_grads[11], param_grads[12])
```

```python
import functools

import jax
import jax.numpy as jnp
from jax import lax
from jax.experimental import pallas as pl
from jax.experimental.pallas import tpu as pltpu
from jax.sharding import PartitionSpec as P

CT, CH, CW = 16, 14, 14
WT, WH, WW = 8, 7, 7
ST, SH, SW = 4, 3, 3
FRAME = CH * CW
SIDE = WH * WW
WIN = WT * SIDE
PAIR = 2
PADDED = -(-WIN // 16) * 16
ROWS = PAIR * PADDED
HEAD = 32
GROUP = 128
HEADS_IN = GROUP // HEAD
SPAN_T, SPAN_H, SPAN_W = 2 * WT - 1, 2 * WH - 1, 2 * WW - 1
PLANE = SPAN_H * SPAN_W
TABLE = SPAN_T * PLANE
TABLE_PAD = -(-TABLE // 128) * 128
DIAG = SPAN_T * SIDE
DIAG_PAD = -(-DIAG // 128) * 128
SIDE_PAD = -(-SIDE // 8) * 8
CORNER = PLANE // 2
LOG2E = 1.4426950408889634
SCALE = HEAD ** (-0.5)
FAR = -(2.0**100)
f32 = jnp.float32
bf16 = jnp.bfloat16
PARAMS = functools.partial(pltpu.CompilerParams, vmem_limit_bytes=56 * 1024 * 1024)


def cost(micros):
    return pl.CostEstimate(flops=int(micros * 1.1e9), bytes_accessed=1 << 20, transcendentals=0)


def dot(a, b):
    return lax.dot_general(a, b, (((1,), (0,)), ((), ())), preferred_element_type=f32)


def dot_t(a, b):
    return lax.dot_general(a, b, (((1,), (1,)), ((), ())), preferred_element_type=f32)


def moments(rows):
    centered = rows - jnp.mean(rows, axis=-1, keepdims=True)
    inverse = lax.rsqrt(jnp.mean(centered * centered, axis=-1, keepdims=True) + 1e-05)
    return centered * inverse, inverse


def norm_back(grad, unit, inverse, gain):
    scaled = grad * gain
    shared = jnp.mean(scaled, axis=-1, keepdims=True)
    along = jnp.mean(scaled * unit, axis=-1, keepdims=True)
    return inverse * (scaled - shared - unit * along)


def bias_kernel(table_ref, pick_ref, bias_ref, sheared, spread):
    heads = table_ref.shape[0]
    row_of = lax.broadcasted_iota(jnp.int32, (8, TABLE_PAD), 0)
    for head in range(heads):
        flat = jnp.broadcast_to(table_ref[head], (8, TABLE_PAD))
        stairs = flat
        for step in range(1, WW):
            stairs = jnp.where(row_of == step, pltpu.roll(flat, step, 1), stairs)
        for row in range(WH):
            shift = (row * SPAN_W - CORNER) % TABLE_PAD
            sheared[head, pl.ds(row * WW, 8), :] = pltpu.roll(stairs, shift, 1)
    everything = sheared[...].reshape(heads * SIDE_PAD, TABLE_PAD).astype(bf16)
    spread[...] = dot(everything, pick_ref[...]).reshape(heads, SIDE_PAD, DIAG_PAD) * LOG2E
    for head in range(heads):
        block = spread[head]
        for frame in range(WT):
            shift = -(WT - 1 - frame) * SIDE % DIAG_PAD
            moved = pltpu.roll(block, shift, 1) if shift else block
            bias_ref[head, pl.ds(frame * SIDE, SIDE_PAD), :] = moved[:, :PADDED]


def table_kernel(sums_ref, pick_ref, grad_ref, spread, sheared):
    heads = sums_ref.shape[0]
    row_of = lax.broadcasted_iota(jnp.int32, (SIDE_PAD, DIAG_PAD), 0)
    lane_of = lax.broadcasted_iota(jnp.int32, (SIDE_PAD, DIAG_PAD), 1)
    blank = jnp.zeros((SIDE_PAD, DIAG_PAD - PADDED), f32)
    for head in range(heads):
        total = jnp.zeros((SIDE_PAD, DIAG_PAD), f32)
        for frame in range(WT):
            piece = sums_ref[head, pl.ds(frame * SIDE, SIDE_PAD), :]
            piece = jnp.concatenate([piece, blank], axis=1)
            piece = jnp.where(lane_of < WIN, piece, 0.0)
            shift = (WT - 1 - frame) * SIDE
            total = total + (pltpu.roll(piece, shift, 1) if shift else piece)
        spread[head] = jnp.where(row_of < SIDE, total, 0.0)
    everything = spread[...].reshape(heads * SIDE_PAD, DIAG_PAD)
    high = everything.astype(bf16)
    low = (everything - high.astype(f32)).astype(bf16)
    grads = dot_t(high, pick_ref[...]) + dot_t(low, pick_ref[...])
    sheared[...] = grads.reshape(heads, SIDE_PAD, TABLE_PAD)
    row_in = lax.broadcasted_iota(jnp.int32, (8, TABLE_PAD), 0)
    for head in range(heads):
        stairs = jnp.zeros((8, TABLE_PAD), f32)
        for row in range(WH):
            shift = (CORNER - row * SPAN_W) % TABLE_PAD
            stairs = stairs + pltpu.roll(sheared[head, pl.ds(row * WW, 8), :], shift, 1)
        flat = jnp.where(row_in == 0, stairs, 0.0)
        for step in range(1, WW):
            moved = pltpu.roll(stairs, TABLE_PAD - step, 1)
            flat = flat + jnp.where(row_in == step, moved, 0.0)
        grad_ref[head] = jnp.sum(flat, axis=0, keepdims=True)


def attention_kernel(first, *refs):
    if first:
        x_ref, gain_ref, shift_ref, w_ref, wb_ref, bias_ref, qf_ref, kf_ref = refs[:8]
        a1_ref, a1_t_ref, qkv_ref, o_ref, lse_ref = refs[8:]
        unit, _ = moments(x_ref[...].astype(f32))
        low = unit * gain_ref[...] + shift_ref[...]
        a1_ref[...] = low.astype(bf16)
        a1_t_ref[...] = low.T.astype(bf16)
    else:
        a1_ref, w_ref, wb_ref, bias_ref, qf_ref, kf_ref = refs[:6]
        qkv_ref, o_ref, lse_ref = refs[6:]
    qkv_ref[...] = (dot(a1_ref[...], w_ref[...]) + wb_ref[...]).astype(bf16)
    lane = lax.broadcasted_iota(jnp.int32, (PADDED, GROUP), 1) // HEAD
    for window in range(PAIR):
        rows = slice(window * PADDED, (window + 1) * PADDED)
        query = qkv_ref[rows, 0:GROUP]
        key = qkv_ref[rows, GROUP : 2 * GROUP]
        value = qkv_ref[rows, 2 * GROUP : 3 * GROUP]
        query = jnp.concatenate([query, qf_ref[window]], axis=1)
        value_t = value.astype(f32).T.astype(bf16)
        parts = []
        for head in range(HEADS_IN):
            own = jnp.where(lane == head, key, jnp.zeros_like(key))
            own = jnp.concatenate([own, kf_ref[window]], axis=1)
            logits = dot_t(own, query) * (SCALE * LOG2E) + bias_ref[head]
            top = jnp.max(logits, axis=0, keepdims=True)
            probs = jnp.exp2(logits - top)
            total = jnp.sum(probs, axis=0, keepdims=True)
            lse_ref[pl.ds(window * HEADS_IN + head, 1), :] = top + jnp.log2(total)
            mixed = dot(value_t[head * HEAD : (head + 1) * HEAD], probs.astype(bf16))
            parts.append(mixed / total)
        o_ref[rows, :] = jnp.concatenate(parts, axis=0).T.astype(bf16)


def mlp_kernel(
    x_ref, o0_ref, o1_ref, o2_ref, o3_ref, g_ref, home_in, away_in, home_out, away_out,
    pb_ref, gain_ref, shift_ref, ib_ref, ob_ref,
    out_ref, dh_ref, dow_ref, gwi_keep, gwi_send, gwo_keep, gwo_send, gwp_keep, gwp_send,
    gib_ref, vec_ref,
    hidden, a2, a2_t, g_t, unit_s, inv_s, acc_out, acc_in, o_all, wp, wi, wo,
):
    step = pl.program_id(0)
    width = x_ref.shape[1]
    units = home_out.shape[2]

    @pl.when(step == 0)
    def _():
        for i, (o_ref, w_ref, j) in enumerate(
            [(o0_ref, home_in, 0), (o1_ref, away_in, 0), (o2_ref, home_in, 1), (o3_ref, away_in, 1)]
        ):
            o_all[:, i * GROUP : (i + 1) * GROUP] = o_ref[...]
            wp[:, i * GROUP : (i + 1) * GROUP] = w_ref[j, :, units : units + GROUP]
        branch = dot_t(o_all[...], wp[...])
        hidden[...] = x_ref[...].astype(f32) + branch + pb_ref[...]
        unit, inverse = moments(hidden[...])
        unit_s[...] = unit
        inv_s[...] = inverse
        low = unit * gain_ref[...] + shift_ref[...]
        a2[...] = low.astype(bf16)
        a2_t[...] = low.T.astype(bf16)
        g_t[...] = g_ref[...].astype(f32).T.astype(bf16)
        acc_out[...] = jnp.zeros_like(acc_out)
        acc_in[...] = jnp.zeros_like(acc_in)

    for place, (in_ref, out_w, j) in enumerate(
        [(away_in, away_out, 0), (away_in, away_out, 1), (home_in, home_out, 0), (home_in, home_out, 1)]
    ):

        @pl.when(step == place)
        def _():
            wi[...] = in_ref[j, :, 0:units]
            wo[...] = out_w[j]

    u = dot(a2[...], wi[...]) + ib_ref[0]
    half = 0.5 * (1.0 + lax.erf(u * (0.5**0.5)))
    act = (u * half).astype(bf16)
    acc_out[...] += dot_t(act, wo[...])
    back = dot(g_ref[...], wo[...])
    slope = half + u * jnp.exp(-0.5 * u * u) * 0.3989422804014327
    du_low = (back * slope).astype(bf16)
    acc_in[...] += dot_t(du_low, wi[...])
    grad_out_w = dot(g_t[...], act)
    grad_in_w = dot(a2_t[...], du_low)
    gib_ref[0] = jnp.sum(du_low.astype(f32), axis=0, keepdims=True)

    @pl.when(step < 2)
    def _():
        gwo_send[0] = grad_out_w.astype(bf16)
        gwi_send[0] = grad_in_w.astype(bf16)

    @pl.when(step >= 2)
    def _():
        gwo_keep[0] = grad_out_w
        gwi_keep[0] = grad_in_w

    @pl.when(step == pl.num_programs(0) - 1)
    def _():
        out_ref[...] = (hidden[...] + acc_out[...] + ob_ref[...]).astype(bf16)
        upstream = g_ref[...].astype(f32)
        grad = acc_in[...]
        unit = unit_s[...]
        dh = upstream + norm_back(grad, unit, inv_s[...], gain_ref[...])
        dh_ref[...] = dh
        dz = dh.astype(bf16)
        dow_ref[...] = dot(dz, wp[...]).astype(bf16)
        grad_wp = dot(dz.astype(f32).T.astype(bf16), o_all[...])
        for i in range(2):
            gwp_keep[i] = grad_wp[:, 2 * i * GROUP : (2 * i + 1) * GROUP]
            gwp_send[i] = grad_wp[:, (2 * i + 1) * GROUP : (2 * i + 2) * GROUP].astype(bf16)
        vec_ref[...] = jnp.concatenate(
            [
                jnp.sum(grad * unit, axis=0, keepdims=True),
                jnp.sum(grad, axis=0, keepdims=True),
                jnp.sum(dz.astype(f32), axis=0, keepdims=True),
                jnp.sum(upstream, axis=0, keepdims=True),
            ],
            axis=0,
        )


def attention_back_kernel(
    first, last, a1_t_ref, w_ref, qkv_ref, dow_ref, lse_ref, bias_ref, qf_ref, kf_ref, *refs
):
    if last:
        acc_ref, x_ref, gain_ref, dh_ref, gx_ref, vec_ref, gw_ref, gb_ref, sums_ref, dqkv = refs
    elif first:
        out_ref, gw_ref, gb_ref, sums_ref, dqkv = refs
    else:
        acc_ref, out_ref, gw_ref, gb_ref, sums_ref, dqkv = refs
    lane = lax.broadcasted_iota(jnp.int32, (PADDED, GROUP), 1) // HEAD
    for window in range(PAIR):
        rows = slice(window * PADDED, (window + 1) * PADDED)
        query = qkv_ref[rows, 0:GROUP]
        key = qkv_ref[rows, GROUP : 2 * GROUP]
        value = qkv_ref[rows, 2 * GROUP : 3 * GROUP]
        dow = dow_ref[rows, :]
        query_f = jnp.concatenate([query, qf_ref[window]], axis=1)
        key_t = key.astype(f32).T.astype(bf16)
        none = jnp.zeros((PADDED, GROUP), f32)
        dk, dv, dq_t = none, none, []
        for head in range(HEADS_IN):
            mine = lane == head
            own = jnp.where(mine, key, jnp.zeros_like(key))
            own = jnp.concatenate([own, kf_ref[window]], axis=1)
            logits = dot_t(own, query_f) * (SCALE * LOG2E) + bias_ref[head]
            probs = jnp.exp2(logits - lse_ref[pl.ds(window * HEADS_IN + head, 1), :])
            dp = dot_t(jnp.where(mine, value, jnp.zeros_like(value)), dow)
            dots = jnp.sum(probs * dp, axis=0, keepdims=True)
            ds = (probs * (dp - dots)).astype(bf16)
            if window == 0:
                sums_ref[head] = ds.astype(f32)
            else:
                sums_ref[head] += ds.astype(f32)
            dv = jnp.where(mine, dot(probs.astype(bf16), dow), dv)
            dk = jnp.where(mine, dot(ds, query), dk)
            dq_t.append(dot(key_t[head * HEAD : (head + 1) * HEAD], ds))
        dq = jnp.concatenate(dq_t, axis=0).T
        dqkv[rows, 0:GROUP] = (dq * SCALE).astype(bf16)
        dqkv[rows, GROUP : 2 * GROUP] = (dk * SCALE).astype(bf16)
        dqkv[rows, 2 * GROUP : 3 * GROUP] = dv.astype(bf16)
    grad = dot_t(dqkv[...], w_ref[...])
    if not first:
        grad = grad + acc_ref[...]
    gw_ref[...] = dot(a1_t_ref[...], dqkv[...]).astype(gw_ref.dtype)
    gb_ref[...] = jnp.sum(dqkv[...].astype(f32), axis=0, keepdims=True)
    if last:
        unit, inverse = moments(x_ref[...].astype(f32))
        gx_ref[...] = (dh_ref[...] + norm_back(grad, unit, inverse, gain_ref[...])).astype(bf16)
        vec_ref[...] = jnp.concatenate(
            [jnp.sum(grad * unit, axis=0, keepdims=True), jnp.sum(grad, axis=0, keepdims=True)],
            axis=0,
        )
    else:
        out_ref[...] = grad


def whole(shape):
    return pl.BlockSpec(shape, lambda *i: (0,) * len(shape))


def shaped(shape, kind=f32):
    return jax.ShapeDtypeStruct(shape, kind)


def pick_matrix():
    place = lax.iota(jnp.int32, TABLE_PAD)
    row, column = place % PLANE // SPAN_W, place % PLANE % SPAN_W
    target = place // PLANE * SIDE + row * WW + column
    good = (place < TABLE) & (row < WH) & (column < WW)
    target = lax.optimization_barrier(jnp.where(good, target, -1))
    lane = lax.broadcasted_iota(jnp.int32, (TABLE_PAD, DIAG_PAD), 1)
    return (lane == target[:, None]).astype(bf16)


def region_features(late, low):
    cell = lax.broadcasted_iota(jnp.int32, (PAIR, PADDED, GROUP), 1)
    lane = lax.broadcasted_iota(jnp.int32, (PAIR, PADDED, GROUP), 2)
    right = lax.broadcasted_iota(jnp.int32, (PAIR, PADDED, GROUP), 0)
    code = (
        (late * (cell // SIDE >= WT - ST)) * 4
        + (low * (cell // WW % WH >= WH - SH)) * 2
        + right * (cell % WW >= WW - SW)
    )
    real = cell < WIN
    ours = (real & (lane == code)) | (lane == 8)
    theirs = jnp.where(real, (lane < 8) & (lane != code), lane == 8)
    return ours.astype(bf16), jnp.where(theirs, FAR, 0.0).astype(bf16)


class Windows:
    def __init__(self, clips, local, groups, shares):
        self.share = clips // shares
        self.local = local
        self.half = groups // 2
        first = ST * FRAME // local
        order = [(first + i) % groups for i in range(groups)]
        self.groups = [order[: self.half], order[self.half :]]
        self.frames = local // FRAME if local % FRAME == 0 else 0
        slot = (lax.axis_index("grp") - first) % groups
        self.late = slot // self.half
        self.low = slot % 2

    def exchange(self, rows):
        return lax.all_to_all(
            rows, "grp", split_axis=0, concat_axis=0, tiled=True, axis_index_groups=self.groups
        )

    def gather(self, field):
        width = field.shape[-1]
        if self.frames:
            cells = field.reshape(self.share, self.frames, CH, CW, width)
            cells = jnp.roll(cells, (-SH, -SW), axis=(2, 3))
            cells = cells.reshape(self.share, self.frames, 2, WH, 2, WW, width)
            cells = cells.transpose(0, 2, 4, 1, 3, 5, 6)
            cells = self.exchange(cells.reshape(self.half, 2, self.frames * SIDE, width))
            cells = cells.transpose(1, 0, 2, 3).reshape(PAIR, WIN, width)
        else:
            cells = self.exchange(jnp.repeat(field, 2, axis=0))
            cells = cells.reshape(WT, CH, CW, width)
            cells = jnp.roll(cells, (-SH, -SW), axis=(1, 2))
            cells = lax.dynamic_slice_in_dim(cells, self.low * WH, WH, 1)
            cells = cells.reshape(WT, WH, 2, WW, width).transpose(2, 0, 1, 3, 4)
            cells = cells.reshape(PAIR, WIN, width)
        cells = jnp.pad(cells, ((0, 0), (0, PADDED - WIN), (0, 0)))
        return cells.reshape(ROWS, width)

    def scatter(self, rows):
        width = rows.shape[-1]
        cells = rows.reshape(PAIR, PADDED, width)[:, :WIN]
        if self.frames:
            cells = cells.reshape(PAIR, self.half, self.frames * SIDE, width)
            cells = self.exchange(cells.transpose(1, 0, 2, 3))
            cells = cells.reshape(self.share, 2, 2, self.frames, WH, WW, width)
            cells = cells.transpose(0, 3, 1, 4, 2, 5, 6)
            cells = cells.reshape(self.share, self.frames, CH, CW, width)
            cells = jnp.roll(cells, (SH, SW), axis=(2, 3))
        else:
            cells = cells.reshape(2, WT, WH, WW, width).transpose(1, 2, 0, 3, 4)
            cells = cells.reshape(WT, WH, CW, width)
            blank = jnp.zeros((WT, CH, CW, width), cells.dtype)
            cells = lax.dynamic_update_slice_in_dim(blank, cells, self.low * WH, 1)
            cells = jnp.roll(cells, (SH, SW), axis=(1, 2))
            cells = self.exchange(cells.reshape(self.half, self.local, width))
            cells = cells.reshape(self.share, 2, self.local, width)
            cells = cells[:, 0] + cells[:, 1]
        return gather_over(cells.reshape(self.share, self.local, width), "tp", 0)


def swap(field, axis, bit):
    size = lax.axis_size(axis)
    return lax.ppermute(field, axis, [(i, i ^ bit) for i in range(size)])


def bits_of(axis):
    size = lax.axis_size(axis)
    return [1 << i for i in reversed(range(size.bit_length() - 1))]


def flag_of(axis, bit):
    return lax.axis_index(axis) // bit % 2


def gather_over(part, axis, lead):
    bits = bits_of(axis)
    shape = part.shape
    part = part.reshape(shape[:lead] + (1,) * len(bits) + shape[lead:])
    for place, bit in enumerate(bits):
        other = swap(part, axis, bit)
        second = flag_of(axis, bit) == 1
        part = jnp.concatenate(
            [jnp.where(second, other, part), jnp.where(second, part, other)], axis=lead + place
        )
    return part.reshape(shape[:lead] + (-1,) + shape[lead + 1 :])


def split_rows(field, lead):
    bits = bits_of("grp")
    shape = field.shape
    rows = shape[lead] >> len(bits)
    return field.reshape(shape[:lead] + (2,) * len(bits) + (rows,) + shape[lead + 1 :])


def halve(field, lead, bit):
    place = lead + bits_of("grp").index(bit)
    mine = flag_of("grp", bit)
    keep = lax.dynamic_index_in_dim(field, mine, place, keepdims=True)
    send = lax.dynamic_index_in_dim(field, 1 - mine, place, keepdims=True)
    return keep + swap(send.astype(bf16), "grp", bit).astype(f32)


def reduce_rows(field, lead):
    for bit in reversed(bits_of("grp")):
        field = halve(field, lead, bit)
    return field


def pass_on(pair):
    return pair[0] + swap(pair[1].astype(bf16), "tp", 2).astype(f32)


def per_device(
    tokens, grad_out, ln1_gain, ln1_shift, w_qkv, qkv_bias, rel_table, w_proj, proj_bias,
    ln2_gain, ln2_shift, w_in, in_bias, w_out, out_bias,
):
    groups, shares = lax.axis_size("grp"), lax.axis_size("tp")
    clips, local, width = tokens.shape
    move = Windows(clips, local, groups, shares)
    depth = w_qkv.shape[0]
    hidden = w_in.shape[1]
    heads = rel_table.shape[1]

    def own_share(field):
        return lax.dynamic_slice_in_dim(field, lax.axis_index("tp") * move.share, move.share, 0)

    split = jnp.concatenate([rel_table.T.reshape(-1), qkv_bias.reshape(-1), in_bias])
    split = jnp.stack([split, swap(split, "tp", 1)])
    split = jnp.concatenate([split, swap(split, "tp", 2)]).astype(f32)
    size = rel_table.size
    tables = split[:, :size].reshape(shares, heads, 1, TABLE)
    tables = jnp.pad(tables, ((0, 0), (0, 0), (0, 0), (0, TABLE_PAD - TABLE)))
    qkv_shift = split[:, size : size + qkv_bias.size].reshape(shares, 2, 1, GROUP)
    qkv_shift = jnp.concatenate(
        [qkv_shift[:, 0], jnp.zeros_like(qkv_shift[:, 0]), qkv_shift[:, 1]], axis=-1
    )
    in_shift = split[:, size + qkv_bias.size :][:, None]

    vectors = jnp.stack([ln1_gain, ln1_shift, proj_bias, ln2_gain, ln2_shift, out_bias])
    first = jnp.concatenate(
        [w_qkv.reshape(depth, 3 * GROUP), jnp.pad(vectors.T, ((0, 0), (0, GROUP - 6)))], axis=1
    )
    first = gather_over(first, "grp", 0)
    vectors = first[:, 3 * GROUP : 3 * GROUP + 6].T.astype(f32)
    gain_one, shift_one, proj_shift, gain_two, shift_two, out_shift = (
        vectors[i : i + 1] for i in range(6)
    )
    own = first[:, : 3 * GROUP]
    across = swap(own, "tp", 2)
    w_slots = [own, swap(own, "tp", 1), across, swap(across, "tp", 1)]

    x_rows = move.gather(own_share(tokens))

    home_in = gather_over(jnp.concatenate([w_in, w_proj], axis=1), "grp", 0)
    home_in = jnp.stack([home_in, swap(home_in, "tp", 2)])
    away_in = swap(home_in, "tp", 1)
    home_out = jnp.stack([w_out, swap(w_out, "tp", 2)])
    home_out = gather_over(home_out, "grp", 1)
    away_out = swap(home_out, "tp", 1)

    g_rows = move.gather(own_share(grad_out))

    pick = pick_matrix()
    ours, theirs = region_features(move.late, move.low)

    def bias_of(table):
        return pl.pallas_call(
            bias_kernel,
            out_shape=shaped((heads, PADDED, PADDED)),
            scratch_shapes=[
                pltpu.VMEM((heads, SIDE_PAD, TABLE_PAD), f32),
                pltpu.VMEM((heads, SIDE_PAD, DIAG_PAD), f32),
            ],
            compiler_params=PARAMS(),
            cost_estimate=cost(4.5),
            name="bias",
        )(table, pick)

    biases = [bias_of(tables[i]) for i in range(shares)]

    per_slot = [
        shaped((ROWS, 3 * GROUP), bf16),
        shaped((ROWS, GROUP), bf16),
        shaped((PAIR * heads, PADDED)),
    ]
    qkvs, o_parts, sums = [], [], []
    for i in range(shares):
        if i == 0:
            a1, a1_t, *made = pl.pallas_call(
                functools.partial(attention_kernel, True),
                out_shape=[shaped((ROWS, width), bf16), shaped((width, ROWS), bf16), *per_slot],
                compiler_params=PARAMS(),
                cost_estimate=cost(6),
                name="attention",
            )(x_rows, gain_one, shift_one, w_slots[i], qkv_shift[i], biases[i], ours, theirs)
        else:
            made = pl.pallas_call(
                functools.partial(attention_kernel, False),
                out_shape=per_slot,
                compiler_params=PARAMS(),
                cost_estimate=cost(5),
                name="attention",
            )(a1, w_slots[i], qkv_shift[i], biases[i], ours, theirs)
        qkvs.append(made[0])
        o_parts.append(made[1])
        sums.append(made[2])

    half = shares // 2
    rows, row = whole((ROWS, width)), whole((1, width))
    part = whole((ROWS, GROUP))
    in_block, out_block = whole((half, width, hidden + GROUP)), whole((half, width, hidden))
    proj_block = whole((half, width, GROUP))
    keep_spec = pl.BlockSpec((1, width, hidden), lambda i: (jnp.maximum(i - half, 0), 0, 0))
    send_spec = pl.BlockSpec((1, width, hidden), lambda i: (jnp.minimum(i, half - 1), 0, 0))
    unit_spec = pl.BlockSpec((1, 1, hidden), lambda i: (jnp.where(i < half, 2 * i + 1, 2 * i - shares), 0, 0))
    (
        out_rows, dh, dow, in_keep, in_send, out_keep, out_send, proj_keep, proj_send,
        grad_in_shift, vec_two,
    ) = pl.pallas_call(
        mlp_kernel,
        grid=(shares,),
        in_specs=[
            rows, part, part, part, part, rows, in_block, in_block, out_block, out_block,
            row, row, row, unit_spec, row,
        ],
        out_specs=[
            rows, rows, rows, keep_spec, send_spec, keep_spec, send_spec, proj_block, proj_block,
            unit_spec, whole((4, width)),
        ],
        out_shape=[
            shaped((ROWS, width), bf16),
            shaped((ROWS, width)),
            shaped((ROWS, width), bf16),
            shaped((half, width, hidden)),
            shaped((half, width, hidden), bf16),
            shaped((half, width, hidden)),
            shaped((half, width, hidden), bf16),
            shaped((half, width, GROUP)),
            shaped((half, width, GROUP), bf16),
            shaped((shares, 1, hidden)),
            shaped((4, width)),
        ],
        scratch_shapes=[
            pltpu.VMEM((ROWS, width), f32),
            pltpu.VMEM((ROWS, width), bf16),
            pltpu.VMEM((width, ROWS), bf16),
            pltpu.VMEM((width, ROWS), bf16),
            pltpu.VMEM((ROWS, width), f32),
            pltpu.VMEM((ROWS, 1), f32),
            pltpu.VMEM((ROWS, width), f32),
            pltpu.VMEM((ROWS, width), f32),
            pltpu.VMEM((ROWS, width), bf16),
            pltpu.VMEM((width, width), bf16),
            pltpu.VMEM((width, hidden), bf16),
            pltpu.VMEM((width, hidden), bf16),
        ],
        compiler_params=PARAMS(),
        cost_estimate=cost(22),
        name="mlp",
    )(
        x_rows, *o_parts, g_rows, home_in, away_in, home_out, away_out,
        proj_shift, gain_two, shift_two, in_shift, out_shift,
    )
    output = move.scatter(out_rows)

    got_out = out_keep + swap(out_send, "tp", 1).astype(f32)
    got_out = pass_on(got_out)
    got_out = reduce_rows(split_rows(got_out, 0), 0).reshape(depth, hidden)
    got_in = jnp.concatenate(
        [
            in_keep + swap(in_send, "tp", 1).astype(f32),
            proj_keep + swap(proj_send, "tp", 1).astype(f32),
        ],
        axis=-1,
    )
    got_in = reduce_rows(split_rows(got_in, 1), 1)
    got_in = pass_on(got_in).reshape(depth, hidden + GROUP)

    back = {}
    order = [1, 3, 0, 2]
    for i in order:
        first_call, last_call = i == order[0], i == order[-1]
        given = [a1_t, w_slots[i], qkvs[i], dow, sums[i], biases[i], ours, theirs]
        specs = [whole(v.shape) for v in given]
        specs[3] = pl.BlockSpec((ROWS, GROUP), functools.partial(lambda j, s: (0, j), i))
        if not first_call:
            given.append(running)
        if last_call:
            given += [x_rows, gain_one, dh]
        specs += [whole(v.shape) for v in given[8:]]
        made = [shaped((ROWS, width), bf16 if last_call else f32)]
        if last_call:
            made.append(shaped((2, width)))
        made += [
            shaped((width, 3 * GROUP), bf16 if i % 2 else f32),
            shaped((1, 3 * GROUP)),
            shaped((heads, PADDED, PADDED)),
        ]
        running, *made = pl.pallas_call(
            functools.partial(attention_back_kernel, first_call, last_call),
            grid=(1,),
            in_specs=specs,
            out_specs=[whole(v.shape) for v in made],
            out_shape=made,
            scratch_shapes=[pltpu.VMEM((ROWS, 3 * GROUP), bf16)],
            compiler_params=PARAMS(),
            cost_estimate=cost(9),
            name="attention_back",
        )(*given)
        if last_call:
            vec_one, *made = made
        back[i] = made
    grad_tokens = move.scatter(running).astype(f32)

    got_qkv = [back[i][0] + swap(back[i + 1][0], "tp", 1).astype(f32) for i in (0, 2)]
    got_qkv = pass_on(got_qkv)
    got_qkv = reduce_rows(split_rows(got_qkv, 0), 0).reshape(depth, 3, GROUP)

    def table_of(pair_sums):
        return pl.pallas_call(
            table_kernel,
            out_shape=shaped((heads, 1, TABLE_PAD)),
            scratch_shapes=[
                pltpu.VMEM((heads, SIDE_PAD, DIAG_PAD), f32),
                pltpu.VMEM((heads, SIDE_PAD, TABLE_PAD), f32),
            ],
            compiler_params=PARAMS(),
            cost_estimate=cost(4.5),
            name="table",
        )(pair_sums, pick)

    table_grads = {i: table_of(back[i][2]) for i in order}
    by_slot = [
        jnp.concatenate(
            [table_grads[i].reshape(-1), back[i][1].reshape(-1), grad_in_shift[i].reshape(-1)]
        ).reshape(-1, GROUP)
        for i in range(shares)
    ]
    vec = jnp.concatenate([vec_one, vec_two]).reshape(-1, GROUP)
    vec_size = vec.shape[0]
    kept = jnp.concatenate([vec, by_slot[0], by_slot[2]])
    kept = kept + swap(jnp.concatenate([vec, by_slot[1], by_slot[3]]), "tp", 1)
    cut = vec_size + by_slot[0].shape[0]
    rest = kept[:cut]
    small = rest + swap(jnp.concatenate([kept[:vec_size], kept[cut:]]), "tp", 2)
    for bit in reversed(bits_of("grp")):
        small = small + swap(small, "grp", bit)
    vec = small[:vec_size].reshape(6, width)
    vec = lax.dynamic_slice_in_dim(vec, lax.axis_index("grp") * depth, depth, 1)
    small = small[vec_size:].reshape(-1)
    got_table = small[: heads * TABLE_PAD].reshape(heads, TABLE_PAD)[:, :TABLE].T
    got_shift = small[heads * TABLE_PAD :][: 3 * GROUP].reshape(3, GROUP)
    got_in_shift = small[heads * TABLE_PAD + 3 * GROUP :]
    return (
        output,
        grad_tokens,
        vec[0],
        vec[1],
        got_qkv,
        jnp.stack([got_shift[0], got_shift[2]]),
        got_table,
        got_in[:, hidden:],
        vec[4],
        vec[2],
        vec[3],
        got_in[:, :hidden],
        got_in_shift,
        got_out,
        vec[5],
    )


def solution(mesh):
    shard = P("grp")
    tokens = P(None, "grp", None)
    placed = (
        tokens, tokens, shard, shard, P("grp", None, "tp"), P(None, "tp"), P(None, "tp"),
        P("grp", "tp"), shard, shard, shard, P("grp", "tp"), P("tp"), P("grp", "tp"), shard,
    )
    return jax.shard_map(
        per_device, mesh=mesh, in_specs=placed, out_specs=placed, check_vma=False
    )
```

```python
import functools

import jax
import jax.numpy as jnp
import numpy as np
from jax import lax
from jax.experimental import pallas as pl
from jax.experimental.pallas import tpu as pltpu
from jax.sharding import PartitionSpec as P

CT, CH, CW = 16, 14, 14
WT, WH, WW = 8, 7, 7
ST, SH, SW = 4, 3, 3
FRAME = CH * CW
SIDE = WH * WW
WIN = WT * SIDE
PAIR = 2
PADDED = -(-WIN // 16) * 16
ROWS = PAIR * PADDED
HEAD = 32
GROUP = 128
HEADS_IN = GROUP // HEAD
SPAN_T, SPAN_H, SPAN_W = 2 * WT - 1, 2 * WH - 1, 2 * WW - 1
PLANE = SPAN_H * SPAN_W
TABLE = SPAN_T * PLANE
TABLE_PAD = -(-TABLE // 128) * 128
DIAG = SPAN_T * SIDE
DIAG_PAD = -(-DIAG // 128) * 128
SIDE_PAD = -(-SIDE // 8) * 8
CORNER = PLANE // 2
LOG2E = 1.4426950408889634
SCALE = HEAD ** (-0.5)
FAR = -(2.0**100)
f32 = jnp.float32
bf16 = jnp.bfloat16


def room(mib):
    return pltpu.CompilerParams(vmem_limit_bytes=mib * 1024 * 1024)


def cost(micros):
    return pl.CostEstimate(flops=int(micros * 1.1e9), bytes_accessed=1 << 20, transcendentals=0)


def dot(a, b):
    return lax.dot_general(a, b, (((1,), (0,)), ((), ())), preferred_element_type=f32)


def dot_t(a, b):
    return lax.dot_general(a, b, (((1,), (1,)), ((), ())), preferred_element_type=f32)


def moments(rows):
    centered = rows - jnp.mean(rows, axis=-1, keepdims=True)
    inverse = lax.rsqrt(jnp.mean(centered * centered, axis=-1, keepdims=True) + 1e-05)
    return centered * inverse, inverse


def norm_back(grad, unit, inverse, gain):
    scaled = grad * gain
    shared = jnp.mean(scaled, axis=-1, keepdims=True)
    along = jnp.mean(scaled * unit, axis=-1, keepdims=True)
    return inverse * (scaled - shared - unit * along)


def read_rows(target, refs, place_ref, stack):
    if stack is None:
        target[...] = refs[0][...].astype(f32)
        return
    for i, ref in enumerate(refs):
        stack[i] = ref[...]
    size = refs[0].shape[1]
    for window in range(PAIR):
        for i in range(len(refs)):
            piece = stack[i ^ place_ref[0], window]
            target[pl.ds(window * PADDED + i * size, size), :] = piece.astype(f32)
        start = window * PADDED + WIN
        target[pl.ds(start, PADDED - WIN), :] = jnp.zeros((PADDED - WIN, target.shape[1]), f32)


def write_rows(refs, source, place_ref, stack):
    if stack is None:
        refs[0][...] = source[...].astype(bf16)
        return
    size = refs[0].shape[1]
    for window in range(PAIR):
        for i in range(len(refs)):
            piece = source[pl.ds(window * PADDED + i * size, size), :]
            stack[i, window] = piece.astype(bf16)
    for i, ref in enumerate(refs):
        ref[...] = stack[i ^ place_ref[0]]


def cells_kernel(place_ref, tokens_ref, order_ref, *refs):
    outs, stack = refs[:-1], refs[-1]
    step = pl.program_id(0)
    size = stack.shape[2]
    rows = dot(order_ref[...], tokens_ref[0])
    for i in range(4):
        start = i * (order_ref.shape[0] // 4)
        stack[2 * step + i // 2, i % 2] = rows[start : start + size].astype(bf16)

    @pl.when(step == pl.num_programs(0) - 1)
    def _():
        for i, ref in enumerate(outs):
            ref[...] = stack[i ^ place_ref[1]]


def positions_kernel(place_ref, *refs):
    out_ref, rows, stack = refs[-3:]
    cells, order_ref = refs[: stack.shape[0]], refs[stack.shape[0]]
    size = cells[0].shape[1]
    block = rows.shape[0] // 4
    step = pl.program_id(0)

    @pl.when(step == 0)
    def _():
        rows[...] = jnp.zeros_like(rows)
        for i, ref in enumerate(cells):
            stack[i] = ref[...]

    for i in range(4):
        piece = stack[(2 * step + i // 2) ^ place_ref[1], i % 2]
        rows[i * block : i * block + size, :] = piece
    out_ref[0] = dot(order_ref[...], rows[...]).astype(out_ref.dtype)


SPANS = []
for _lane in range(0, DIAG_PAD, 256):
    _low = _lane // SIDE * PLANE // 256 * 256
    _high = -(-(min(_lane + 255, DIAG - 1) // SIDE * PLANE + PLANE) // 256) * 256
    SPANS.append((_lane, _low, min(_high, TABLE_PAD)))
PICK_ROWS = sum(high - low for _, low, high in SPANS)


def bias_kernel(table_ref, pick_ref, bias_ref, sheared, spread):
    heads = table_ref.shape[0]
    row_of = lax.broadcasted_iota(jnp.int32, (8, TABLE_PAD), 0)
    for head in range(heads):
        flat = jnp.broadcast_to(table_ref[head], (8, TABLE_PAD))
        stairs = flat
        for step in range(1, WW):
            stairs = jnp.where(row_of == step, pltpu.roll(flat, step, 1), stairs)
        for row in range(WH):
            shift = (row * SPAN_W - CORNER) % TABLE_PAD
            sheared[head, pl.ds(row * WW, 8), :] = pltpu.roll(stairs, shift, 1)
    everything = sheared[...].reshape(heads * SIDE_PAD, TABLE_PAD).astype(bf16)
    start = 0
    for lane, low, high in SPANS:
        part = dot(everything[:, low:high], pick_ref[start : start + high - low]) * LOG2E
        spread[:, :, lane : lane + 256] = part.reshape(heads, SIDE_PAD, 256)
        start += high - low
    for head in range(heads):
        block = spread[head]
        for frame in range(WT):
            shift = -(WT - 1 - frame) * SIDE % DIAG_PAD
            moved = pltpu.roll(block, shift, 1) if shift else block
            bias_ref[head, pl.ds(frame * SIDE, SIDE_PAD), :] = moved[:, :PADDED]
        bias_ref[head, WIN:PADDED, :] = jnp.zeros((PADDED - WIN, PADDED), f32)


def table_kernel(sums_ref, pick_ref, grad_ref, spread, sheared):
    heads = sums_ref.shape[0]
    row_of = lax.broadcasted_iota(jnp.int32, (SIDE_PAD, DIAG_PAD), 0)
    lane_of = lax.broadcasted_iota(jnp.int32, (SIDE_PAD, DIAG_PAD), 1)
    blank = jnp.zeros((SIDE_PAD, DIAG_PAD - PADDED), f32)
    for head in range(heads):
        total = jnp.zeros((SIDE_PAD, DIAG_PAD), f32)
        for frame in range(WT):
            piece = sums_ref[head, pl.ds(frame * SIDE, SIDE_PAD), :]
            piece = jnp.concatenate([piece, blank], axis=1)
            piece = jnp.where(lane_of < WIN, piece, 0.0)
            shift = (WT - 1 - frame) * SIDE
            total = total + (pltpu.roll(piece, shift, 1) if shift else piece)
        spread[head] = jnp.where(row_of < SIDE, total, 0.0)
    everything = spread[...].reshape(heads * SIDE_PAD, DIAG_PAD).astype(bf16)
    sheared[...] = jnp.zeros_like(sheared)
    start = 0
    for lane, low, high in SPANS:
        part = dot_t(everything[:, lane : lane + 256], pick_ref[start : start + high - low])
        sheared[:, :, low:high] += part.reshape(heads, SIDE_PAD, high - low)
        start += high - low
    row_in = lax.broadcasted_iota(jnp.int32, (8, TABLE_PAD), 0)
    for head in range(heads):
        stairs = jnp.zeros((8, TABLE_PAD), f32)
        for row in range(WH):
            shift = (CORNER - row * SPAN_W) % TABLE_PAD
            stairs = stairs + pltpu.roll(sheared[head, pl.ds(row * WW, 8), :], shift, 1)
        flat = jnp.where(row_in == 0, stairs, 0.0)
        for step in range(1, WW):
            moved = pltpu.roll(stairs, TABLE_PAD - step, 1)
            flat = flat + jnp.where(row_in == step, moved, 0.0)
        grad_ref[head] = jnp.sum(flat, axis=0, keepdims=True)


def attention_kernel(first, count, *refs):
    step = pl.program_id(0)
    place_ref, refs = refs[0], refs[1:]
    if first:
        got, refs = refs[:count], refs[count:]
        gain_ref, shift_ref, w0_ref, w1_ref, wb_ref, bias_ref, qf_ref, kf_ref = refs[:8]
        x_ref, a1_ref, a1_t_ref, qkv_ref, o_ref, lse_ref, w_ref, rows_in = refs[8:16]
        stack = refs[16] if count > 1 else None

        @pl.when(step == 0)
        def _():
            read_rows(rows_in, got, place_ref, stack)
            x_ref[...] = rows_in[...].astype(bf16)
            unit, _ = moments(rows_in[...])
            low = unit * gain_ref[...] + shift_ref[...]
            a1_ref[...] = low.astype(bf16)
            a1_t_ref[...] = low.T.astype(bf16)
    else:
        a1_ref, w0_ref, w1_ref, wb_ref, bias_ref, qf_ref, kf_ref = refs[:7]
        qkv_ref, o_ref, lse_ref, w_ref = refs[7:]

    @pl.when(step == 0)
    def _():
        w_ref[...] = w0_ref[...]

    @pl.when(step == 1)
    def _():
        w_ref[...] = w1_ref[...]

    qkv_ref[0] = (dot(a1_ref[...], w_ref[...]) + wb_ref[0]).astype(bf16)
    lane = lax.broadcasted_iota(jnp.int32, (PADDED, GROUP), 1) // HEAD
    for window in range(PAIR):
        rows = slice(window * PADDED, (window + 1) * PADDED)
        query = qkv_ref[0, rows, 0:GROUP]
        key = qkv_ref[0, rows, GROUP : 2 * GROUP]
        value = qkv_ref[0, rows, 2 * GROUP : 3 * GROUP]
        query = jnp.concatenate([query, qf_ref[window]], axis=1)
        value_t = value.astype(f32).T.astype(bf16)
        parts = []
        for head in range(HEADS_IN):
            own = jnp.where(lane == head, key, jnp.zeros_like(key))
            own = jnp.concatenate([own, kf_ref[window]], axis=1)
            logits = dot_t(own, query) * (SCALE * LOG2E) + bias_ref[head]
            top = jnp.max(logits, axis=0, keepdims=True)
            probs = jnp.exp2(logits - top)
            total = jnp.sum(probs, axis=0, keepdims=True)
            lse_ref[0, pl.ds(window * HEADS_IN + head, 1), :] = top + jnp.log2(total)
            mixed = dot(value_t[head * HEAD : (head + 1) * HEAD], probs.astype(bf16))
            parts.append(mixed / total)
        o_ref[rows, :] = jnp.concatenate(parts, axis=0).T.astype(bf16)


def mlp_kernel(count, place_ref, slot_ref, *refs):
    got, refs = refs[:count], refs[count:]
    x_ref, oa_ref, ob_ref, wi_ref, wo_ref, wp_ref = refs[:6]
    pb_ref, gain_ref, shift_ref, ib_ref, out_shift_ref = refs[6:11]
    outs, refs = refs[11 : 11 + count], refs[11 + count :]
    dh_ref, dow_ref, gwi_keep, gwi_send, gwo_keep, gwo_send, gwp_keep, gwp_send = refs[:8]
    gib_ref, vec_ref = refs[8:10]
    hidden, a2, a2_t, g_ref, g_t, unit_s, inv_s, acc_out, acc_in, o_all, wp = refs[10:21]
    stack = refs[21] if count > 1 else None
    step = pl.program_id(0)
    width = x_ref.shape[1]

    @pl.when(step == 0)
    def _():
        o_all[:, 0 : 2 * GROUP] = oa_ref[...]
        o_all[:, 2 * GROUP : 4 * GROUP] = ob_ref[...]
        for i, j in enumerate((2, 0, 3, 1)):
            wp[:, i * GROUP : (i + 1) * GROUP] = wp_ref[:, slot_ref[j]].reshape(width, GROUP)
        branch = dot_t(o_all[...], wp[...])
        hidden[...] = x_ref[...].astype(f32) + branch + pb_ref[...]
        unit, inverse = moments(hidden[...])
        unit_s[...] = unit
        inv_s[...] = inverse
        low = unit * gain_ref[...] + shift_ref[...]
        a2[...] = low.astype(bf16)
        a2_t[...] = low.T.astype(bf16)
        read_rows(acc_out, got, place_ref, stack)
        g_ref[...] = acc_out[...].astype(bf16)
        g_t[...] = acc_out[...].T.astype(bf16)
        acc_out[...] = jnp.zeros_like(acc_out)
        acc_in[...] = jnp.zeros_like(acc_in)

    wi = wi_ref[...].reshape(width, wi_ref.shape[-1])
    wo = wo_ref[...].reshape(width, wo_ref.shape[-1])
    u = dot(a2[...], wi) + ib_ref[0]
    half = 0.5 * (1.0 + lax.erf(u * (0.5**0.5)))
    act = (u * half).astype(bf16)
    acc_out[...] += dot_t(act, wo)
    back = dot(g_ref[...], wo)
    slope = half + u * jnp.exp(-0.5 * u * u) * 0.3989422804014327
    du_low = (back * slope).astype(bf16)
    acc_in[...] += dot_t(du_low, wi)
    grad_out_w = dot(g_t[...], act)
    grad_in_w = dot(a2_t[...], du_low)
    gib_ref[0] = jnp.sum(du_low.astype(f32), axis=0, keepdims=True)

    @pl.when(step < 2)
    def _():
        gwo_send[0] = grad_out_w.astype(bf16)
        gwi_send[0] = grad_in_w.astype(bf16)

    @pl.when(step >= 2)
    def _():
        gwo_keep[0] = grad_out_w.astype(bf16)
        gwi_keep[0] = grad_in_w.astype(bf16)

    @pl.when(step == pl.num_programs(0) - 1)
    def _():
        acc_out[...] += hidden[...] + out_shift_ref[...]
        write_rows(outs, acc_out, place_ref, stack)
        upstream = g_ref[...].astype(f32)
        grad = acc_in[...]
        unit = unit_s[...]
        dh = upstream + norm_back(grad, unit, inv_s[...], gain_ref[...])
        dh_ref[...] = dh
        dz = dh.astype(bf16)
        dow_ref[...] = dot(dz, wp[...]).astype(bf16)
        grad_wp = dot(dz.astype(f32).T.astype(bf16), o_all[...])
        for i in range(2):
            gwp_keep[i] = grad_wp[:, 2 * i * GROUP : (2 * i + 1) * GROUP].astype(bf16)
            gwp_send[i] = grad_wp[:, (2 * i + 1) * GROUP : (2 * i + 2) * GROUP].astype(bf16)
        vec_ref[...] = jnp.concatenate(
            [
                jnp.sum(grad * unit, axis=0, keepdims=True),
                jnp.sum(grad, axis=0, keepdims=True),
                jnp.sum(dz.astype(f32), axis=0, keepdims=True),
                jnp.sum(upstream, axis=0, keepdims=True),
            ],
            axis=0,
        )


def attention_back_kernel(last, count, place_ref, *refs):
    a1_t_ref, w0_ref, w1_ref, qkv_ref, dow_ref, lse_ref, bias_ref, qf_ref, kf_ref = refs[:9]
    refs = refs[9:]
    stack = None
    if last:
        sum_ref, x_ref, gain_ref, dh_ref = refs[:4]
        outs, refs = refs[4 : 4 + count], refs[4 + count :]
        vec_ref, keep_ref, send_ref, gb_ref, sums_ref, acc, dqkv, w_ref = refs[:8]
        stack = refs[8] if count > 1 else None
    else:
        sum_ref, keep_ref, send_ref, gb_ref, sums_ref, acc, dqkv, w_ref = refs
    step = pl.program_id(0)

    @pl.when(step == 0)
    def _():
        w_ref[...] = w0_ref[...]

    @pl.when(step == 1)
    def _():
        w_ref[...] = w1_ref[...]

    lane = lax.broadcasted_iota(jnp.int32, (PADDED, GROUP), 1) // HEAD
    for window in range(PAIR):
        rows = slice(window * PADDED, (window + 1) * PADDED)
        query = qkv_ref[0, rows, 0:GROUP]
        key = qkv_ref[0, rows, GROUP : 2 * GROUP]
        value = qkv_ref[0, rows, 2 * GROUP : 3 * GROUP]
        dow = dow_ref[rows, :]
        query_f = jnp.concatenate([query, qf_ref[window]], axis=1)
        key_t = key.astype(f32).T.astype(bf16)
        none = jnp.zeros((PADDED, GROUP), f32)
        dk, dv, dq_t = none, none, []
        for head in range(HEADS_IN):
            mine = lane == head
            own = jnp.where(mine, key, jnp.zeros_like(key))
            own = jnp.concatenate([own, kf_ref[window]], axis=1)
            logits = dot_t(own, query_f) * (SCALE * LOG2E) + bias_ref[head]
            probs = jnp.exp2(logits - lse_ref[0, pl.ds(window * HEADS_IN + head, 1), :])
            dp = dot_t(jnp.where(mine, value, jnp.zeros_like(value)), dow)
            dots = jnp.sum(probs * dp, axis=0, keepdims=True)
            ds = (probs * (dp - dots)).astype(bf16)
            if window == 0:
                sums_ref[head] = ds.astype(f32)
            else:
                sums_ref[head] += ds.astype(f32)
            dv = jnp.where(mine, dot(probs.astype(bf16), dow), dv)
            dk = jnp.where(mine, dot(ds, query), dk)
            dq_t.append(dot(key_t[head * HEAD : (head + 1) * HEAD], ds))
        dq = jnp.concatenate(dq_t, axis=0).T
        dqkv[rows, 0:GROUP] = (dq * SCALE).astype(bf16)
        dqkv[rows, GROUP : 2 * GROUP] = (dk * SCALE).astype(bf16)
        dqkv[rows, 2 * GROUP : 3 * GROUP] = dv.astype(bf16)
    grad = dot_t(dqkv[...], w_ref[...])
    grad_w = dot(a1_t_ref[...], dqkv[...])
    gb_ref[0] = jnp.sum(dqkv[...].astype(f32), axis=0, keepdims=True)

    @pl.when(step == 0)
    def _():
        acc[...] = grad + sum_ref[...] if last else grad
        keep_ref[...] = grad_w.astype(bf16)

    @pl.when(step == 1)
    def _():
        send_ref[...] = grad_w.astype(bf16)
        total = acc[...] + grad
        if last:
            unit, inverse = moments(x_ref[...].astype(f32))
            acc[...] = dh_ref[...] + norm_back(total, unit, inverse, gain_ref[...])
            write_rows(outs, acc, place_ref, stack)
            vec_ref[...] = jnp.concatenate(
                [jnp.sum(total * unit, axis=0, keepdims=True), jnp.sum(total, axis=0, keepdims=True)],
                axis=0,
            )
        else:
            sum_ref[...] = total


def whole(shape):
    return pl.BlockSpec(shape, lambda *i: (0,) * len(shape))


def shaped(shape, kind=f32):
    return jax.ShapeDtypeStruct(shape, kind)


def chunk(shape):
    return pl.BlockSpec((1,) + shape, lambda i, *_: (i,) + (0,) * len(shape))


def pick_matrix():
    place = np.arange(TABLE_PAD)
    row, column = place % PLANE // SPAN_W, place % PLANE % SPAN_W
    target = place // PLANE * SIDE + row * WW + column
    good = (place < TABLE) & (row < WH) & (column < WW)
    target = np.where(good, target, -1)
    target = np.concatenate([target[low:high] - lane for lane, low, high in SPANS])
    return jnp.asarray(np.arange(256) == target[:, None], bf16)


def region_features(late, low):
    cell = np.arange(PADDED)[:, None]
    lane = np.arange(GROUP)
    real = cell < WIN
    ours, theirs = [], []
    for is_late in range(2):
        for is_low in range(2):
            for is_right in range(PAIR):
                code = (
                    (is_late * (cell // SIDE >= WT - ST)) * 4
                    + (is_low * (cell // WW % WH >= WH - SH)) * 2
                    + is_right * (cell % WW >= WW - SW)
                )
                ours.append((real & (lane == code)) | (lane == 8))
                other = np.where(real, (lane < 8) & (lane != code), lane == 8)
                theirs.append(np.where(other, FAR, 0.0))
    which = late * 2 + low
    shape = (4, PAIR, PADDED, GROUP)
    ours = jnp.asarray(np.reshape(ours, shape), bf16)
    theirs = jnp.asarray(np.reshape(theirs, shape), bf16)
    return lax.dynamic_index_in_dim(ours, which, 0, False), lax.dynamic_index_in_dim(theirs, which, 0, False)


def cell_order(frames):
    size = frames * SIDE
    step = -(-size // 16) * 16
    matrix = np.zeros((4 * step, frames * FRAME), bool)
    for low in range(2):
        for right in range(2):
            for cell in range(size):
                frame, row, column = cell // SIDE, cell // WW % WH, cell % WW
                row = (low * WH + row + SH) % CH
                column = (right * WW + column + SW) % CW
                place = frame * FRAME + row * CW + column
                matrix[(low * 2 + right) * step + cell, place] = True
    return matrix


class Windows:
    def __init__(self, clips, local, groups, shares):
        self.share = clips // shares
        self.local = local
        self.half = groups // 2
        first = ST * FRAME // local
        order = [(first + i) % groups for i in range(groups)]
        self.groups = [order[: self.half], order[self.half :]]
        self.frames = local // FRAME if local % FRAME == 0 else 0
        slot = (lax.axis_index("grp") - first) % groups
        self.late = slot // self.half
        self.low = slot % 2
        self.place = slot % self.half
        self.count = self.half if self.frames else 1

    def exchange(self, parts):
        if not self.frames:
            got = lax.all_to_all(
                parts[0], "grp", split_axis=0, concat_axis=0, tiled=True,
                axis_index_groups=self.groups,
            )
            return (got,)
        got = [parts[0]]
        for i in range(1, self.half):
            pairs = [(group[j], group[j ^ i]) for group in self.groups for j in range(self.half)]
            got.append(lax.ppermute(parts[i], "grp", pairs))
        return tuple(got)

    def places(self, clip):
        return jnp.stack([clip, self.place]).astype(jnp.int32)

    def before(self, field):
        width = field.shape[-1]
        place = lax.axis_index("tp") * self.share
        if not self.frames:
            own = lax.dynamic_slice_in_dim(field, place, self.share, 0)
            return (jnp.repeat(own, 2, axis=0),)
        order = jnp.asarray(cell_order(self.frames), bf16)
        piece = (2, self.frames * SIDE, width)
        return pl.pallas_call(
            cells_kernel,
            grid_spec=pltpu.PrefetchScalarGridSpec(
                num_scalar_prefetch=1,
                grid=(self.share,),
                in_specs=[
                    pl.BlockSpec((1, self.local, width), lambda i, p: (p[0] + i, 0, 0)),
                    whole(order.shape),
                ],
                out_specs=[whole(piece)] * self.half,
                scratch_shapes=[pltpu.VMEM((self.half,) + piece, bf16)],
            ),
            out_shape=[shaped(piece, bf16)] * self.half,
            compiler_params=room(60),
            cost_estimate=cost(2),
            name="cells",
        )(self.places(place), field, order)

    def positions(self, cells, clip, into, clips, kind):
        width = cells[0].shape[-1]
        if not self.frames:
            cells = cells[0].reshape(self.share, 2, self.local, width)
            cells = (cells[:, 0] + cells[:, 1]).astype(kind)
            if into is None:
                into = jnp.zeros((clips, self.local, width), kind)
            return lax.dynamic_update_slice_in_dim(into, cells, clip, 0)
        order = jnp.asarray(cell_order(self.frames).T, bf16)
        extra = [] if into is None else [into]
        return pl.pallas_call(
            positions_kernel,
            grid_spec=pltpu.PrefetchScalarGridSpec(
                num_scalar_prefetch=1,
                grid=(self.share,),
                in_specs=[whole(cells[0].shape)] * self.half
                + [whole(order.shape)]
                + [pl.BlockSpec(memory_space=pl.ANY)] * len(extra),
                out_specs=pl.BlockSpec((1, self.local, width), lambda i, p: (p[0] + i, 0, 0)),
                scratch_shapes=[
                    pltpu.VMEM((order.shape[1], width), bf16),
                    pltpu.VMEM((self.half,) + cells[0].shape, bf16),
                ],
            ),
            out_shape=shaped((clips, self.local, width), kind),
            input_output_aliases={self.half + 2: 0} if extra else {},
            compiler_params=room(60),
            cost_estimate=cost(2),
            name="positions",
        )(self.places(clip), *cells, order, *extra)

    def rows_shapes(self, width):
        shape = (2, self.frames * SIDE, width) if self.frames else (ROWS, width)
        return [shaped(shape, bf16)] * self.count

    def stacks(self, width):
        shape = (self.count, 2, self.frames * SIDE, width)
        return [pltpu.VMEM(shape, bf16)] if self.frames else []

    def arrange(self, cells):
        if self.frames:
            return cells
        cells = cells[0]
        width = cells.shape[-1]
        cells = cells.reshape(WT, CH, CW, width)
        cells = jnp.roll(cells, (-SH, -SW), axis=(1, 2))
        cells = lax.dynamic_slice_in_dim(cells, self.low * WH, WH, 1)
        cells = cells.reshape(WT, WH, 2, WW, width).transpose(2, 0, 1, 3, 4)
        cells = cells.reshape(PAIR, WIN, width)
        cells = jnp.pad(cells, ((0, 0), (0, PADDED - WIN), (0, 0)))
        return (cells.reshape(ROWS, width),)

    def leave(self, rows):
        if self.frames:
            return rows
        rows = rows[0]
        width = rows.shape[-1]
        cells = rows.reshape(PAIR, PADDED, width)[:, :WIN]
        cells = cells.reshape(2, WT, WH, WW, width).transpose(1, 2, 0, 3, 4)
        cells = cells.reshape(WT, WH, CW, width)
        blank = jnp.zeros((WT, CH, CW, width), cells.dtype)
        cells = lax.dynamic_update_slice_in_dim(blank, cells, self.low * WH, 1)
        cells = jnp.roll(cells, (SH, SW), axis=(1, 2))
        return (cells.reshape(self.half, self.local, width),)


def swap(field, axis, bit):
    size = lax.axis_size(axis)
    return lax.ppermute(field, axis, [(i, i ^ bit) for i in range(size)])


def bits_of(axis):
    size = lax.axis_size(axis)
    return [1 << i for i in reversed(range(size.bit_length() - 1))]


def flag_of(axis, bit):
    return lax.axis_index(axis) // bit % 2


def after(value, *others):
    return lax.optimization_barrier((value, others))[0]


def join(mine, other, bit, axis, place):
    second = flag_of(axis, bit) == 1
    return jnp.concatenate(
        [jnp.where(second, other, mine), jnp.where(second, mine, other)], axis=place
    )


def plus(one, other):
    return (one.astype(f32) + other.astype(f32)).astype(bf16)


def split_rows(field, lead):
    bits = bits_of("grp")
    shape = field.shape
    rows = shape[lead] >> len(bits)
    return field.reshape(shape[:lead] + (2,) * len(bits) + (rows,) + shape[lead + 1 :])


def halves(field, lead, bit):
    place = lead + bits_of("grp").index(bit)
    mine = flag_of("grp", bit)
    keep = lax.dynamic_index_in_dim(field, mine, place, keepdims=True)
    send = lax.dynamic_index_in_dim(field, 1 - mine, place, keepdims=True)
    return keep, send


def per_device(
    tokens, grad_out, ln1_gain, ln1_shift, w_qkv, qkv_bias, rel_table, w_proj, proj_bias,
    ln2_gain, ln2_shift, w_in, in_bias, w_out, out_bias,
):
    groups, shares = lax.axis_size("grp"), lax.axis_size("tp")
    clips, local, width = tokens.shape
    move = Windows(clips, local, groups, shares)
    depth = w_qkv.shape[0]
    hidden = w_in.shape[1]
    heads = rel_table.shape[1]
    half = shares // 2

    packed = jnp.concatenate([w_in, w_out, w_proj], axis=1)
    later = lax.all_gather(packed, ("grp", "tp"), axis=0, tiled=False)
    later = later.reshape(groups, shares, depth, 2 * hidden + GROUP)
    if depth % 16:
        later = later.transpose(1, 0, 2, 3).reshape(1, shares, width, 2 * hidden + GROUP)
    places = lax.axis_index("tp") ^ jnp.array([1, 3, 0, 2], jnp.int32)

    vectors = jnp.stack([ln1_gain, ln1_shift, proj_bias, ln2_gain, ln2_shift, out_bias])
    first = jnp.concatenate(
        [w_qkv.reshape(depth, 3 * GROUP), jnp.pad(vectors.T, ((0, 0), (0, GROUP - 6)))], axis=1
    )
    split = jnp.concatenate([rel_table.T.reshape(-1), qkv_bias.reshape(-1), in_bias])
    split = jnp.stack([split, swap(split, "tp", 1)])
    other_split = swap(split, "tp", 2)

    pick = pick_matrix()
    ours, theirs = region_features(move.late, move.low)

    def bias_of(half_split):
        tables = half_split[:, : rel_table.size].astype(f32).reshape(2 * heads, 1, TABLE)
        tables = jnp.pad(tables, ((0, 0), (0, 0), (0, TABLE_PAD - TABLE)))
        block = pl.BlockSpec((heads, PADDED, PADDED), lambda i: (i, 0, 0))
        return pl.pallas_call(
            bias_kernel,
            grid=(2,),
            in_specs=[
                pl.BlockSpec((heads, 1, TABLE_PAD), lambda i: (i, 0, 0)),
                whole((PICK_ROWS, 256)),
            ],
            out_specs=block,
            out_shape=shaped((2 * heads, PADDED, PADDED)),
            scratch_shapes=[
                pltpu.VMEM((heads, SIDE_PAD, TABLE_PAD), f32),
                pltpu.VMEM((heads, SIDE_PAD, DIAG_PAD), f32),
            ],
            compiler_params=room(60),
            cost_estimate=cost(6),
            name="bias",
        )(tables, pick)

    def shifts_of(half_split):
        values = half_split[:, rel_table.size :].astype(f32)
        qkv_part = values[:, : 2 * GROUP].reshape(2, 2, 1, GROUP)
        nothing = jnp.zeros_like(qkv_part[:, 0])
        qkv_part = jnp.concatenate([qkv_part[:, 0], nothing, qkv_part[:, 1]], axis=-1)
        return qkv_part, values[:, None, 2 * GROUP :]

    x_send = move.before(after(tokens, first))
    x_got = move.exchange(x_send)
    bits = bits_of("grp")
    shape = first.shape
    first = first.reshape((1,) * len(bits) + shape)
    bias = {}
    beside = [
        lambda: (x_send,),
        lambda: bias.setdefault(0, bias_of(after(split, first))),
        lambda: bias.setdefault(1, bias_of(after(other_split, first))),
    ]
    for i, bit in enumerate(bits):
        done = beside[i]() if i < 3 else ()
        first = join(first, swap(first, "grp", bit), bit, "grp", i)
        first = after(first, *(done if isinstance(done, tuple) else (done,)))
    first = first.reshape(width, shape[1])
    bias_a, bias_b = bias[0], bias[1]
    vectors = first[:, 3 * GROUP : 3 * GROUP + 6].T.astype(f32)
    gain_one, shift_one, proj_shift, gain_two, shift_two, out_shift = (
        vectors[i : i + 1] for i in range(6)
    )
    own = first[:, : 3 * GROUP]
    place = move.places(lax.axis_index("tp"))[1:]
    across = swap(own, "tp", 2)
    w_a = (own, swap(own, "tp", 1))
    x_got = move.arrange(x_got)

    g_send = move.before(after(grad_out, own))
    g_got = move.exchange(g_send)
    qkv_shift_a, in_shift_a = shifts_of(split)
    qkv_shift_b, in_shift_b = shifts_of(other_split)

    rows, row = whole((ROWS, width)), whole((1, width))
    feature = whole((PAIR, PADDED, GROUP))
    bias_block = pl.BlockSpec((heads, PADDED, PADDED), lambda i, *_: (i, 0, 0))
    pair_columns = pl.BlockSpec((ROWS, GROUP), lambda i, *_: (0, i))
    pair_specs = [chunk((ROWS, 3 * GROUP)), pair_columns, chunk((PAIR * heads, PADDED))]
    pair_shapes = [
        shaped((2, ROWS, 3 * GROUP), bf16),
        shaped((ROWS, 2 * GROUP), bf16),
        shaped((2, PAIR * heads, PADDED)),
    ]
    w_block = whole((width, 3 * GROUP))
    w_specs = [w_block, w_block, chunk((1, 3 * GROUP)), bias_block, feature, feature]
    w_scratch = pltpu.VMEM((width, 3 * GROUP), bf16)
    x_rows, a1, a1_t, qkv_a, o_a, lse_a = pl.pallas_call(
        functools.partial(attention_kernel, True, move.count),
        grid_spec=pltpu.PrefetchScalarGridSpec(
            num_scalar_prefetch=1,
            grid=(2,),
            in_specs=[whole(v.shape) for v in x_got] + [row, row, *w_specs],
            out_specs=[rows, rows, whole((width, ROWS)), *pair_specs],
            scratch_shapes=[w_scratch, pltpu.VMEM((ROWS, width), f32), *move.stacks(width)],
        ),
        out_shape=[
            shaped((ROWS, width), bf16),
            shaped((ROWS, width), bf16),
            shaped((width, ROWS), bf16),
            *pair_shapes,
        ],
        compiler_params=room(60),
        cost_estimate=cost(12),
        name="attention",
    )(place, *x_got, gain_one, shift_one, *after(w_a, g_send), qkv_shift_a, bias_a, ours, theirs)
    across = after(across, a1)
    w_b = (across, swap(across, "tp", 1))
    qkv_b, o_b, lse_b = pl.pallas_call(
        functools.partial(attention_kernel, False, 0),
        grid_spec=pltpu.PrefetchScalarGridSpec(
            num_scalar_prefetch=1,
            grid=(2,),
            in_specs=[rows, *w_specs],
            out_specs=pair_specs,
            scratch_shapes=[w_scratch],
        ),
        out_shape=pair_shapes,
        compiler_params=room(60),
        cost_estimate=cost(11),
        name="attention",
    )(place, a1, *w_b, qkv_shift_b, bias_b, ours, theirs)

    g_got = move.arrange(g_got)
    in_shift = jnp.concatenate([in_shift_a, in_shift_b])
    both = whole((ROWS, 2 * GROUP))
    proj_block = whole((half, width, GROUP))
    lead, rest = later.shape[0], later.shape[2]
    keep_spec = pl.BlockSpec((1, width, hidden), lambda i, *_: (jnp.maximum(i - half, 0), 0, 0))
    send_spec = pl.BlockSpec((1, width, hidden), lambda i, *_: (jnp.minimum(i, half - 1), 0, 0))
    unit_spec = pl.BlockSpec(
        (1, 1, hidden), lambda i, *_: (jnp.where(i < half, 2 * i + 1, 2 * i - shares), 0, 0)
    )
    made = pl.pallas_call(
        functools.partial(mlp_kernel, move.count),
        grid_spec=pltpu.PrefetchScalarGridSpec(
            num_scalar_prefetch=2,
            grid=(shares,),
            in_specs=[whole(v.shape) for v in g_got]
            + [
                rows, both, both,
                pl.BlockSpec((lead, 1, rest, hidden), lambda i, _, p: (0, p[i], 0, 0)),
                pl.BlockSpec((lead, 1, rest, hidden), lambda i, _, p: (0, p[i], 0, 1)),
                pl.BlockSpec(
                    (lead, shares, rest, GROUP), lambda i, *_: (0, 0, 0, 2 * hidden // GROUP)
                ),
                row, row, row, unit_spec, row,
            ],
            out_specs=[whole(v.shape) for v in move.rows_shapes(width)]
            + [
                rows, rows,
                keep_spec, send_spec, keep_spec, send_spec, proj_block,
                proj_block, unit_spec, whole((4, width)),
            ],
            scratch_shapes=[
                pltpu.VMEM((ROWS, width), f32),
                pltpu.VMEM((ROWS, width), bf16),
                pltpu.VMEM((width, ROWS), bf16),
                pltpu.VMEM((ROWS, width), bf16),
                pltpu.VMEM((width, ROWS), bf16),
                pltpu.VMEM((ROWS, width), f32),
                pltpu.VMEM((ROWS, 1), f32),
                pltpu.VMEM((ROWS, width), f32),
                pltpu.VMEM((ROWS, width), f32),
                pltpu.VMEM((ROWS, width), bf16),
                pltpu.VMEM((width, width), bf16),
                *move.stacks(width),
            ],
        ),
        out_shape=[
            *move.rows_shapes(width),
            shaped((ROWS, width)),
            shaped((ROWS, width), bf16),
            shaped((half, width, hidden), bf16),
            shaped((half, width, hidden), bf16),
            shaped((half, width, hidden), bf16),
            shaped((half, width, hidden), bf16),
            shaped((half, width, GROUP), bf16),
            shaped((half, width, GROUP), bf16),
            shaped((shares, 1, hidden)),
            shaped((4, width)),
        ],
        compiler_params=room(60),
        cost_estimate=cost(22),
        name="mlp",
    )(
        place, places, *g_got, x_rows, o_a, o_b, later, later, later,
        proj_shift, gain_two, shift_two, in_shift, out_shift,
    )
    out_rows, made = made[: move.count], made[move.count :]
    dh, dow, in_keep, in_send, out_keep, out_send, proj_keep, proj_send, *made = made
    grad_in_shift, vec_two = made

    mine = jnp.concatenate(
        [
            plus(in_keep, swap(in_send, "tp", 1)),
            plus(out_keep, swap(out_send, "tp", 1)),
            plus(proj_keep, swap(proj_send, "tp", 1)),
        ],
        axis=-1,
    )
    far = mine[1]
    out_cells = move.leave(out_rows)
    out_got = move.exchange(out_cells)
    far_got = swap(far, "tp", 2)

    def back(pair, weights, given, extra, last):
        specs = [
            whole((width, ROWS)), w_block, w_block, chunk((ROWS, 3 * GROUP)),
            pl.BlockSpec((ROWS, GROUP), lambda i, *_: (0, 2 * pair + i)),
            chunk((PAIR * heads, PADDED)), bias_block, feature, feature,
        ]
        specs += [whole(v.shape) for v in extra]
        made = [shaped((ROWS, width))]
        if last:
            made = [*move.rows_shapes(width), shaped((2, width))]
        made_specs = [whole(v.shape) for v in made]
        made += [
            shaped((width, 3 * GROUP), bf16),
            shaped((width, 3 * GROUP), bf16),
            shaped((2, 1, 3 * GROUP)),
            shaped((2 * heads, PADDED, PADDED)),
        ]
        made_specs += [
            whole((width, 3 * GROUP)), whole((width, 3 * GROUP)), chunk((1, 3 * GROUP)), bias_block,
        ]
        scratch = [
            pltpu.VMEM((ROWS, width), f32), pltpu.VMEM((ROWS, 3 * GROUP), bf16), w_scratch,
        ]
        return pl.pallas_call(
            functools.partial(attention_back_kernel, last, move.count),
            grid_spec=pltpu.PrefetchScalarGridSpec(
                num_scalar_prefetch=1,
                grid=(2,),
                in_specs=specs,
                out_specs=made_specs,
                scratch_shapes=scratch + (move.stacks(width) if last else []),
            ),
            out_shape=made,
            compiler_params=room(60),
            cost_estimate=cost(19),
            name="attention_back",
        )(place, a1_t, *weights, *given, ours, theirs, *extra)

    dow_b = after(dow, far, out_cells)
    running, keep_b, send_b, shift_b, sums_b = back(1, w_b, (qkv_b, dow_b, lse_b, bias_b), (), False)

    start = lax.axis_index("tp") * move.share
    zero = jnp.zeros((), jnp.int32)
    mine = plus(mine[0], after(far_got, keep_b))
    mine = split_rows(mine, 0)
    steps = list(reversed(bits_of("grp")))
    near_b = swap(send_b, "tp", 1)
    keep, send = halves(mine, 0, steps[0])
    got_first = swap(send, "grp", steps[0])
    out_got = after(out_got, keep_b)
    out_part = move.positions(out_got, zero, None, move.share, bf16)
    output = lax.all_gather(out_part, "tp", axis=0, tiled=True)
    far_b = plus(keep_b, near_b)
    far_got_b = swap(far_b, "tp", 2)
    running = after(running, far_b, out_part, send)
    made = back(0, w_a, (qkv_a, dow, lse_a, bias_a), (running, x_rows, gain_one, dh), True)
    gx, made = made[: move.count], made[move.count :]
    vec_one, keep_a, send_a, shift_a, sums_a = made

    gx_cells = move.leave(after(tuple(gx), got_first))
    gx_got = move.exchange(gx_cells)
    near_a = swap(after(send_a, gx_cells), "tp", 1)

    def table_of(pair_sums):
        return pl.pallas_call(
            table_kernel,
            grid=(2,),
            in_specs=[bias_block, whole((PICK_ROWS, 256))],
            out_specs=pl.BlockSpec((heads, 1, TABLE_PAD), lambda i: (i, 0, 0)),
            out_shape=shaped((2 * heads, 1, TABLE_PAD)),
            scratch_shapes=[
                pltpu.VMEM((heads, SIDE_PAD, DIAG_PAD), f32),
                pltpu.VMEM((heads, SIDE_PAD, TABLE_PAD), f32),
            ],
            compiler_params=room(60),
            cost_estimate=cost(6),
            name="table",
        )(pair_sums, pick)

    def rows_of(*parts):
        return jnp.concatenate([part.reshape(-1) for part in parts]).reshape(-1, 3 * GROUP)

    def slot(tables, shifts, which, in_slot):
        return (tables[which * heads : (which + 1) * heads], shifts[which], grad_in_shift[in_slot])

    tables_b = table_of(after(sums_b, gx_cells, output))
    gx_part = after(gx_got, tables_b)
    keep, send = halves(plus(after(keep, gx_part), got_first), 0, steps[1])
    got_second = swap(send, "grp", steps[1])
    gx_near = tuple(swap(piece, "tp", 1) for piece in gx_part)
    cut_at = -(-move.count // 2)
    far_one = tuple(swap(piece, "tp", 2) for piece in gx_part[:cut_at])
    got_a = plus(plus(keep_a, near_a), far_got_b)
    got_a = split_rows(got_a, 0)
    grad_tokens = move.positions(gx_part, start, None, clips, f32)
    tables_a = table_of(after(sums_a, gx_part, send))
    vec = rows_of(vec_one, vec_two)
    small = rows_of(vec, *slot(tables_a, shift_a, 0, 0), *slot(tables_b, shift_b, 0, 2))
    sent = rows_of(vec, *slot(tables_a, shift_a, 1, 1), *slot(tables_b, shift_b, 1, 3))
    sent = after(sent, far_one, got_second)
    small = small + swap(sent, "tp", 1)
    far_two = tuple(swap(piece, "tp", 2) for piece in after(gx_part[cut_at:], sent))
    mine = plus(keep, got_second)
    for bit in steps[2:]:
        keep, send = halves(mine, 0, bit)
        mine = plus(keep, swap(send, "grp", bit))
    mine = mine.reshape(depth, 2 * hidden + GROUP).astype(f32)
    lead = vec.shape[0]
    cut = lead + (small.shape[0] - lead) // 2
    small = small[:cut] + swap(jnp.concatenate([small[:lead], small[cut:]]), "tp", 2)

    for i, bit in enumerate(steps):
        keep, send = halves(got_a, 0, bit)
        high = lax.reduce_precision(small, 8, 7)
        low = (small - high).astype(bf16)
        size = send.size // (3 * GROUP)
        sent = jnp.concatenate([send.reshape(size, 3 * GROUP), high.astype(bf16), low])
        if i == 1:
            sent = after(sent, far_two)
        got = swap(sent, "grp", bit)
        got_a = plus(keep, got[:size].reshape(keep.shape))
        got = got[size:].astype(f32)
        small = small + got[:cut] + got[cut:]
    got_a = got_a.reshape(depth, 3, GROUP).astype(f32)
    vec = small[:lead].reshape(6, width)
    vec = lax.dynamic_slice_in_dim(vec, lax.axis_index("grp") * depth, depth, 1)
    small = small[lead:].reshape(-1)
    got_table = small[: heads * TABLE_PAD].reshape(heads, TABLE_PAD)[:, :TABLE].T
    got_shift = small[heads * TABLE_PAD :][: 3 * GROUP].reshape(3, GROUP)
    got_in_shift = small[heads * TABLE_PAD + 3 * GROUP :]

    me = lax.axis_index("tp")
    gx_far = far_one + far_two
    gx_last = tuple(swap(piece, "tp", 1) for piece in gx_far)
    for slot_at, piece in ((1, gx_near), (2, gx_far), (3, gx_last)):
        grad_tokens = move.positions(piece, (me ^ slot_at) * move.share, grad_tokens, clips, f32)
    return (
        output,
        grad_tokens,
        vec[0],
        vec[1],
        got_a,
        jnp.stack([got_shift[0], got_shift[2]]),
        got_table,
        mine[:, 2 * hidden :],
        vec[4],
        vec[2],
        vec[3],
        mine[:, :hidden],
        got_in_shift,
        mine[:, hidden : 2 * hidden],
        vec[5],
    )


def solution(mesh):
    shard = P("grp")
    tokens = P(None, "grp", None)
    placed = (
        tokens, tokens, shard, shard, P("grp", None, "tp"), P(None, "tp"), P(None, "tp"),
        P("grp", "tp"), shard, shard, shard, P("grp", "tp"), P("tp"), P("grp", "tp"), shard,
    )
    return jax.shard_map(
        per_device, mesh=mesh, in_specs=placed, out_specs=placed, check_vma=False
    )
```

```python
import functools

import jax
import jax.numpy as jnp
import numpy as np
from jax import lax
from jax.experimental import pallas as pl
from jax.experimental.pallas import tpu as pltpu
from jax.sharding import PartitionSpec as P

CT, CH, CW = 16, 14, 14
WT, WH, WW = 8, 7, 7
ST, SH, SW = 4, 3, 3
FRAME = CH * CW
SIDE = WH * WW
WIN = WT * SIDE
PAIR = 2
PADDED = -(-WIN // 16) * 16
ROWS = PAIR * PADDED
HEAD = 32
GROUP = 128
HEADS_IN = GROUP // HEAD
SPAN_T, SPAN_H, SPAN_W = 2 * WT - 1, 2 * WH - 1, 2 * WW - 1
PLANE = SPAN_H * SPAN_W
TABLE = SPAN_T * PLANE
TABLE_PAD = -(-TABLE // 128) * 128
LANES = 64
DIAG_PAD = (SPAN_T + 1) * LANES
KEYS = -(-SIDE // 8) * 8
ALL_KEYS, ALL_QUERIES = WT * KEYS, WT * LANES
CORNER = PLANE // 2
LOG2E = 1.4426950408889634
SCALE = HEAD ** (-0.5)
FAR = -(2.0**100)
f32 = jnp.float32
bf16 = jnp.bfloat16


def room(mib):
    return pltpu.CompilerParams(vmem_limit_bytes=mib * 1024 * 1024)


def cost(micros):
    return pl.CostEstimate(flops=int(micros * 1.1e9), bytes_accessed=1 << 20, transcendentals=0)


def dot(a, b):
    return lax.dot_general(a, b, (((1,), (0,)), ((), ())), preferred_element_type=f32)


def dot_t(a, b):
    return lax.dot_general(a, b, (((1,), (1,)), ((), ())), preferred_element_type=f32)


def moments(rows):
    centered = rows - jnp.mean(rows, axis=-1, keepdims=True)
    inverse = lax.rsqrt(jnp.mean(centered * centered, axis=-1, keepdims=True) + 1e-05)
    return centered * inverse, inverse


def norm_back(grad, unit, inverse, gain):
    scaled = grad * gain
    shared = jnp.mean(scaled, axis=-1, keepdims=True)
    along = jnp.mean(scaled * unit, axis=-1, keepdims=True)
    return inverse * (scaled - shared - unit * along)


def read_rows(target, ref, frames):
    if not frames:
        target[...] = ref[...].astype(f32)
        return
    count, _, size, _ = ref.shape
    for window in range(PAIR):
        for i in range(count):
            start = window * PADDED + i * frames * SIDE
            target[pl.ds(start, size), :] = ref[i, window].astype(f32)
        start = window * PADDED + WIN
        target[pl.ds(start, PADDED - WIN), :] = jnp.zeros((PADDED - WIN, target.shape[1]), f32)


def write_rows(ref, source, frames):
    if not frames:
        ref[...] = source[...].astype(bf16)
        return
    count, _, size, _ = ref.shape
    for window in range(PAIR):
        for i in range(count):
            start = window * PADDED + i * frames * SIDE
            ref[i, window] = source[pl.ds(start, size), :].astype(bf16)


def cells_kernel(facts_ref, tokens_ref, order_ref, out_ref):
    size, block = out_ref.shape[2], order_ref.shape[0] // 4
    rows = dot(order_ref[...], tokens_ref[0])
    for i in range(4):
        out_ref[i // 2, i % 2] = rows[i * block : i * block + size].astype(bf16)


def home_kernel(count, facts_ref, *refs):
    order_ref = refs[count]
    out_ref, rows = refs[-2:]
    step = pl.program_id(0)
    size, block = refs[0].shape[2], rows.shape[0] // 4

    @pl.when(step == 0)
    def _():
        rows[...] = jnp.zeros_like(rows)

    for clip in range(out_ref.shape[0]):
        for device in range(count):

            @pl.when(step == device)
            def _():
                for i in range(4):
                    piece = refs[device][2 * clip + i // 2, i % 2]
                    rows[i * block : i * block + size, :] = piece.astype(f32)

        out_ref[clip] = dot(order_ref[...], rows[...].astype(bf16)).astype(out_ref.dtype)


SPANS = []
for _lane in range(0, DIAG_PAD, 256):
    _low = _lane // LANES * PLANE // 128 * 128
    _high = min((_lane + 255) // LANES + 1, SPAN_T) * PLANE
    SPANS.append((_lane, _low, -(-_high // 128) * 128))
PICK_ROWS = sum(high - low for _, low, high in SPANS)


def bias_kernel(table_ref, pick_ref, bias_ref, sheared):
    heads = bias_ref.shape[0]
    tables = table_ref[0].astype(f32)
    for head in range(heads):
        flat = jnp.broadcast_to(tables[head : head + 1], (8, TABLE_PAD))
        stairs = pltpu.roll(flat, 0, 1, stride=1, stride_axis=0)
        for row in range(WH):
            shift = (row * SPAN_W - CORNER) % TABLE_PAD
            sheared[head, pl.ds(row * WW, 8), :] = pltpu.roll(stairs, shift, 1)
        sheared[head, SIDE:KEYS, :] = jnp.zeros((KEYS - SIDE, TABLE_PAD), f32)
    everything = sheared[...].reshape(heads * KEYS, TABLE_PAD).astype(bf16)
    start = 0
    for lane, low, high in SPANS:
        part = dot(everything[:, low:high], pick_ref[start : start + high - low]) * LOG2E
        bias_ref[:, :, lane : lane + 256] = part.reshape(heads, KEYS, 256)
        start += high - low


def table_kernel(sums_ref, pick_ref, grad_ref, sheared):
    heads = sums_ref.shape[0]
    everything = sums_ref[...].reshape(heads * KEYS, DIAG_PAD).astype(bf16)
    done = 0
    start = 0
    for lane, low, high in SPANS:
        part = dot_t(everything[:, lane : lane + 256], pick_ref[start : start + high - low])
        part = part.reshape(heads, KEYS, high - low)
        if done > low:
            sheared[:, :, low:done] += part[:, :, : done - low]
            sheared[:, :, done:high] = part[:, :, done - low :]
        else:
            sheared[:, :, low:high] = part
        done = high
        start += high - low
    row_in = lax.broadcasted_iota(jnp.int32, (8, TABLE_PAD), 0)
    for head in range(heads):
        stairs = jnp.zeros((8, TABLE_PAD), f32)
        for row in range(WH):
            shift = (CORNER - row * SPAN_W) % TABLE_PAD
            stairs = stairs + pltpu.roll(sheared[head, pl.ds(row * WW, 8), :], shift, 1)
        flat = jnp.where(row_in == 0, stairs, 0.0)
        for step in range(1, WW):
            moved = pltpu.roll(stairs, TABLE_PAD - step, 1)
            flat = flat + jnp.where(row_in == step, moved, 0.0)
        grad_ref[head] = jnp.sum(flat, axis=0, keepdims=True)


def spread_frames(source, window, columns, stride):
    place = lax.broadcasted_iota(jnp.int32, (KEYS, GROUP), 0)
    parts = []
    for frame in range(WT):
        rows = source[pl.ds(window * PADDED + frame * SIDE, KEYS), columns]
        parts.append(jnp.where(place < SIDE, rows, 0.0))
        if stride > KEYS:
            parts.append(jnp.zeros((stride - KEYS, GROUP), f32))
    return jnp.concatenate(parts, axis=0)


def close_frames(target, window, columns, rows, stride):
    for frame in range(WT):
        place = pl.ds(window * PADDED + frame * SIDE, KEYS)
        target[place, columns] = rows[frame * stride : frame * stride + KEYS]
    place = slice(window * PADDED + WIN, (window + 1) * PADDED)
    target[place, columns] = jnp.zeros((PADDED - WIN, GROUP), f32)


def turn_bias(target, bias_ref):
    for head in range(bias_ref.shape[0]):
        target[head, 0] = bias_ref[head]
        target[head, 1] = pltpu.roll(bias_ref[head], DIAG_PAD - LANES, 1)


def frame_bias(head, frame, lanes):
    start = (WT - 1 - frame) * LANES
    copy = start // LANES % 2
    start = start - copy * LANES + lanes
    return (head, copy, slice(None), slice(start, start + 256))


def by_tile(rows, how):
    return how(rows.reshape(rows.shape[0] // 8, 8, rows.shape[1]), axis=0)


def mask_heads(target, rows, lane):
    for head in range(HEADS_IN):
        masked = jnp.where(lane == head, rows, jnp.zeros_like(rows))
        target[head * ALL_KEYS : (head + 1) * ALL_KEYS, 0:GROUP] = masked


def attention_kernel(first, frames, *refs):
    step = pl.program_id(0)
    refs = refs[1:]
    if first:
        got_ref, gain_ref, shift_ref, w0_ref, w1_ref, wb_ref, bias_ref, qf_ref, kf_ref = refs[:9]
        x_ref, a1_ref, a1_t_ref, q_ref, k_ref, v_ref, o_ref, lse_ref = refs[9:17]
        w_ref, wide, keys, logits, probs, rows_o, bias, rows_in = refs[17:]

        @pl.when(step == 0)
        def _():
            read_rows(rows_in, got_ref, frames)
            x_ref[...] = rows_in[...].astype(bf16)
            unit, _ = moments(rows_in[...])
            low = unit * gain_ref[...] + shift_ref[...]
            a1_ref[...] = low.astype(bf16)
            a1_t_ref[...] = low.T.astype(bf16)
    else:
        a1_ref, w0_ref, w1_ref, wb_ref, bias_ref, qf_ref, kf_ref = refs[:7]
        q_ref, k_ref, v_ref, o_ref, lse_ref = refs[7:12]
        w_ref, wide, keys, logits, probs, rows_o, bias = refs[12:]

    @pl.when(step == 0)
    def _():
        w_ref[...] = w0_ref[...]

    @pl.when(step == 1)
    def _():
        w_ref[...] = w1_ref[...]

    turn_bias(bias, bias_ref)
    shift = wb_ref[0].astype(f32)[HEADS_IN : HEADS_IN + 1]
    nothing = jnp.zeros((1, GROUP), f32)
    shift = jnp.concatenate([shift[:, :GROUP], nothing, shift[:, GROUP : 2 * GROUP]], axis=1)
    wide[...] = dot(a1_ref[...], w_ref[...]) + shift
    lane = lax.broadcasted_iota(jnp.int32, (ALL_KEYS, GROUP), 1) // HEAD
    for window in range(PAIR):
        query = spread_frames(wide, window, slice(0, GROUP), LANES).astype(bf16)
        key = spread_frames(wide, window, slice(GROUP, 2 * GROUP), KEYS).astype(bf16)
        value = spread_frames(wide, window, slice(2 * GROUP, 3 * GROUP), KEYS)
        q_ref[0, window] = query
        k_ref[0, window] = key
        v_ref[0, window] = value.astype(bf16)
        value_t = value.T.astype(bf16)
        mask_heads(keys, key, lane)
        for head in range(HEADS_IN):
            keys[head * ALL_KEYS : (head + 1) * ALL_KEYS, GROUP : 2 * GROUP] = kf_ref[0, window]
        logits[...] = dot_t(keys[...], jnp.concatenate([query, qf_ref[0, window]], axis=1))
        parts = []
        for head in range(HEADS_IN):
            tops, totals = [], []
            for lanes in range(0, ALL_QUERIES, 256):
                across = slice(lanes, lanes + 256)
                top = jnp.full((8, 256), -jnp.inf, f32)
                for frame in range(WT):
                    at = head * ALL_KEYS + frame * KEYS
                    block = logits[at : at + KEYS, across] * (SCALE * LOG2E)
                    block = block + bias[frame_bias(head, frame, lanes)]
                    logits[at : at + KEYS, across] = block
                    top = jnp.maximum(top, by_tile(block, jnp.max))
                top = jnp.max(top, axis=0, keepdims=True)
                total = jnp.zeros((8, 256), f32)
                for pair in range(0, ALL_KEYS, 2 * KEYS):
                    at = head * ALL_KEYS + pair
                    block = jnp.exp2(logits[at : at + 2 * KEYS, across] - top)
                    total = total + by_tile(block, jnp.sum)
                    probs[pair : pair + 2 * KEYS, across] = block.astype(bf16)
                tops.append(top)
                totals.append(jnp.sum(total, axis=0, keepdims=True))
            total = jnp.concatenate(totals, axis=1)
            lse = jnp.concatenate(tops, axis=1) + jnp.log2(total)
            lse_ref[0, pl.ds(window * HEADS_IN + head, 1), :] = lse
            mixed = dot(value_t[head * HEAD : (head + 1) * HEAD], probs[...])
            parts.append(mixed / total)
        mixed = jnp.concatenate(parts, axis=0).T
        close_frames(rows_o, window, slice(None), mixed, LANES)
    o_ref[...] = rows_o[...].astype(bf16)


def mlp_kernel(frames, facts_ref, *refs):
    got_ref, x_ref, oa_ref, ob_ref = refs[:4]
    weights, home_ref, away_ref = refs[4:8], refs[8], refs[9]
    pb_ref, gain_ref, shift_ref, near_ref, far_ref, out_shift_ref = refs[10:16]
    out_ref, refs = refs[16], refs[17:]
    dh_ref, dow_ref, gwi_keep, gwi_send, gwo_keep, gwo_send, gwp_keep, gwp_send = refs[:8]
    gib_ref, vec_ref = refs[8:10]
    hidden, a2, a2_t, g_ref, g_t, unit_s, inv_s, acc_out, acc_in, o_all, wp = refs[10:21]
    wi, wo, ib_ref, u_s, back_s, act, du, grad_out_w, grad_in_w = refs[21:]
    step = pl.program_id(0)
    width = x_ref.shape[1]
    units = gib_ref.shape[2]

    @pl.when(step == 0)
    def _():
        o_all[:, 0 : 2 * GROUP] = oa_ref[...]
        o_all[:, 2 * GROUP : 4 * GROUP] = ob_ref[...]
        for i, ref in enumerate(weights):
            wp[:, i * GROUP : (i + 1) * GROUP] = ref[:, units : units + GROUP]
        branch = dot_t(o_all[...], wp[...])
        hidden[...] = x_ref[...].astype(f32) + branch + pb_ref[...]
        unit, inverse = moments(hidden[...])
        unit_s[...] = unit
        inv_s[...] = inverse
        low = unit * gain_ref[...] + shift_ref[...]
        a2[...] = low.astype(bf16)
        a2_t[...] = low.T.astype(bf16)
        read_rows(acc_out, got_ref, frames)
        g_ref[...] = acc_out[...].astype(bf16)
        g_t[...] = acc_out[...].T.astype(bf16)
        acc_out[...] = jnp.zeros_like(acc_out)
        acc_in[...] = jnp.zeros_like(acc_in)

    for i, slot in enumerate((1, 3, 0, 2)):

        @pl.when(step == i)
        def _():
            wi[...] = weights[slot][:, 0:units]
            wo[...] = (away_ref if slot % 2 else home_ref)[0]
            shifts = (near_ref if slot < 2 else far_ref)[slot % 2].astype(f32)
            ib_ref[...] = shifts[HEADS_IN + 1 : HEADS_IN + 2, 0:units]

    for first in range(0, units, 256):
        some = slice(first, first + 256)
        u_s[...] = dot(a2[...], wi[:, some])
        back_s[...] = dot(g_ref[...], wo[:, some])
        sums = jnp.zeros((8, 256), f32)
        for row in range(0, ROWS, 80):
            rows = slice(row, row + 80)
            u = u_s[rows] + ib_ref[:, some]
            half = 0.5 * (1.0 + lax.erf(u * (0.5**0.5)))
            act[rows, some] = (u * half).astype(bf16)
            slope = half + u * jnp.exp(-0.5 * u * u) * 0.3989422804014327
            low = (back_s[rows] * slope).astype(bf16)
            du[rows, some] = low
            sums = sums + by_tile(low.astype(f32), jnp.sum)
        gib_ref[0, :, some] = jnp.sum(sums, axis=0, keepdims=True)
        grad_out_w[:, some] = dot(g_t[...], act[:, some]).astype(bf16)
        grad_in_w[:, some] = dot(a2_t[...], du[:, some]).astype(bf16)
    acc_out[...] += dot_t(act[...], wo[...])
    acc_in[...] += dot_t(du[...], wi[...])

    @pl.when(step < 2)
    def _():
        gwo_send[0] = grad_out_w[...]
        gwi_send[0] = grad_in_w[...]

    @pl.when(step >= 2)
    def _():
        gwo_keep[0] = grad_out_w[...]
        gwi_keep[0] = grad_in_w[...]

    @pl.when(step == pl.num_programs(0) - 1)
    def _():
        acc_out[...] += hidden[...] + out_shift_ref[...]
        write_rows(out_ref, acc_out, frames)
        upstream = g_ref[...].astype(f32)
        grad = acc_in[...]
        unit = unit_s[...]
        dh = upstream + norm_back(grad, unit, inv_s[...], gain_ref[...])
        dh_ref[...] = dh
        dz = dh.astype(bf16)
        dow_ref[...] = dot(dz, wp[...]).astype(bf16)
        grad_wp = dot(dz.astype(f32).T.astype(bf16), o_all[...])
        for i in range(2):
            gwp_keep[i] = grad_wp[:, 2 * i * GROUP : (2 * i + 1) * GROUP].astype(bf16)
            gwp_send[i] = grad_wp[:, (2 * i + 1) * GROUP : (2 * i + 2) * GROUP].astype(bf16)
        vec_ref[...] = jnp.concatenate(
            [
                jnp.sum(grad * unit, axis=0, keepdims=True),
                jnp.sum(grad, axis=0, keepdims=True),
                jnp.sum(dz.astype(f32), axis=0, keepdims=True),
                jnp.sum(upstream, axis=0, keepdims=True),
            ],
            axis=0,
        )


def attention_back_kernel(last, frames, facts_ref, *refs):
    a1_t_ref, w0_ref, w1_ref, q_ref, k_ref, v_ref, dow_ref, lse_ref, bias_ref, qf_ref, kf_ref = refs[:11]
    refs = refs[11:]
    if last:
        sum_ref, x_ref, gain_ref, dh_ref, gx_ref, vec_ref = refs[:6]
        refs = refs[6:]
    else:
        sum_ref, refs = refs[0], refs[1:]
    keep_ref, send_ref, gb_ref, sums_ref, acc, dqkv, w_ref = refs[:7]
    rows_in, keys, values, probs_f, dp, probs, ds, shifted, bias = refs[7:]
    step = pl.program_id(0)

    @pl.when(step == 0)
    def _():
        w_ref[...] = w0_ref[...]

    @pl.when(step == 1)
    def _():
        w_ref[...] = w1_ref[...]

    shifted[...] = jnp.zeros_like(shifted)
    turn_bias(bias, bias_ref)
    rows_in[...] = dow_ref[...].astype(f32)
    lane = lax.broadcasted_iota(jnp.int32, (ALL_KEYS, GROUP), 1) // HEAD
    for window in range(PAIR):
        query, key, value = q_ref[0, window], k_ref[0, window], v_ref[0, window]
        dow = spread_frames(rows_in, window, slice(None), LANES).astype(bf16)
        key_t = key.astype(f32).T.astype(bf16)
        mask_heads(keys, key, lane)
        mask_heads(values, value, lane)
        for head in range(HEADS_IN):
            keys[head * ALL_KEYS : (head + 1) * ALL_KEYS, GROUP : 2 * GROUP] = kf_ref[0, window]
        probs_f[...] = dot_t(keys[...], jnp.concatenate([query, qf_ref[0, window]], axis=1))
        dp[...] = dot_t(values[...], dow)
        for head in range(HEADS_IN):
            lse = lse_ref[0, pl.ds(window * HEADS_IN + head, 1), :]
            for lanes in range(0, ALL_QUERIES, 256):
                across = slice(lanes, lanes + 256)
                dots = jnp.zeros((8, 256), f32)
                for pair in range(0, WT, 2):
                    blocks = []
                    for frame in (pair, pair + 1):
                        at = head * ALL_KEYS + frame * KEYS
                        block = probs_f[at : at + KEYS, across] * (SCALE * LOG2E)
                        block = block + bias[frame_bias(head, frame, lanes)]
                        blocks.append(block)
                    at = head * ALL_KEYS + pair * KEYS
                    block = jnp.exp2(jnp.concatenate(blocks, axis=0) - lse[:, across])
                    probs_f[at : at + 2 * KEYS, across] = block
                    probs[at : at + 2 * KEYS, across] = block.astype(bf16)
                    dots = dots + by_tile(block * dp[at : at + 2 * KEYS, across], jnp.sum)
                dots = jnp.sum(dots, axis=0, keepdims=True)
                for pair in range(0, WT, 2):
                    at = head * ALL_KEYS + pair * KEYS
                    block = probs_f[at : at + 2 * KEYS, across]
                    block = block * (dp[at : at + 2 * KEYS, across] - dots)
                    ds[at : at + 2 * KEYS, across] = block.astype(bf16)
                    for i in range(2):
                        place = frame_bias(head, pair + i, lanes)
                        shifted[place] += block[i * KEYS : (i + 1) * KEYS]
        dv_all = dot(probs[...], dow)
        dk_all = dot(ds[...], query)
        none = jnp.zeros((ALL_KEYS, GROUP), f32)
        dk, dv, dq_t = none, none, []
        for head in range(HEADS_IN):
            part = slice(head * ALL_KEYS, (head + 1) * ALL_KEYS)
            dv = jnp.where(lane == head, dv_all[part], dv)
            dk = jnp.where(lane == head, dk_all[part], dk)
            dq_t.append(dot(key_t[head * HEAD : (head + 1) * HEAD], ds[part]))
        dq = jnp.concatenate(dq_t, axis=0).T
        close_frames(dqkv, window, slice(0, GROUP), dq * SCALE, LANES)
        close_frames(dqkv, window, slice(GROUP, 2 * GROUP), dk * SCALE, KEYS)
        close_frames(dqkv, window, slice(2 * GROUP, 3 * GROUP), dv, KEYS)
    for head in range(HEADS_IN):
        sums_ref[head] = shifted[head, 0] + pltpu.roll(shifted[head, 1], LANES, 1)
    low = dqkv[...].astype(bf16)
    grad = dot_t(low, w_ref[...])
    grad_w = dot(a1_t_ref[...], low)
    gb_ref[0] = jnp.sum(low.astype(f32), axis=0, keepdims=True)

    @pl.when(step == 0)
    def _():
        acc[...] = grad + sum_ref[...] if last else grad
        keep_ref[...] = grad_w.astype(bf16)

    @pl.when(step == 1)
    def _():
        send_ref[...] = grad_w.astype(bf16)
        total = acc[...] + grad
        if last:
            unit, inverse = moments(x_ref[...].astype(f32))
            acc[...] = dh_ref[...] + norm_back(total, unit, inverse, gain_ref[...])
            write_rows(gx_ref, acc, frames)
            vec_ref[...] = jnp.concatenate(
                [jnp.sum(total * unit, axis=0, keepdims=True), jnp.sum(total, axis=0, keepdims=True)],
                axis=0,
            )
        else:
            sum_ref[...] = total


def whole(shape):
    return pl.BlockSpec(shape, lambda *i: (0,) * len(shape))


def shaped(shape, kind=f32):
    return jax.ShapeDtypeStruct(shape, kind)


def chunk(shape):
    return pl.BlockSpec((1,) + shape, lambda i, *_: (i,) + (0,) * len(shape))


def pick_matrix():
    place = np.arange(TABLE_PAD)
    row, column = place % PLANE // SPAN_W, place % PLANE % SPAN_W
    target = place // PLANE * LANES + row * WW + column
    good = (place < TABLE) & (row < WH) & (column < WW)
    target = np.where(good, target, -1)
    target = np.concatenate([target[low:high] - lane for lane, low, high in SPANS])
    return jnp.asarray(np.arange(256) == target[:, None], bf16)


def region_features():
    lane = np.arange(GROUP)

    def codes(stride, is_late, is_low, is_right):
        frame, cell = np.divmod(np.arange(WT * stride), stride)
        code = (
            (is_late * (frame >= WT - ST)) * 4
            + (is_low * (cell // WW >= WH - SH)) * 2
            + is_right * (cell % WW >= WW - SW)
        )
        return (cell < SIDE)[:, None], code[:, None]

    ours, theirs = [], []
    for is_late in range(2):
        for is_low in range(2):
            for is_right in range(PAIR):
                real, code = codes(LANES, is_late, is_low, is_right)
                ours.append((real & (lane == code)) | (lane == 8))
                real, code = codes(KEYS, is_late, is_low, is_right)
                other = np.where(real, (lane < 8) & (lane != code), lane == 8)
                theirs.append(np.where(other, FAR, 0.0))
    ours = jnp.asarray(np.reshape(ours, (4, PAIR, ALL_QUERIES, GROUP)), bf16)
    return ours, jnp.asarray(np.reshape(theirs, (4, PAIR, ALL_KEYS, GROUP)), bf16)


def cell_order(frames):
    size = frames * SIDE
    step = -(-size // 16) * 16
    matrix = np.zeros((4 * step, frames * FRAME), bool)
    for low in range(2):
        for right in range(2):
            for cell in range(size):
                frame, row, column = cell // SIDE, cell // WW % WH, cell % WW
                row = (low * WH + row + SH) % CH
                column = (right * WW + column + SW) % CW
                place = frame * FRAME + row * CW + column
                matrix[(low * 2 + right) * step + cell, place] = True
    return matrix


class Windows:
    def __init__(self, clips, local, groups, shares):
        self.share = clips // shares
        self.local = local
        self.half = groups // 2
        first = ST * FRAME // local
        order = [(first + i) % groups for i in range(groups)]
        self.groups = [order[: self.half], order[self.half :]]
        self.frames = local // FRAME if local % FRAME == 0 else 0
        slot = (lax.axis_index("grp") - first) % groups
        self.low = slot % 2
        me = lax.axis_index("tp")
        order = [me * self.share, slot // self.half * 2 + self.low]
        order += [me ^ i for i in range(shares)]
        self.facts = lax.optimization_barrier(jnp.stack(order).astype(jnp.int32))

    def exchange(self, rows):
        return lax.all_to_all(
            rows, "grp", split_axis=0, concat_axis=0, tiled=True, axis_index_groups=self.groups
        )

    def shape(self, width):
        if not self.frames:
            return (ROWS, width)
        return (self.half, 2, -(-self.frames * SIDE // 8) * 8, width)

    def before(self, field):
        width = field.shape[-1]
        place = lax.axis_index("tp") * self.share
        if not self.frames:
            own = lax.dynamic_slice_in_dim(field, place, self.share, 0)
            return jnp.repeat(own, 2, axis=0)
        order = jnp.asarray(cell_order(self.frames), bf16)
        shape = self.shape(width)
        return pl.pallas_call(
            cells_kernel,
            grid_spec=pltpu.PrefetchScalarGridSpec(
                num_scalar_prefetch=1,
                grid=(self.share,),
                in_specs=[
                    pl.BlockSpec((1, self.local, width), lambda i, facts: (facts[0] + i, 0, 0)),
                    whole(order.shape),
                ],
                out_specs=pl.BlockSpec((2,) + shape[1:], lambda i, facts: (i, 0, 0, 0)),
            ),
            out_shape=shaped(shape, bf16),
            compiler_params=room(60),
            cost_estimate=cost(3),
            name="cells",
        )(self.facts, field, order)

    def home(self, parts, first, into, kind):
        width = parts[0].shape[-1]
        size = lax.axis_size("tp")
        clips = size * self.share
        if not self.frames:
            if into is None:
                into = jnp.zeros((clips, self.local, width), kind)
            for i, part in enumerate(parts):
                part = part.reshape(self.share, 2, self.local, width)
                part = (part[:, 0] + part[:, 1]).astype(kind)
                start = (lax.axis_index("tp") ^ (first + i)) * self.share
                into = lax.dynamic_update_slice_in_dim(into, part, start, 0)
            return into
        order = jnp.asarray(cell_order(self.frames).T, bf16)
        extra = [] if into is None else [into]

        def place(step, facts):
            return (facts[2 + first + step], 0, 0)

        return pl.pallas_call(
            functools.partial(home_kernel, len(parts)),
            grid_spec=pltpu.PrefetchScalarGridSpec(
                num_scalar_prefetch=1,
                grid=(len(parts),),
                in_specs=[whole(parts[0].shape)] * len(parts)
                + [whole(order.shape)]
                + [pl.BlockSpec(memory_space=pl.ANY)] * len(extra),
                out_specs=pl.BlockSpec((self.share, self.local, width), place),
                scratch_shapes=[pltpu.VMEM((order.shape[1], width), f32)],
            ),
            out_shape=shaped((clips, self.local, width), kind),
            input_output_aliases={len(parts) + 2: 0} if extra else {},
            compiler_params=room(60),
            cost_estimate=cost(3),
            name="home",
        )(self.facts, *parts, order, *extra)

    def arrange(self, cells):
        if self.frames:
            return cells
        width = cells.shape[-1]
        cells = cells.reshape(WT, CH, CW, width)
        cells = jnp.roll(cells, (-SH, -SW), axis=(1, 2))
        cells = lax.dynamic_slice_in_dim(cells, self.low * WH, WH, 1)
        cells = cells.reshape(WT, WH, 2, WW, width).transpose(2, 0, 1, 3, 4)
        cells = cells.reshape(PAIR, WIN, width)
        cells = jnp.pad(cells, ((0, 0), (0, PADDED - WIN), (0, 0)))
        return cells.reshape(ROWS, width)

    def leave(self, rows):
        if self.frames:
            return rows
        width = rows.shape[-1]
        cells = rows.reshape(PAIR, PADDED, width)[:, :WIN]
        cells = cells.reshape(2, WT, WH, WW, width).transpose(1, 2, 0, 3, 4)
        cells = cells.reshape(WT, WH, CW, width)
        blank = jnp.zeros((WT, CH, CW, width), cells.dtype)
        cells = lax.dynamic_update_slice_in_dim(blank, cells, self.low * WH, 1)
        cells = jnp.roll(cells, (SH, SW), axis=(1, 2))
        return cells.reshape(self.half, self.local, width)


def swap(field, axis, bit):
    size = lax.axis_size(axis)
    return lax.ppermute(field, axis, [(i, i ^ bit) for i in range(size)])


def bits_of(axis):
    size = lax.axis_size(axis)
    return [1 << i for i in reversed(range(size.bit_length() - 1))]


def flag_of(axis, bit):
    return lax.axis_index(axis) // bit % 2


def after(value, *others):
    return lax.optimization_barrier((value, others))[0]


def join(mine, other, bit, axis, place):
    second = flag_of(axis, bit) == 1
    return jnp.concatenate(
        [jnp.where(second, other, mine), jnp.where(second, mine, other)], axis=place
    )


class Gather:
    def __init__(self, part):
        self.bits = bits_of("grp")
        self.shape = part.shape
        self.field = part.reshape((1,) * len(self.bits) + part.shape)
        self.coming = ()
        self.done = 0

    def send(self, *others, double=False):
        self.field = after(self.field, *others)
        bit = self.bits[self.done]
        which = [bit, bit // 2, bit + bit // 2] if double else [bit]
        self.coming = [swap(self.field, "grp", i) for i in which]
        return self.field

    def take(self):
        bit, place = self.bits[self.done], self.done
        if len(self.coming) == 1:
            self.field = join(self.field, self.coming[0], bit, "grp", place)
            self.done += 1
            return
        one, two, both = self.coming
        near = join(self.field, two, bit // 2, "grp", place + 1)
        far = join(one, both, bit // 2, "grp", place + 1)
        self.field = join(near, far, bit, "grp", place)
        self.done += 2

    def result(self):
        return self.field.reshape((self.shape[0] << len(self.bits),) + self.shape[1:])


def plus(one, other):
    return (one.astype(f32) + other.astype(f32)).astype(bf16)


def split_rows(field, lead):
    bits = bits_of("grp")
    shape = field.shape
    rows = shape[lead] >> len(bits)
    return field.reshape(shape[:lead] + (2,) * len(bits) + (rows,) + shape[lead + 1 :])


def halves(field, lead, bit):
    place = lead + bits_of("grp").index(bit)
    mine = flag_of("grp", bit)
    keep = lax.dynamic_index_in_dim(field, mine, place, keepdims=True)
    send = lax.dynamic_index_in_dim(field, 1 - mine, place, keepdims=True)
    return keep, send


def per_device(
    tokens, grad_out, ln1_gain, ln1_shift, w_qkv, qkv_bias, rel_table, w_proj, proj_bias,
    ln2_gain, ln2_shift, w_in, in_bias, w_out, out_bias,
):
    groups, shares = lax.axis_size("grp"), lax.axis_size("tp")
    clips, local, width = tokens.shape
    move = Windows(clips, local, groups, shares)
    depth = w_qkv.shape[0]
    hidden = w_in.shape[1]
    heads = rel_table.shape[1]
    half = shares // 2

    later = Gather(jnp.concatenate([w_in, w_out, w_proj], axis=1))
    later_bits = later.bits
    vectors = jnp.stack([ln1_gain, ln1_shift, proj_bias, ln2_gain, ln2_shift, out_bias])
    first = jnp.concatenate(
        [w_qkv.reshape(depth, 3 * GROUP), jnp.pad(vectors.T, ((0, 0), (0, GROUP - 6)))], axis=1
    )
    first = Gather(first)
    for _ in range(len(first.bits) - 3):
        for chain in (first, later):
            chain.send()
            chain.take()
    split = jnp.concatenate(
        [
            jnp.pad(rel_table.T, ((0, 0), (0, TABLE_PAD - TABLE))),
            jnp.pad(qkv_bias.reshape(1, -1), ((0, 0), (0, TABLE_PAD - qkv_bias.size))),
            jnp.pad(in_bias[None], ((0, 3 - heads % 2), (0, TABLE_PAD - hidden))),
        ]
    )
    split = jnp.stack([split, swap(split, "tp", 1)])
    other_split = swap(split, "tp", 2)

    pick = pick_matrix()
    ours, theirs = region_features()

    def bias_of(half_split):
        return pl.pallas_call(
            bias_kernel,
            grid=(2,),
            in_specs=[chunk(half_split.shape[1:]), whole((PICK_ROWS, 256))],
            out_specs=pl.BlockSpec((heads, KEYS, DIAG_PAD), lambda i: (i, 0, 0)),
            out_shape=shaped((2 * heads, KEYS, DIAG_PAD)),
            scratch_shapes=[pltpu.VMEM((heads, KEYS, TABLE_PAD), f32)],
            compiler_params=room(60),
            cost_estimate=cost(6),
            name="bias",
        )(half_split, pick)

    sent = first.send(double=True)
    sent = sent, later.send(sent)
    x_send = move.before(after(tokens, sent))
    first.take()
    later.take()
    sent = first.send(x_send), later.send(x_send)
    x_got = move.exchange(after(x_send, sent))
    bias_a = bias_of(after(split, sent))
    first.take()
    later.take()
    first, later = after((first.result(), later.field), bias_a)
    bit, at = later_bits[-1], len(later_bits) - 1
    ins = jnp.concatenate([later[..., :hidden], later[..., 2 * hidden :]], axis=-1)
    outs = later[..., hidden : 2 * hidden]
    ins_got = swap(ins, "grp", bit)
    outs_got = swap(outs, "tp", 2)
    vectors = first[:, 3 * GROUP : 3 * GROUP + 6].T.astype(f32)
    gain_one, shift_one, proj_shift, gain_two, shift_two, out_shift = (
        vectors[i : i + 1] for i in range(6)
    )
    own = first[:, : 3 * GROUP]
    place = move.facts
    across = swap(own, "tp", 2)
    w_a = (own, swap(own, "tp", 1))
    x_got = move.arrange(x_got)


    rows, row = whole((ROWS, width)), whole((1, width))
    features = [
        pl.BlockSpec((1, PAIR, size, GROUP), lambda i, facts: (facts[1], 0, 0, 0))
        for size in (ALL_QUERIES, ALL_KEYS)
    ]
    bias_block = pl.BlockSpec((heads, KEYS, DIAG_PAD), lambda i, *_: (i, 0, 0))
    bias_scratch = pltpu.VMEM((heads, 2, KEYS, DIAG_PAD), f32)
    pair_columns = pl.BlockSpec((ROWS, GROUP), lambda i, *_: (0, i))
    query_block, key_block = chunk((PAIR, ALL_QUERIES, GROUP)), chunk((PAIR, ALL_KEYS, GROUP))
    lse_block = chunk((PAIR * heads, ALL_QUERIES))
    pair_specs = [query_block, key_block, key_block, pair_columns, lse_block]
    pair_shapes = [
        shaped((2, PAIR, ALL_QUERIES, GROUP), bf16),
        shaped((2, PAIR, ALL_KEYS, GROUP), bf16),
        shaped((2, PAIR, ALL_KEYS, GROUP), bf16),
        shaped((ROWS, 2 * GROUP), bf16),
        shaped((2, PAIR * heads, ALL_QUERIES)),
    ]
    w_block = whole((width, 3 * GROUP))
    w_specs = [w_block, w_block, chunk(split.shape[1:]), bias_block, *features]
    w_scratch = pltpu.VMEM((width, 3 * GROUP), bf16)
    attention_scratch = [
        w_scratch,
        pltpu.VMEM((ROWS, 3 * GROUP), f32),
        pltpu.VMEM((heads * ALL_KEYS, 2 * GROUP), bf16),
        pltpu.VMEM((heads * ALL_KEYS, ALL_QUERIES), f32),
        pltpu.VMEM((ALL_KEYS, ALL_QUERIES), bf16),
        pltpu.VMEM((ROWS, GROUP), f32),
        bias_scratch,
    ]
    x_rows, a1, a1_t, q_a, k_a, v_a, o_a, lse_a = pl.pallas_call(
        functools.partial(attention_kernel, True, move.frames),
        grid_spec=pltpu.PrefetchScalarGridSpec(
            num_scalar_prefetch=1,
            grid=(2,),
            in_specs=[whole(x_got.shape), row, row, *w_specs],
            out_specs=[rows, rows, whole((width, ROWS)), *pair_specs],
            scratch_shapes=[
                *attention_scratch, pltpu.VMEM((ROWS, width), f32),
            ],
        ),
        out_shape=[
            shaped((ROWS, width), bf16),
            shaped((ROWS, width), bf16),
            shaped((width, ROWS), bf16),
            *pair_shapes,
        ],
        compiler_params=room(60),
        cost_estimate=cost(12),
        name="attention",
    )(place, x_got, gain_one, shift_one, *after(w_a, ins, outs), split, bias_a, ours, theirs)
    ins_got, outs_got, across = after((ins_got, outs_got, across), a1)
    ins = join(ins, ins_got, bit, "grp", at).reshape(width, hidden + GROUP)
    outs = jnp.stack([outs, outs_got])
    far_ins = swap(ins, "tp", 2)
    outs_got = swap(outs, "grp", bit)
    g_send = move.before(after(grad_out, ins, outs, across))
    g_got = move.exchange(g_send)
    bias_b = bias_of(after(other_split, g_send))
    far_ins, outs_got = after((far_ins, outs_got), bias_b)
    outs = join(outs, outs_got, bit, "grp", at + 1).reshape(half, width, hidden)
    near_ins, last_ins = swap(ins, "tp", 1), swap(far_ins, "tp", 1)
    away_outs = swap(outs, "tp", 1)
    w_b = (across, swap(across, "tp", 1))
    q_b, k_b, v_b, o_b, lse_b = pl.pallas_call(
        functools.partial(attention_kernel, False, 0),
        grid_spec=pltpu.PrefetchScalarGridSpec(
            num_scalar_prefetch=1,
            grid=(2,),
            in_specs=[rows, *w_specs],
            out_specs=pair_specs,
            scratch_shapes=attention_scratch,
        ),
        out_shape=pair_shapes,
        compiler_params=room(60),
        cost_estimate=cost(11),
        name="attention",
    )(place, a1, *after(w_b, ins, far_ins, outs), other_split, bias_b, ours, theirs)

    g_got = move.arrange(g_got)
    both = whole((ROWS, 2 * GROUP))
    proj_block = whole((half, width, GROUP))
    keep_spec = pl.BlockSpec((1, width, hidden), lambda i, *_: (jnp.maximum(i - half, 0), 0, 0))
    send_spec = pl.BlockSpec((1, width, hidden), lambda i, *_: (jnp.minimum(i, half - 1), 0, 0))
    unit_spec = pl.BlockSpec(
        (1, 1, hidden), lambda i, *_: (jnp.where(i < half, 2 * i + 1, 2 * i - shares), 0, 0)
    )
    made = pl.pallas_call(
        functools.partial(mlp_kernel, move.frames),
        grid_spec=pltpu.PrefetchScalarGridSpec(
            num_scalar_prefetch=1,
            grid=(shares,),
            in_specs=[
                whole(g_got.shape), rows, both, both,
                *[whole((width, hidden + GROUP))] * shares,
                pl.BlockSpec((1, width, hidden), lambda i, *_: (jnp.maximum(i - half, 0), 0, 0)),
                pl.BlockSpec((1, width, hidden), lambda i, *_: (jnp.minimum(i, half - 1), 0, 0)),
                row, row, row, whole(split.shape), whole(split.shape), row,
            ],
            out_specs=[
                whole(move.shape(width)), rows, rows,
                keep_spec, send_spec, keep_spec, send_spec, proj_block,
                proj_block, unit_spec, whole((4, width)),
            ],
            scratch_shapes=[
                pltpu.VMEM((ROWS, width), f32),
                pltpu.VMEM((ROWS, width), bf16),
                pltpu.VMEM((width, ROWS), bf16),
                pltpu.VMEM((ROWS, width), bf16),
                pltpu.VMEM((width, ROWS), bf16),
                pltpu.VMEM((ROWS, width), f32),
                pltpu.VMEM((ROWS, 1), f32),
                pltpu.VMEM((ROWS, width), f32),
                pltpu.VMEM((ROWS, width), f32),
                pltpu.VMEM((ROWS, width), bf16),
                pltpu.VMEM((width, width), bf16),
                pltpu.VMEM((width, hidden), bf16),
                pltpu.VMEM((width, hidden), bf16),
                pltpu.VMEM((1, hidden), f32),
                pltpu.VMEM((ROWS, 256), f32),
                pltpu.VMEM((ROWS, 256), f32),
                pltpu.VMEM((ROWS, hidden), bf16),
                pltpu.VMEM((ROWS, hidden), bf16),
                pltpu.VMEM((width, hidden), bf16),
                pltpu.VMEM((width, hidden), bf16),
            ],
        ),
        out_shape=[
            shaped(move.shape(width), bf16),
            shaped((ROWS, width)),
            shaped((ROWS, width), bf16),
            shaped((half, width, hidden), bf16),
            shaped((half, width, hidden), bf16),
            shaped((half, width, hidden), bf16),
            shaped((half, width, hidden), bf16),
            shaped((half, width, GROUP), bf16),
            shaped((half, width, GROUP), bf16),
            shaped((shares, 1, hidden)),
            shaped((4, width)),
        ],
        compiler_params=room(60),
        cost_estimate=cost(22),
        name="mlp",
    )(
        place, g_got, x_rows, o_a, o_b, ins, near_ins, far_ins, last_ins, outs, away_outs,
        proj_shift, gain_two, shift_two, split, other_split, out_shift,
    )
    out_rows, dh, dow, in_keep, in_send, out_keep, out_send, proj_keep, proj_send, *made = made
    grad_in_shift, vec_two = made

    mine = jnp.concatenate(
        [
            plus(in_keep, swap(in_send, "tp", 1)),
            plus(out_keep, swap(out_send, "tp", 1)),
            plus(proj_keep, swap(proj_send, "tp", 1)),
        ],
        axis=-1,
    )
    far = mine[1]
    out_cells = move.leave(out_rows)
    out_got = move.exchange(out_cells)
    far_got = swap(far, "tp", 2)

    def back(pair, weights, given, extra, last):
        specs = [
            whole((width, ROWS)), w_block, w_block, query_block, key_block, key_block,
            pl.BlockSpec((ROWS, GROUP), lambda i, *_: (0, 2 * pair + i)),
            lse_block, bias_block, *features,
        ]
        specs += [whole(v.shape) for v in extra]
        made = [shaped((ROWS, width))]
        if last:
            made = [shaped(move.shape(width), bf16), shaped((2, width))]
        made_specs = [whole(v.shape) for v in made]
        made += [
            shaped((width, 3 * GROUP), bf16),
            shaped((width, 3 * GROUP), bf16),
            shaped((2, 1, 3 * GROUP)),
            shaped((2 * heads, KEYS, DIAG_PAD)),
        ]
        made_specs += [
            whole((width, 3 * GROUP)), whole((width, 3 * GROUP)), chunk((1, 3 * GROUP)), bias_block,
        ]
        scratch = [
            pltpu.VMEM((ROWS, width), f32),
            pltpu.VMEM((ROWS, 3 * GROUP), f32),
            w_scratch,
            pltpu.VMEM((ROWS, GROUP), f32),
            pltpu.VMEM((heads * ALL_KEYS, 2 * GROUP), bf16),
            pltpu.VMEM((heads * ALL_KEYS, GROUP), bf16),
            pltpu.VMEM((heads * ALL_KEYS, ALL_QUERIES), f32),
            pltpu.VMEM((heads * ALL_KEYS, ALL_QUERIES), f32),
            pltpu.VMEM((heads * ALL_KEYS, ALL_QUERIES), bf16),
            pltpu.VMEM((heads * ALL_KEYS, ALL_QUERIES), bf16),
            bias_scratch,
            bias_scratch,
        ]
        return pl.pallas_call(
            functools.partial(attention_back_kernel, last, move.frames),
            grid_spec=pltpu.PrefetchScalarGridSpec(
                num_scalar_prefetch=1,
                grid=(2,),
                in_specs=specs,
                out_specs=made_specs,
                scratch_shapes=scratch,
            ),
            out_shape=made,
            compiler_params=room(60),
            cost_estimate=cost(19),
            name="attention_back",
        )(place, a1_t, *weights, *given, ours, theirs, *extra)

    dow_b = after(dow, far, out_cells)
    running, keep_b, send_b, shift_b, sums_b = back(1, w_b, (q_b, k_b, v_b, dow_b, lse_b, bias_b), (), False)

    mine = plus(mine[0], after(far_got, keep_b))
    mine = split_rows(mine, 0)
    steps = list(reversed(bits_of("grp")))
    near_b = swap(send_b, "tp", 1)
    keep, send = halves(mine, 0, steps[0])
    got_first = swap(send, "grp", steps[0])
    out_part = after(out_got, keep_b)
    out_far = swap(out_part, "tp", 2)
    out_near = swap(out_part, "tp", 1)
    far_b = plus(keep_b, near_b)
    far_got_b = swap(far_b, "tp", 2)
    running = after(running, far_b, out_part, send)
    made = back(0, w_a, (q_a, k_a, v_a, dow, lse_a, bias_a), (running, x_rows, gain_one, dh), True)
    gx, vec_one, keep_a, send_a, shift_a, sums_a = made

    gx_cells = move.leave(after(gx, got_first))
    gx_got = move.exchange(gx_cells)
    out_far = after(out_far, gx_cells)
    near_a = swap(after(send_a, gx_cells), "tp", 1)

    def table_of(pair_sums):
        return pl.pallas_call(
            table_kernel,
            grid=(2,),
            in_specs=[bias_block, whole((PICK_ROWS, 256))],
            out_specs=pl.BlockSpec((heads, 1, TABLE_PAD), lambda i: (i, 0, 0)),
            out_shape=shaped((2 * heads, 1, TABLE_PAD)),
            scratch_shapes=[pltpu.VMEM((heads, KEYS, TABLE_PAD), f32)],
            compiler_params=room(60),
            cost_estimate=cost(6),
            name="table",
        )(pair_sums, pick)

    def rows_of(*parts):
        return jnp.concatenate([part.reshape(-1) for part in parts]).reshape(-1, 3 * GROUP)

    def slot(tables, shifts, which, in_slot):
        return (tables[which * heads : (which + 1) * heads], shifts[which], grad_in_shift[in_slot])

    tables_b = table_of(after(sums_b, gx_cells))
    tables_a = table_of(after(sums_a, tables_b))
    gx_part = after(gx_got, tables_a)
    gx_far = swap(gx_part, "tp", 2)
    gx_near = swap(gx_part, "tp", 1)
    keep, send = halves(plus(after(keep, gx_part), got_first), 0, steps[1])
    got_second = swap(send, "grp", steps[1])
    got_a = plus(plus(keep_a, near_a), far_got_b)
    got_a = split_rows(got_a, 0)
    vec = rows_of(vec_one, vec_two)
    small = rows_of(vec, *slot(tables_a, shift_a, 0, 0), *slot(tables_b, shift_b, 0, 2))
    sent = rows_of(vec, *slot(tables_a, shift_a, 1, 1), *slot(tables_b, shift_b, 1, 3))
    small = small + swap(sent, "tp", 1)
    mine = plus(keep, got_second)
    for bit in steps[2:]:
        keep, send = halves(mine, 0, bit)
        mine = plus(keep, swap(send, "grp", bit))
    mine = mine.reshape(depth, 2 * hidden + GROUP).astype(f32)
    lead = vec.shape[0]
    cut = lead + (small.shape[0] - lead) // 2
    small = small[:cut] + swap(jnp.concatenate([small[:lead], small[cut:]]), "tp", 2)
    tail = small

    for i, bit in enumerate(steps):
        keep, send = halves(got_a, 0, bit)
        high = lax.reduce_precision(small, 8, 7)
        low = (small - high).astype(bf16)
        size = send.size // (3 * GROUP)
        sent = jnp.concatenate([send.reshape(size, 3 * GROUP), high.astype(bf16), low])
        if i == 0:
            sent = after(sent, gx_far)
        if i == 1:
            sent = after(sent, got_second)
        got = swap(sent, "grp", bit)
        got_a = plus(keep, got[:size].reshape(keep.shape))
        got = got[size:].astype(f32)
        small = small + got[:cut] + got[cut:]
    got_a = got_a.reshape(depth, 3, GROUP).astype(f32)
    vec = small[:lead].reshape(6, width)
    vec = lax.dynamic_slice_in_dim(vec, lax.axis_index("grp") * depth, depth, 1)
    small = small[lead:].reshape(-1)
    got_table = small[: heads * TABLE_PAD].reshape(heads, TABLE_PAD)[:, :TABLE].T
    got_shift = small[heads * TABLE_PAD :][: 3 * GROUP].reshape(3, GROUP)
    got_in_shift = small[heads * TABLE_PAD + 3 * GROUP :]

    output = (out_part, out_near, out_far, swap(after(out_far, tail), "tp", 1))
    output = move.home(output, 0, None, bf16)
    grad_tokens = move.home((gx_part, after(gx_near, tail)), 0, None, f32)
    gx_far = after(gx_far, grad_tokens)
    grad_tokens = move.home((gx_far, swap(gx_far, "tp", 1)), 2, grad_tokens, f32)
    return (
        output,
        grad_tokens,
        vec[0],
        vec[1],
        got_a,
        jnp.stack([got_shift[0], got_shift[2]]),
        got_table,
        mine[:, 2 * hidden :],
        vec[4],
        vec[2],
        vec[3],
        mine[:, :hidden],
        got_in_shift,
        mine[:, hidden : 2 * hidden],
        vec[5],
    )


def solution(mesh):
    shard = P("grp")
    tokens = P(None, "grp", None)
    placed = (
        tokens, tokens, shard, shard, P("grp", None, "tp"), P(None, "tp"), P(None, "tp"),
        P("grp", "tp"), shard, shard, shard, P("grp", "tp"), P("tp"), P("grp", "tp"), shard,
    )
    return jax.shard_map(
        per_device, mesh=mesh, in_specs=placed, out_specs=placed, check_vma=False
    )
```

```python
import functools

import jax
import jax.numpy as jnp
import numpy as np
from jax import lax
from jax.experimental import pallas as pl
from jax.experimental.pallas import tpu as pltpu
from jax.sharding import PartitionSpec as P

CT, CH, CW = 16, 14, 14
WT, WH, WW = 8, 7, 7
ST, SH, SW = 4, 3, 3
FRAME = CH * CW
SIDE = WH * WW
WIN = WT * SIDE
PAIR = 2
PADDED = -(-WIN // 16) * 16
ROWS = PAIR * PADDED
HEAD = 32
GROUP = 128
HEADS_IN = GROUP // HEAD
SPAN_T, SPAN_H, SPAN_W = 2 * WT - 1, 2 * WH - 1, 2 * WW - 1
PLANE = SPAN_H * SPAN_W
TABLE = SPAN_T * PLANE
TABLE_PAD = -(-TABLE // 128) * 128
LANES = 64
DIAG_PAD = (SPAN_T + 1) * LANES
KEYS = -(-SIDE // 8) * 8
ALL_KEYS, ALL_QUERIES = WT * KEYS, WT * LANES
CORNER = PLANE // 2
LOG2E = 1.4426950408889634
SCALE = HEAD ** (-0.5)
FAR = -(2.0**100)
f32 = jnp.float32
bf16 = jnp.bfloat16


def room(mib):
    return pltpu.CompilerParams(vmem_limit_bytes=mib * 1024 * 1024)


def cost(micros):
    return pl.CostEstimate(flops=int(micros * 1.1e9), bytes_accessed=1 << 20, transcendentals=0)


def dot(a, b):
    return lax.dot_general(a, b, (((1,), (0,)), ((), ())), preferred_element_type=f32)


def dot_t(a, b):
    return lax.dot_general(a, b, (((1,), (1,)), ((), ())), preferred_element_type=f32)


def moments(rows):
    centered = rows - jnp.mean(rows, axis=-1, keepdims=True)
    inverse = lax.rsqrt(jnp.mean(centered * centered, axis=-1, keepdims=True) + 1e-05)
    return centered * inverse, inverse


def norm_back(grad, unit, inverse, gain):
    scaled = grad * gain
    shared = jnp.mean(scaled, axis=-1, keepdims=True)
    along = jnp.mean(scaled * unit, axis=-1, keepdims=True)
    return inverse * (scaled - shared - unit * along)


def read_rows(target, ref, frames):
    if not frames:
        target[...] = ref[...].astype(f32)
        return
    count, _, size, _ = ref.shape
    for window in range(PAIR):
        for i in range(count):
            start = window * PADDED + i * frames * SIDE
            target[pl.ds(start, size), :] = ref[i, window].astype(f32)
        start = window * PADDED + WIN
        target[pl.ds(start, PADDED - WIN), :] = jnp.zeros((PADDED - WIN, target.shape[1]), f32)


def write_rows(ref, source, frames):
    if not frames:
        ref[...] = source[...].astype(bf16)
        return
    count, _, size, _ = ref.shape
    for window in range(PAIR):
        for i in range(count):
            start = window * PADDED + i * frames * SIDE
            ref[i, window] = source[pl.ds(start, size), :].astype(bf16)


def cells_kernel(facts_ref, tokens_ref, order_ref, out_ref):
    size, block = out_ref.shape[2], order_ref.shape[0] // 4
    rows = dot(order_ref[...], tokens_ref[0])
    for i in range(4):
        out_ref[i // 2, i % 2] = rows[i * block : i * block + size].astype(bf16)


def home_kernel(count, facts_ref, *refs):
    order_ref = refs[count]
    out_ref, rows = refs[-2:]
    step = pl.program_id(0)
    size, block = refs[0].shape[2], rows.shape[0] // 4

    @pl.when(step == 0)
    def _():
        rows[...] = jnp.zeros_like(rows)

    for clip in range(out_ref.shape[0]):
        for device in range(count):

            @pl.when(step == device)
            def _():
                for i in range(4):
                    piece = refs[device][2 * clip + i // 2, i % 2]
                    rows[i * block : i * block + size, :] = piece.astype(f32)

        out_ref[clip] = dot(order_ref[...], rows[...].astype(bf16)).astype(out_ref.dtype)


SPANS = []
for _lane in range(0, DIAG_PAD, 256):
    _low = _lane // LANES * PLANE // 128 * 128
    _high = min((_lane + 255) // LANES + 1, SPAN_T) * PLANE
    SPANS.append((_lane, _low, -(-_high // 128) * 128))
PICK_ROWS = sum(high - low for _, low, high in SPANS)


def bias_kernel(table_ref, pick_ref, bias_ref, sheared):
    heads = bias_ref.shape[0]
    tables = table_ref[0].astype(f32)
    for head in range(heads):
        flat = jnp.broadcast_to(tables[head : head + 1], (8, TABLE_PAD))
        stairs = pltpu.roll(flat, 0, 1, stride=1, stride_axis=0)
        for row in range(WH):
            shift = (row * SPAN_W - CORNER) % TABLE_PAD
            sheared[head, pl.ds(row * WW, 8), :] = pltpu.roll(stairs, shift, 1)
        sheared[head, SIDE:KEYS, :] = jnp.zeros((KEYS - SIDE, TABLE_PAD), f32)
    everything = sheared[...].reshape(heads * KEYS, TABLE_PAD).astype(bf16)
    start = 0
    for lane, low, high in SPANS:
        part = dot(everything[:, low:high], pick_ref[start : start + high - low]) * LOG2E
        bias_ref[:, :, lane : lane + 256] = part.reshape(heads, KEYS, 256)
        start += high - low


def table_kernel(sums_ref, pick_ref, grad_ref, sheared):
    heads = sums_ref.shape[0]
    everything = sums_ref[...].reshape(heads * KEYS, DIAG_PAD).astype(bf16)
    done = 0
    start = 0
    for lane, low, high in SPANS:
        part = dot_t(everything[:, lane : lane + 256], pick_ref[start : start + high - low])
        part = part.reshape(heads, KEYS, high - low)
        if done > low:
            sheared[:, :, low:done] += part[:, :, : done - low]
            sheared[:, :, done:high] = part[:, :, done - low :]
        else:
            sheared[:, :, low:high] = part
        done = high
        start += high - low
    row_in = lax.broadcasted_iota(jnp.int32, (8, TABLE_PAD), 0)
    for head in range(heads):
        stairs = jnp.zeros((8, TABLE_PAD), f32)
        for row in range(WH):
            shift = (CORNER - row * SPAN_W) % TABLE_PAD
            stairs = stairs + pltpu.roll(sheared[head, pl.ds(row * WW, 8), :], shift, 1)
        flat = jnp.where(row_in == 0, stairs, 0.0)
        for step in range(1, WW):
            moved = pltpu.roll(stairs, TABLE_PAD - step, 1)
            flat = flat + jnp.where(row_in == step, moved, 0.0)
        grad_ref[head] = jnp.sum(flat, axis=0, keepdims=True)


def spread_frames(source, window, columns, stride):
    place = lax.broadcasted_iota(jnp.int32, (KEYS, GROUP), 0)
    parts = []
    for frame in range(WT):
        rows = source[pl.ds(window * PADDED + frame * SIDE, KEYS), columns]
        parts.append(jnp.where(place < SIDE, rows, 0.0))
        if stride > KEYS:
            parts.append(jnp.zeros((stride - KEYS, GROUP), f32))
    return jnp.concatenate(parts, axis=0)


def close_frames(target, window, columns, rows, stride):
    for frame in range(WT):
        place = pl.ds(window * PADDED + frame * SIDE, KEYS)
        target[place, columns] = rows[frame * stride : frame * stride + KEYS]
    place = slice(window * PADDED + WIN, (window + 1) * PADDED)
    target[place, columns] = jnp.zeros((PADDED - WIN, GROUP), f32)


def turn_bias(target, bias_ref):
    for head in range(bias_ref.shape[0]):
        target[head, 0] = bias_ref[head]
        target[head, 1] = pltpu.roll(bias_ref[head], DIAG_PAD - LANES, 1)


def frame_bias(head, frame, lanes):
    start = (WT - 1 - frame) * LANES
    copy = start // LANES % 2
    start = start - copy * LANES + lanes
    return (head, copy, slice(None), slice(start, start + 256))


def by_tile(rows, how):
    return how(rows.reshape(rows.shape[0] // 8, 8, rows.shape[1]), axis=0)


def mask_heads(target, rows, lane):
    for head in range(HEADS_IN):
        masked = jnp.where(lane == head, rows, jnp.zeros_like(rows))
        target[head * ALL_KEYS : (head + 1) * ALL_KEYS, 0:GROUP] = masked


def attention_kernel(first, frames, *refs):
    step = pl.program_id(0)
    refs = refs[1:]
    if first:
        got_ref, gain_ref, shift_ref, w0_ref, w1_ref, wb_ref, bias_ref, qf_ref, kf_ref = refs[:9]
        x_ref, a1_ref, a1_t_ref, q_ref, k_ref, v_ref, o_ref, lse_ref = refs[9:17]
        w_ref, wide, keys, logits, probs, rows_o, bias, rows_in = refs[17:]

        @pl.when(step == 0)
        def _():
            read_rows(rows_in, got_ref, frames)
            x_ref[...] = rows_in[...].astype(bf16)
            unit, _ = moments(rows_in[...])
            low = unit * gain_ref[...] + shift_ref[...]
            a1_ref[...] = low.astype(bf16)
            a1_t_ref[...] = low.T.astype(bf16)
    else:
        a1_ref, w0_ref, w1_ref, wb_ref, bias_ref, qf_ref, kf_ref = refs[:7]
        q_ref, k_ref, v_ref, o_ref, lse_ref = refs[7:12]
        w_ref, wide, keys, logits, probs, rows_o, bias = refs[12:]

    @pl.when(step == 0)
    def _():
        w_ref[...] = w0_ref[...]

    @pl.when(step == 1)
    def _():
        w_ref[...] = w1_ref[...]

    turn_bias(bias, bias_ref)
    shift = wb_ref[0].astype(f32)[HEADS_IN : HEADS_IN + 1]
    nothing = jnp.zeros((1, GROUP), f32)
    shift = jnp.concatenate([shift[:, :GROUP], nothing, shift[:, GROUP : 2 * GROUP]], axis=1)
    wide[...] = dot(a1_ref[...], w_ref[...]) + shift
    lane = lax.broadcasted_iota(jnp.int32, (ALL_KEYS, GROUP), 1) // HEAD
    for window in range(PAIR):
        query = spread_frames(wide, window, slice(0, GROUP), LANES).astype(bf16)
        key = spread_frames(wide, window, slice(GROUP, 2 * GROUP), KEYS).astype(bf16)
        value = spread_frames(wide, window, slice(2 * GROUP, 3 * GROUP), KEYS)
        q_ref[0, window] = query
        k_ref[0, window] = key
        v_ref[0, window] = value.astype(bf16)
        value_t = value.T.astype(bf16)
        mask_heads(keys, key, lane)
        for head in range(HEADS_IN):
            keys[head * ALL_KEYS : (head + 1) * ALL_KEYS, GROUP : 2 * GROUP] = kf_ref[0, window]
        logits[...] = dot_t(keys[...], jnp.concatenate([query, qf_ref[0, window]], axis=1))
        parts = []
        for head in range(HEADS_IN):
            tops, totals = [], []
            for lanes in range(0, ALL_QUERIES, 256):
                across = slice(lanes, lanes + 256)
                top = jnp.full((8, 256), -jnp.inf, f32)
                for frame in range(WT):
                    at = head * ALL_KEYS + frame * KEYS
                    block = logits[at : at + KEYS, across] * (SCALE * LOG2E)
                    block = block + bias[frame_bias(head, frame, lanes)]
                    logits[at : at + KEYS, across] = block
                    top = jnp.maximum(top, by_tile(block, jnp.max))
                top = jnp.max(top, axis=0, keepdims=True)
                total = jnp.zeros((8, 256), f32)
                for pair in range(0, ALL_KEYS, 2 * KEYS):
                    at = head * ALL_KEYS + pair
                    block = jnp.exp2(logits[at : at + 2 * KEYS, across] - top)
                    total = total + by_tile(block, jnp.sum)
                    probs[pair : pair + 2 * KEYS, across] = block.astype(bf16)
                tops.append(top)
                totals.append(jnp.sum(total, axis=0, keepdims=True))
            total = jnp.concatenate(totals, axis=1)
            lse = jnp.concatenate(tops, axis=1) + jnp.log2(total)
            lse_ref[0, pl.ds(window * HEADS_IN + head, 1), :] = lse
            mixed = dot(value_t[head * HEAD : (head + 1) * HEAD], probs[...])
            parts.append(mixed / total)
        mixed = jnp.concatenate(parts, axis=0).T
        close_frames(rows_o, window, slice(None), mixed, LANES)
    o_ref[...] = rows_o[...].astype(bf16)


def mlp_kernel(frames, facts_ref, *refs):
    got_ref, x_ref, oa_ref, ob_ref = refs[:4]
    weights, home_ref, away_ref = refs[4:8], refs[8], refs[9]
    pb_ref, gain_ref, shift_ref, near_ref, far_ref, out_shift_ref = refs[10:16]
    out_ref, refs = refs[16], refs[17:]
    dh_ref, dow_ref, gwi_keep, gwi_send, gwo_keep, gwo_send, gwp_keep, gwp_send = refs[:8]
    gib_ref, vec_ref = refs[8:10]
    hidden, a2, a2_t, g_ref, g_t, unit_s, inv_s, acc_out, acc_in, o_all, wp = refs[10:21]
    wi, wo, ib_ref, u_s, back_s, act, du, grad_out_w, grad_in_w = refs[21:]
    step = pl.program_id(0)
    width = x_ref.shape[1]
    units = gib_ref.shape[2]

    @pl.when(step == 0)
    def _():
        o_all[:, 0 : 2 * GROUP] = oa_ref[...]
        o_all[:, 2 * GROUP : 4 * GROUP] = ob_ref[...]
        for i, ref in enumerate(weights):
            wp[:, i * GROUP : (i + 1) * GROUP] = ref[:, units : units + GROUP]
        branch = dot_t(o_all[...], wp[...])
        hidden[...] = x_ref[...].astype(f32) + branch + pb_ref[...]
        unit, inverse = moments(hidden[...])
        unit_s[...] = unit
        inv_s[...] = inverse
        low = unit * gain_ref[...] + shift_ref[...]
        a2[...] = low.astype(bf16)
        a2_t[...] = low.T.astype(bf16)
        read_rows(acc_out, got_ref, frames)
        g_ref[...] = acc_out[...].astype(bf16)
        g_t[...] = acc_out[...].T.astype(bf16)
        acc_out[...] = jnp.zeros_like(acc_out)
        acc_in[...] = jnp.zeros_like(acc_in)

    for i, slot in enumerate((1, 3, 0, 2)):

        @pl.when(step == i)
        def _():
            wi[...] = weights[slot][:, 0:units]
            wo[...] = (away_ref if slot % 2 else home_ref)[0]
            shifts = (near_ref if slot < 2 else far_ref)[slot % 2].astype(f32)
            ib_ref[...] = shifts[HEADS_IN + 1 : HEADS_IN + 2, 0:units]

    for first in range(0, units, 256):
        some = slice(first, first + 256)
        u_s[...] = dot(a2[...], wi[:, some])
        back_s[...] = dot(g_ref[...], wo[:, some])
        sums = jnp.zeros((8, 256), f32)
        for row in range(0, ROWS, 80):
            rows = slice(row, row + 80)
            u = u_s[rows] + ib_ref[:, some]
            half = 0.5 * (1.0 + lax.erf(u * (0.5**0.5)))
            act[rows, some] = (u * half).astype(bf16)
            slope = half + u * jnp.exp(-0.5 * u * u) * 0.3989422804014327
            low = (back_s[rows] * slope).astype(bf16)
            du[rows, some] = low
            sums = sums + by_tile(low.astype(f32), jnp.sum)
        gib_ref[0, :, some] = jnp.sum(sums, axis=0, keepdims=True)
        grad_out_w[:, some] = dot(g_t[...], act[:, some]).astype(bf16)
        grad_in_w[:, some] = dot(a2_t[...], du[:, some]).astype(bf16)
    acc_out[...] += dot_t(act[...], wo[...])
    acc_in[...] += dot_t(du[...], wi[...])

    @pl.when(step < 2)
    def _():
        gwo_send[0] = grad_out_w[...]
        gwi_send[0] = grad_in_w[...]

    @pl.when(step >= 2)
    def _():
        gwo_keep[0] = grad_out_w[...]
        gwi_keep[0] = grad_in_w[...]

    @pl.when(step == pl.num_programs(0) - 1)
    def _():
        acc_out[...] += hidden[...] + out_shift_ref[...]
        write_rows(out_ref, acc_out, frames)
        upstream = g_ref[...].astype(f32)
        grad = acc_in[...]
        unit = unit_s[...]
        dh = upstream + norm_back(grad, unit, inv_s[...], gain_ref[...])
        dh_ref[...] = dh
        dz = dh.astype(bf16)
        dow_ref[...] = dot(dz, wp[...]).astype(bf16)
        grad_wp = dot(dz.astype(f32).T.astype(bf16), o_all[...])
        for i in range(2):
            gwp_keep[i] = grad_wp[:, 2 * i * GROUP : (2 * i + 1) * GROUP].astype(bf16)
            gwp_send[i] = grad_wp[:, (2 * i + 1) * GROUP : (2 * i + 2) * GROUP].astype(bf16)
        vec_ref[...] = jnp.concatenate(
            [
                jnp.sum(grad * unit, axis=0, keepdims=True),
                jnp.sum(grad, axis=0, keepdims=True),
                jnp.sum(dz.astype(f32), axis=0, keepdims=True),
                jnp.sum(upstream, axis=0, keepdims=True),
            ],
            axis=0,
        )


def attention_back_kernel(last, frames, facts_ref, *refs):
    a1_t_ref, w0_ref, w1_ref, q_ref, k_ref, v_ref, dow_ref, lse_ref, bias_ref, qf_ref, kf_ref = refs[:11]
    refs = refs[11:]
    if last:
        sum_ref, x_ref, gain_ref, dh_ref, gx_ref, vec_ref = refs[:6]
        refs = refs[6:]
    else:
        sum_ref, refs = refs[0], refs[1:]
    keep_ref, send_ref, gb_ref, sums_ref, acc, dqkv, w_ref = refs[:7]
    rows_in, keys, values, probs_f, dp, probs, ds, shifted, bias = refs[7:]
    step = pl.program_id(0)

    @pl.when(step == 0)
    def _():
        w_ref[...] = w0_ref[...]

    @pl.when(step == 1)
    def _():
        w_ref[...] = w1_ref[...]

    shifted[...] = jnp.zeros_like(shifted)
    turn_bias(bias, bias_ref)
    rows_in[...] = dow_ref[...].astype(f32)
    lane = lax.broadcasted_iota(jnp.int32, (ALL_KEYS, GROUP), 1) // HEAD
    for window in range(PAIR):
        query, key, value = q_ref[0, window], k_ref[0, window], v_ref[0, window]
        dow = spread_frames(rows_in, window, slice(None), LANES).astype(bf16)
        key_t = key.astype(f32).T.astype(bf16)
        mask_heads(keys, key, lane)
        mask_heads(values, value, lane)
        for head in range(HEADS_IN):
            keys[head * ALL_KEYS : (head + 1) * ALL_KEYS, GROUP : 2 * GROUP] = kf_ref[0, window]
        probs_f[...] = dot_t(keys[...], jnp.concatenate([query, qf_ref[0, window]], axis=1))
        dp[...] = dot_t(values[...], dow)
        for head in range(HEADS_IN):
            lse = lse_ref[0, pl.ds(window * HEADS_IN + head, 1), :]
            for lanes in range(0, ALL_QUERIES, 256):
                across = slice(lanes, lanes + 256)
                dots = jnp.zeros((8, 256), f32)
                for pair in range(0, WT, 2):
                    blocks = []
                    for frame in (pair, pair + 1):
                        at = head * ALL_KEYS + frame * KEYS
                        block = probs_f[at : at + KEYS, across] * (SCALE * LOG2E)
                        block = block + bias[frame_bias(head, frame, lanes)]
                        blocks.append(block)
                    at = head * ALL_KEYS + pair * KEYS
                    block = jnp.exp2(jnp.concatenate(blocks, axis=0) - lse[:, across])
                    probs_f[at : at + 2 * KEYS, across] = block
                    probs[at : at + 2 * KEYS, across] = block.astype(bf16)
                    dots = dots + by_tile(block * dp[at : at + 2 * KEYS, across], jnp.sum)
                dots = jnp.sum(dots, axis=0, keepdims=True)
                for pair in range(0, WT, 2):
                    at = head * ALL_KEYS + pair * KEYS
                    block = probs_f[at : at + 2 * KEYS, across]
                    block = block * (dp[at : at + 2 * KEYS, across] - dots)
                    ds[at : at + 2 * KEYS, across] = block.astype(bf16)
                    for i in range(2):
                        place = frame_bias(head, pair + i, lanes)
                        shifted[place] += block[i * KEYS : (i + 1) * KEYS]
        dv_all = dot(probs[...], dow)
        dk_all = dot(ds[...], query)
        none = jnp.zeros((ALL_KEYS, GROUP), f32)
        dk, dv, dq_t = none, none, []
        for head in range(HEADS_IN):
            part = slice(head * ALL_KEYS, (head + 1) * ALL_KEYS)
            dv = jnp.where(lane == head, dv_all[part], dv)
            dk = jnp.where(lane == head, dk_all[part], dk)
            dq_t.append(dot(key_t[head * HEAD : (head + 1) * HEAD], ds[part]))
        dq = jnp.concatenate(dq_t, axis=0).T
        close_frames(dqkv, window, slice(0, GROUP), dq * SCALE, LANES)
        close_frames(dqkv, window, slice(GROUP, 2 * GROUP), dk * SCALE, KEYS)
        close_frames(dqkv, window, slice(2 * GROUP, 3 * GROUP), dv, KEYS)
    for head in range(HEADS_IN):
        sums_ref[head] = shifted[head, 0] + pltpu.roll(shifted[head, 1], LANES, 1)
    low = dqkv[...].astype(bf16)
    grad = dot_t(low, w_ref[...])
    grad_w = dot(a1_t_ref[...], low)
    gb_ref[0] = jnp.sum(low.astype(f32), axis=0, keepdims=True)

    @pl.when(step == 0)
    def _():
        acc[...] = grad + sum_ref[...] if last else grad
        keep_ref[...] = grad_w.astype(bf16)

    @pl.when(step == 1)
    def _():
        send_ref[...] = grad_w.astype(bf16)
        total = acc[...] + grad
        if last:
            unit, inverse = moments(x_ref[...].astype(f32))
            acc[...] = dh_ref[...] + norm_back(total, unit, inverse, gain_ref[...])
            write_rows(gx_ref, acc, frames)
            vec_ref[...] = jnp.concatenate(
                [jnp.sum(total * unit, axis=0, keepdims=True), jnp.sum(total, axis=0, keepdims=True)],
                axis=0,
            )
        else:
            sum_ref[...] = total


def whole(shape):
    return pl.BlockSpec(shape, lambda *i: (0,) * len(shape))


def shaped(shape, kind=f32):
    return jax.ShapeDtypeStruct(shape, kind)


def chunk(shape):
    return pl.BlockSpec((1,) + shape, lambda i, *_: (i,) + (0,) * len(shape))


def pick_matrix():
    place = np.arange(TABLE_PAD)
    row, column = place % PLANE // SPAN_W, place % PLANE % SPAN_W
    target = place // PLANE * LANES + row * WW + column
    good = (place < TABLE) & (row < WH) & (column < WW)
    target = np.where(good, target, -1)
    target = np.concatenate([target[low:high] - lane for lane, low, high in SPANS])
    return jnp.asarray(np.arange(256) == target[:, None], bf16)


def region_features():
    lane = np.arange(GROUP)

    def codes(stride, is_late, is_low, is_right):
        frame, cell = np.divmod(np.arange(WT * stride), stride)
        code = (
            (is_late * (frame >= WT - ST)) * 4
            + (is_low * (cell // WW >= WH - SH)) * 2
            + is_right * (cell % WW >= WW - SW)
        )
        return (cell < SIDE)[:, None], code[:, None]

    ours, theirs = [], []
    for is_late in range(2):
        for is_low in range(2):
            for is_right in range(PAIR):
                real, code = codes(LANES, is_late, is_low, is_right)
                ours.append((real & (lane == code)) | (lane == 8))
                real, code = codes(KEYS, is_late, is_low, is_right)
                other = np.where(real, (lane < 8) & (lane != code), lane == 8)
                theirs.append(np.where(other, FAR, 0.0))
    ours = jnp.asarray(np.reshape(ours, (4, PAIR, ALL_QUERIES, GROUP)), bf16)
    return ours, jnp.asarray(np.reshape(theirs, (4, PAIR, ALL_KEYS, GROUP)), bf16)


def cell_order(frames):
    size = frames * SIDE
    step = -(-size // 16) * 16
    matrix = np.zeros((4 * step, frames * FRAME), bool)
    for low in range(2):
        for right in range(2):
            for cell in range(size):
                frame, row, column = cell // SIDE, cell // WW % WH, cell % WW
                row = (low * WH + row + SH) % CH
                column = (right * WW + column + SW) % CW
                place = frame * FRAME + row * CW + column
                matrix[(low * 2 + right) * step + cell, place] = True
    return matrix


class Windows:
    def __init__(self, clips, local, groups, shares):
        self.share = clips // shares
        self.local = local
        self.half = groups // 2
        first = ST * FRAME // local
        order = [(first + i) % groups for i in range(groups)]
        self.groups = [order[: self.half], order[self.half :]]
        self.frames = local // FRAME if local % FRAME == 0 else 0
        slot = (lax.axis_index("grp") - first) % groups
        self.low = slot % 2
        me = lax.axis_index("tp")
        order = [me * self.share, slot // self.half * 2 + self.low]
        order += [me ^ i for i in range(shares)]
        self.facts = lax.optimization_barrier(jnp.stack(order).astype(jnp.int32))

    def exchange(self, rows):
        return lax.all_to_all(
            rows, "grp", split_axis=0, concat_axis=0, tiled=True, axis_index_groups=self.groups
        )

    def shape(self, width):
        if not self.frames:
            return (ROWS, width)
        return (self.half, 2, -(-self.frames * SIDE // 8) * 8, width)

    def before(self, field):
        width = field.shape[-1]
        place = lax.axis_index("tp") * self.share
        if not self.frames:
            own = lax.dynamic_slice_in_dim(field, place, self.share, 0)
            return jnp.repeat(own, 2, axis=0)
        order = jnp.asarray(cell_order(self.frames), bf16)
        shape = self.shape(width)
        return pl.pallas_call(
            cells_kernel,
            grid_spec=pltpu.PrefetchScalarGridSpec(
                num_scalar_prefetch=1,
                grid=(self.share,),
                in_specs=[
                    pl.BlockSpec((1, self.local, width), lambda i, facts: (facts[0] + i, 0, 0)),
                    whole(order.shape),
                ],
                out_specs=pl.BlockSpec((2,) + shape[1:], lambda i, facts: (i, 0, 0, 0)),
            ),
            out_shape=shaped(shape, bf16),
            compiler_params=room(60),
            cost_estimate=cost(3),
            name="cells",
        )(self.facts, field, order)

    def home(self, parts, first, into, kind, micros):
        width = parts[0].shape[-1]
        size = lax.axis_size("tp")
        clips = size * self.share
        if not self.frames:
            if into is None:
                into = jnp.zeros((clips, self.local, width), kind)
            for i, part in enumerate(parts):
                part = part.reshape(self.share, 2, self.local, width)
                part = (part[:, 0] + part[:, 1]).astype(kind)
                start = (lax.axis_index("tp") ^ (first + i)) * self.share
                into = lax.dynamic_update_slice_in_dim(into, part, start, 0)
            return into
        order = jnp.asarray(cell_order(self.frames).T, bf16)
        extra = [] if into is None else [into]

        def place(step, facts):
            return (facts[2 + first + step], 0, 0)

        return pl.pallas_call(
            functools.partial(home_kernel, len(parts)),
            grid_spec=pltpu.PrefetchScalarGridSpec(
                num_scalar_prefetch=1,
                grid=(len(parts),),
                in_specs=[whole(parts[0].shape)] * len(parts)
                + [whole(order.shape)]
                + [pl.BlockSpec(memory_space=pl.ANY)] * len(extra),
                out_specs=pl.BlockSpec((self.share, self.local, width), place),
                scratch_shapes=[pltpu.VMEM((order.shape[1], width), f32)],
            ),
            out_shape=shaped((clips, self.local, width), kind),
            input_output_aliases={len(parts) + 2: 0} if extra else {},
            compiler_params=room(60),
            cost_estimate=cost(micros),
            name="home",
        )(self.facts, *parts, order, *extra)

    def arrange(self, cells):
        if self.frames:
            return cells
        width = cells.shape[-1]
        cells = cells.reshape(WT, CH, CW, width)
        cells = jnp.roll(cells, (-SH, -SW), axis=(1, 2))
        cells = lax.dynamic_slice_in_dim(cells, self.low * WH, WH, 1)
        cells = cells.reshape(WT, WH, 2, WW, width).transpose(2, 0, 1, 3, 4)
        cells = cells.reshape(PAIR, WIN, width)
        cells = jnp.pad(cells, ((0, 0), (0, PADDED - WIN), (0, 0)))
        return cells.reshape(ROWS, width)

    def leave(self, rows):
        if self.frames:
            return rows
        width = rows.shape[-1]
        cells = rows.reshape(PAIR, PADDED, width)[:, :WIN]
        cells = cells.reshape(2, WT, WH, WW, width).transpose(1, 2, 0, 3, 4)
        cells = cells.reshape(WT, WH, CW, width)
        blank = jnp.zeros((WT, CH, CW, width), cells.dtype)
        cells = lax.dynamic_update_slice_in_dim(blank, cells, self.low * WH, 1)
        cells = jnp.roll(cells, (SH, SW), axis=(1, 2))
        return cells.reshape(self.half, self.local, width)


def swap(field, axis, bit):
    size = lax.axis_size(axis)
    return lax.ppermute(field, axis, [(i, i ^ bit) for i in range(size)])


def bits_of(axis):
    size = lax.axis_size(axis)
    return [1 << i for i in reversed(range(size.bit_length() - 1))]


def flag_of(axis, bit):
    return lax.axis_index(axis) // bit % 2


def after(value, *others):
    return lax.optimization_barrier((value, others))[0]


def join(mine, other, bit, axis, place):
    second = flag_of(axis, bit) == 1
    return jnp.concatenate(
        [jnp.where(second, other, mine), jnp.where(second, mine, other)], axis=place
    )


class Gather:
    def __init__(self, part):
        self.bits = bits_of("grp")
        self.shape = part.shape
        self.field = part.reshape((1,) * len(self.bits) + part.shape)
        self.coming = ()
        self.done = 0

    def send(self, *others, double=False):
        self.field = after(self.field, *others)
        bit = self.bits[self.done]
        which = [bit, bit // 2, bit + bit // 2] if double else [bit]
        self.coming = [swap(self.field, "grp", i) for i in which]
        return self.field

    def take(self):
        bit, place = self.bits[self.done], self.done
        if len(self.coming) == 1:
            self.field = join(self.field, self.coming[0], bit, "grp", place)
            self.done += 1
            return
        one, two, both = self.coming
        near = join(self.field, two, bit // 2, "grp", place + 1)
        far = join(one, both, bit // 2, "grp", place + 1)
        self.field = join(near, far, bit, "grp", place)
        self.done += 2

    def result(self):
        return self.field.reshape((self.shape[0] << len(self.bits),) + self.shape[1:])


def plus(one, other):
    return (one.astype(f32) + other.astype(f32)).astype(bf16)


def split_rows(field, lead):
    bits = bits_of("grp")
    shape = field.shape
    rows = shape[lead] >> len(bits)
    return field.reshape(shape[:lead] + (2,) * len(bits) + (rows,) + shape[lead + 1 :])


def halves(field, lead, bit):
    place = lead + bits_of("grp").index(bit)
    mine = flag_of("grp", bit)
    keep = lax.dynamic_index_in_dim(field, mine, place, keepdims=True)
    send = lax.dynamic_index_in_dim(field, 1 - mine, place, keepdims=True)
    return keep, send


def per_device(
    tokens, grad_out, ln1_gain, ln1_shift, w_qkv, qkv_bias, rel_table, w_proj, proj_bias,
    ln2_gain, ln2_shift, w_in, in_bias, w_out, out_bias,
):
    groups, shares = lax.axis_size("grp"), lax.axis_size("tp")
    clips, local, width = tokens.shape
    move = Windows(clips, local, groups, shares)
    depth = w_qkv.shape[0]
    hidden = w_in.shape[1]
    heads = rel_table.shape[1]
    half = shares // 2

    later = Gather(jnp.concatenate([w_in, w_out, w_proj], axis=1))
    later_bits = later.bits
    vectors = jnp.stack([ln1_gain, ln1_shift, proj_bias, ln2_gain, ln2_shift, out_bias])
    first = jnp.concatenate(
        [w_qkv.reshape(depth, 3 * GROUP), jnp.pad(vectors.T, ((0, 0), (0, GROUP - 6)))], axis=1
    )
    first = Gather(first)
    for _ in range(len(first.bits) - 3):
        for chain in (first, later):
            chain.send()
            chain.take()
    split = jnp.concatenate(
        [
            jnp.pad(rel_table.T, ((0, 0), (0, TABLE_PAD - TABLE))),
            jnp.pad(qkv_bias.reshape(1, -1), ((0, 0), (0, TABLE_PAD - qkv_bias.size))),
            jnp.pad(in_bias[None], ((0, 3 - heads % 2), (0, TABLE_PAD - hidden))),
        ]
    )
    split = jnp.stack([split, swap(split, "tp", 1)])
    other_split = swap(split, "tp", 2)

    pick = pick_matrix()
    ours, theirs = region_features()

    def bias_of(half_split):
        return pl.pallas_call(
            bias_kernel,
            grid=(2,),
            in_specs=[chunk(half_split.shape[1:]), whole((PICK_ROWS, 256))],
            out_specs=pl.BlockSpec((heads, KEYS, DIAG_PAD), lambda i: (i, 0, 0)),
            out_shape=shaped((2 * heads, KEYS, DIAG_PAD)),
            scratch_shapes=[pltpu.VMEM((heads, KEYS, TABLE_PAD), f32)],
            compiler_params=room(60),
            cost_estimate=cost(6),
            name="bias",
        )(half_split, pick)

    sent = first.send(double=True)
    sent = sent, later.send(sent)
    x_send = move.before(after(tokens, sent))
    first.take()
    later.take()
    sent = first.send(x_send), later.send(x_send)
    x_got = move.exchange(after(x_send, sent))
    bias_a = bias_of(after(split, sent))
    first.take()
    later.take()
    first, later = after((first.result(), later.field), bias_a)
    bit, at = later_bits[-1], len(later_bits) - 1
    ins = jnp.concatenate([later[..., :hidden], later[..., 2 * hidden :]], axis=-1)
    outs = later[..., hidden : 2 * hidden]
    ins_got = swap(ins, "grp", bit)
    outs_got = swap(outs, "tp", 2)
    vectors = first[:, 3 * GROUP : 3 * GROUP + 6].T.astype(f32)
    gain_one, shift_one, proj_shift, gain_two, shift_two, out_shift = (
        vectors[i : i + 1] for i in range(6)
    )
    own = first[:, : 3 * GROUP]
    place = move.facts
    across = swap(own, "tp", 2)
    w_a = (own, swap(own, "tp", 1))
    x_got = move.arrange(x_got)


    rows, row = whole((ROWS, width)), whole((1, width))
    features = [
        pl.BlockSpec((1, PAIR, size, GROUP), lambda i, facts: (facts[1], 0, 0, 0))
        for size in (ALL_QUERIES, ALL_KEYS)
    ]
    bias_block = pl.BlockSpec((heads, KEYS, DIAG_PAD), lambda i, *_: (i, 0, 0))
    bias_scratch = pltpu.VMEM((heads, 2, KEYS, DIAG_PAD), f32)
    pair_columns = pl.BlockSpec((ROWS, GROUP), lambda i, *_: (0, i))
    query_block, key_block = chunk((PAIR, ALL_QUERIES, GROUP)), chunk((PAIR, ALL_KEYS, GROUP))
    lse_block = chunk((PAIR * heads, ALL_QUERIES))
    pair_specs = [query_block, key_block, key_block, pair_columns, lse_block]
    pair_shapes = [
        shaped((2, PAIR, ALL_QUERIES, GROUP), bf16),
        shaped((2, PAIR, ALL_KEYS, GROUP), bf16),
        shaped((2, PAIR, ALL_KEYS, GROUP), bf16),
        shaped((ROWS, 2 * GROUP), bf16),
        shaped((2, PAIR * heads, ALL_QUERIES)),
    ]
    w_block = whole((width, 3 * GROUP))
    w_specs = [w_block, w_block, chunk(split.shape[1:]), bias_block, *features]
    w_scratch = pltpu.VMEM((width, 3 * GROUP), bf16)
    attention_scratch = [
        w_scratch,
        pltpu.VMEM((ROWS, 3 * GROUP), f32),
        pltpu.VMEM((heads * ALL_KEYS, 2 * GROUP), bf16),
        pltpu.VMEM((heads * ALL_KEYS, ALL_QUERIES), f32),
        pltpu.VMEM((ALL_KEYS, ALL_QUERIES), bf16),
        pltpu.VMEM((ROWS, GROUP), f32),
        bias_scratch,
    ]
    x_rows, a1, a1_t, q_a, k_a, v_a, o_a, lse_a = pl.pallas_call(
        functools.partial(attention_kernel, True, move.frames),
        grid_spec=pltpu.PrefetchScalarGridSpec(
            num_scalar_prefetch=1,
            grid=(2,),
            in_specs=[whole(x_got.shape), row, row, *w_specs],
            out_specs=[rows, rows, whole((width, ROWS)), *pair_specs],
            scratch_shapes=[
                *attention_scratch, pltpu.VMEM((ROWS, width), f32),
            ],
        ),
        out_shape=[
            shaped((ROWS, width), bf16),
            shaped((ROWS, width), bf16),
            shaped((width, ROWS), bf16),
            *pair_shapes,
        ],
        compiler_params=room(60),
        cost_estimate=cost(12),
        name="attention",
    )(place, x_got, gain_one, shift_one, *after(w_a, ins, outs), split, bias_a, ours, theirs)
    ins_got, outs_got, across = after((ins_got, outs_got, across), a1)
    ins = join(ins, ins_got, bit, "grp", at).reshape(width, hidden + GROUP)
    outs = jnp.stack([outs, outs_got])
    far_ins = swap(ins, "tp", 2)
    outs_got = swap(outs, "grp", bit)
    g_send = move.before(after(grad_out, ins, outs, across))
    g_got = move.exchange(g_send)
    bias_b = bias_of(after(other_split, g_send))
    far_ins, outs_got = after((far_ins, outs_got), bias_b)
    outs = join(outs, outs_got, bit, "grp", at + 1).reshape(half, width, hidden)
    near_ins, last_ins = swap(ins, "tp", 1), swap(far_ins, "tp", 1)
    away_outs = swap(outs, "tp", 1)
    w_b = (across, swap(across, "tp", 1))
    q_b, k_b, v_b, o_b, lse_b = pl.pallas_call(
        functools.partial(attention_kernel, False, 0),
        grid_spec=pltpu.PrefetchScalarGridSpec(
            num_scalar_prefetch=1,
            grid=(2,),
            in_specs=[rows, *w_specs],
            out_specs=pair_specs,
            scratch_shapes=attention_scratch,
        ),
        out_shape=pair_shapes,
        compiler_params=room(60),
        cost_estimate=cost(11),
        name="attention",
    )(place, a1, *after(w_b, ins, far_ins, outs), other_split, bias_b, ours, theirs)

    g_got = move.arrange(g_got)
    both = whole((ROWS, 2 * GROUP))
    proj_block = whole((half, width, GROUP))
    keep_spec = pl.BlockSpec((1, width, hidden), lambda i, *_: (jnp.maximum(i - half, 0), 0, 0))
    send_spec = pl.BlockSpec((1, width, hidden), lambda i, *_: (jnp.minimum(i, half - 1), 0, 0))
    unit_spec = pl.BlockSpec(
        (1, 1, hidden), lambda i, *_: (jnp.where(i < half, 2 * i + 1, 2 * i - shares), 0, 0)
    )
    made = pl.pallas_call(
        functools.partial(mlp_kernel, move.frames),
        grid_spec=pltpu.PrefetchScalarGridSpec(
            num_scalar_prefetch=1,
            grid=(shares,),
            in_specs=[
                whole(g_got.shape), rows, both, both,
                *[whole((width, hidden + GROUP))] * shares,
                pl.BlockSpec((1, width, hidden), lambda i, *_: (jnp.maximum(i - half, 0), 0, 0)),
                pl.BlockSpec((1, width, hidden), lambda i, *_: (jnp.minimum(i, half - 1), 0, 0)),
                row, row, row, whole(split.shape), whole(split.shape), row,
            ],
            out_specs=[
                whole(move.shape(width)), rows, rows,
                keep_spec, send_spec, keep_spec, send_spec, proj_block,
                proj_block, unit_spec, whole((4, width)),
            ],
            scratch_shapes=[
                pltpu.VMEM((ROWS, width), f32),
                pltpu.VMEM((ROWS, width), bf16),
                pltpu.VMEM((width, ROWS), bf16),
                pltpu.VMEM((ROWS, width), bf16),
                pltpu.VMEM((width, ROWS), bf16),
                pltpu.VMEM((ROWS, width), f32),
                pltpu.VMEM((ROWS, 1), f32),
                pltpu.VMEM((ROWS, width), f32),
                pltpu.VMEM((ROWS, width), f32),
                pltpu.VMEM((ROWS, width), bf16),
                pltpu.VMEM((width, width), bf16),
                pltpu.VMEM((width, hidden), bf16),
                pltpu.VMEM((width, hidden), bf16),
                pltpu.VMEM((1, hidden), f32),
                pltpu.VMEM((ROWS, 256), f32),
                pltpu.VMEM((ROWS, 256), f32),
                pltpu.VMEM((ROWS, hidden), bf16),
                pltpu.VMEM((ROWS, hidden), bf16),
                pltpu.VMEM((width, hidden), bf16),
                pltpu.VMEM((width, hidden), bf16),
            ],
        ),
        out_shape=[
            shaped(move.shape(width), bf16),
            shaped((ROWS, width)),
            shaped((ROWS, width), bf16),
            shaped((half, width, hidden), bf16),
            shaped((half, width, hidden), bf16),
            shaped((half, width, hidden), bf16),
            shaped((half, width, hidden), bf16),
            shaped((half, width, GROUP), bf16),
            shaped((half, width, GROUP), bf16),
            shaped((shares, 1, hidden)),
            shaped((4, width)),
        ],
        compiler_params=room(60),
        cost_estimate=cost(22),
        name="mlp",
    )(
        place, g_got, x_rows, o_a, o_b, ins, near_ins, far_ins, last_ins, outs, away_outs,
        proj_shift, gain_two, shift_two, split, other_split, out_shift,
    )
    out_rows, dh, dow, in_keep, in_send, out_keep, out_send, proj_keep, proj_send, *made = made
    grad_in_shift, vec_two = made

    mine = jnp.concatenate(
        [
            plus(in_keep, swap(in_send, "tp", 1)),
            plus(out_keep, swap(out_send, "tp", 1)),
            plus(proj_keep, swap(proj_send, "tp", 1)),
        ],
        axis=-1,
    )
    far = mine[1]
    out_cells = move.leave(out_rows)
    out_got = move.exchange(out_cells)
    far_got = swap(far, "tp", 2)

    def back(pair, weights, given, extra, last):
        specs = [
            whole((width, ROWS)), w_block, w_block, query_block, key_block, key_block,
            pl.BlockSpec((ROWS, GROUP), lambda i, *_: (0, 2 * pair + i)),
            lse_block, bias_block, *features,
        ]
        specs += [whole(v.shape) for v in extra]
        made = [shaped((ROWS, width))]
        if last:
            made = [shaped(move.shape(width), bf16), shaped((2, width))]
        made_specs = [whole(v.shape) for v in made]
        made += [
            shaped((width, 3 * GROUP), bf16),
            shaped((width, 3 * GROUP), bf16),
            shaped((2, 1, 3 * GROUP)),
            shaped((2 * heads, KEYS, DIAG_PAD)),
        ]
        made_specs += [
            whole((width, 3 * GROUP)), whole((width, 3 * GROUP)), chunk((1, 3 * GROUP)), bias_block,
        ]
        scratch = [
            pltpu.VMEM((ROWS, width), f32),
            pltpu.VMEM((ROWS, 3 * GROUP), f32),
            w_scratch,
            pltpu.VMEM((ROWS, GROUP), f32),
            pltpu.VMEM((heads * ALL_KEYS, 2 * GROUP), bf16),
            pltpu.VMEM((heads * ALL_KEYS, GROUP), bf16),
            pltpu.VMEM((heads * ALL_KEYS, ALL_QUERIES), f32),
            pltpu.VMEM((heads * ALL_KEYS, ALL_QUERIES), f32),
            pltpu.VMEM((heads * ALL_KEYS, ALL_QUERIES), bf16),
            pltpu.VMEM((heads * ALL_KEYS, ALL_QUERIES), bf16),
            bias_scratch,
            bias_scratch,
        ]
        return pl.pallas_call(
            functools.partial(attention_back_kernel, last, move.frames),
            grid_spec=pltpu.PrefetchScalarGridSpec(
                num_scalar_prefetch=1,
                grid=(2,),
                in_specs=specs,
                out_specs=made_specs,
                scratch_shapes=scratch,
            ),
            out_shape=made,
            compiler_params=room(60),
            cost_estimate=cost(19),
            name="attention_back",
        )(place, a1_t, *weights, *given, ours, theirs, *extra)

    dow_b = after(dow, far, out_cells)
    running, keep_b, send_b, shift_b, sums_b = back(1, w_b, (q_b, k_b, v_b, dow_b, lse_b, bias_b), (), False)

    mine = plus(mine[0], after(far_got, keep_b))
    mine = split_rows(mine, 0)
    steps = list(reversed(bits_of("grp")))
    near_b = swap(send_b, "tp", 1)
    keep, send = halves(mine, 0, steps[0])
    got_first = swap(send, "grp", steps[0])
    out_part = after(out_got, keep_b)
    out_far = swap(out_part, "tp", 2)
    out_near = swap(out_part, "tp", 1)
    far_b = plus(keep_b, near_b)
    far_got_b = swap(far_b, "tp", 2)
    running = after(running, far_b, out_part, send)
    made = back(0, w_a, (q_a, k_a, v_a, dow, lse_a, bias_a), (running, x_rows, gain_one, dh), True)
    gx, vec_one, keep_a, send_a, shift_a, sums_a = made

    gx_cells = move.leave(after(gx, got_first, far_got_b))
    gx_got = move.exchange(gx_cells)
    out_far = after(out_far, gx_cells)
    near_a = swap(after(send_a, gx_cells), "tp", 1)

    def table_of(pair_sums):
        return pl.pallas_call(
            table_kernel,
            grid=(2,),
            in_specs=[bias_block, whole((PICK_ROWS, 256))],
            out_specs=pl.BlockSpec((heads, 1, TABLE_PAD), lambda i: (i, 0, 0)),
            out_shape=shaped((2 * heads, 1, TABLE_PAD)),
            scratch_shapes=[pltpu.VMEM((heads, KEYS, TABLE_PAD), f32)],
            compiler_params=room(60),
            cost_estimate=cost(6),
            name="table",
        )(pair_sums, pick)

    def rows_of(*parts):
        return jnp.concatenate([part.reshape(-1) for part in parts]).reshape(-1, 3 * GROUP)

    def slot(tables, shifts, which, in_slot):
        return (tables[which * heads : (which + 1) * heads], shifts[which], grad_in_shift[in_slot])

    tables_b = table_of(after(sums_b, gx_cells))
    tables_a = table_of(after(sums_a, tables_b))
    gx_part = after(gx_got, tables_a)
    gx_far = swap(gx_part, "tp", 2)
    gx_near = swap(gx_part, "tp", 1)
    keep, send = halves(plus(after(keep, gx_part), got_first), 0, steps[1])
    got_second = swap(send, "grp", steps[1])
    got_a = plus(plus(keep_a, near_a), far_got_b)
    got_a = split_rows(got_a, 0)
    vec = rows_of(vec_one, vec_two)
    small = rows_of(vec, *slot(tables_a, shift_a, 0, 0), *slot(tables_b, shift_b, 0, 2))
    sent = rows_of(vec, *slot(tables_a, shift_a, 1, 1), *slot(tables_b, shift_b, 1, 3))
    small = small + swap(sent, "tp", 1)
    lead = vec.shape[0]
    cut = lead + (small.shape[0] - lead) // 2
    small = small[:cut] + swap(jnp.concatenate([small[:lead], small[cut:]]), "tp", 2)
    tail = small
    output = (out_part, out_near, out_far, swap(after(out_far, tail), "tp", 1))
    output = move.home(output, 0, None, bf16, 3)
    grad_tokens = move.home((gx_part, after(gx_near, tail)), 0, None, f32, 0.1)
    mine = plus(keep, after(got_second, output))
    for bit in steps[2:]:
        keep, send = halves(mine, 0, bit)
        mine = plus(keep, swap(send, "grp", bit))
    mine = mine.reshape(depth, 2 * hidden + GROUP).astype(f32)

    last = swap(after(gx_far, grad_tokens), "tp", 1)
    final = move.home((gx_far, last), 2, grad_tokens, f32, 0.1)

    for i, bit in enumerate(steps):
        keep, send = halves(got_a, 0, bit)
        high = lax.reduce_precision(small, 8, 7)
        low = (small - high).astype(bf16)
        size = send.size // (3 * GROUP)
        sent = jnp.concatenate([send.reshape(size, 3 * GROUP), high.astype(bf16), low])
        if i == 0:
            sent = after(sent, gx_far, grad_tokens)
        got = swap(sent, "grp", bit)
        if i == len(steps) - 1:
            got = after(got, final)
        got_a = plus(keep, got[:size].reshape(keep.shape))
        got = got[size:].astype(f32)
        small = small + got[:cut] + got[cut:]
    got_a = got_a.reshape(depth, 3, GROUP).astype(f32)
    vec = small[:lead].reshape(6, width)
    vec = lax.dynamic_slice_in_dim(vec, lax.axis_index("grp") * depth, depth, 1)
    small = small[lead:].reshape(-1)
    got_table = small[: heads * TABLE_PAD].reshape(heads, TABLE_PAD)[:, :TABLE].T
    got_shift = small[heads * TABLE_PAD :][: 3 * GROUP].reshape(3, GROUP)
    got_in_shift = small[heads * TABLE_PAD + 3 * GROUP :]

    return (
        output,
        final,
        vec[0],
        vec[1],
        got_a,
        jnp.stack([got_shift[0], got_shift[2]]),
        got_table,
        mine[:, 2 * hidden :],
        vec[4],
        vec[2],
        vec[3],
        mine[:, :hidden],
        got_in_shift,
        mine[:, hidden : 2 * hidden],
        vec[5],
    )


def solution(mesh):
    shard = P("grp")
    tokens = P(None, "grp", None)
    placed = (
        tokens, tokens, shard, shard, P("grp", None, "tp"), P(None, "tp"), P(None, "tp"),
        P("grp", "tp"), shard, shard, shard, P("grp", "tp"), P("tp"), P("grp", "tp"), shard,
    )
    return jax.shard_map(
        per_device, mesh=mesh, in_specs=placed, out_specs=placed, check_vma=False
    )
```

```python
import functools

import jax
import jax.numpy as jnp
import numpy as np
from jax import lax
from jax.experimental import pallas as pl
from jax.experimental.pallas import tpu as pltpu
from jax.sharding import PartitionSpec as P

CT, CH, CW = 16, 14, 14
WT, WH, WW = 8, 7, 7
ST, SH, SW = 4, 3, 3
FRAME = CH * CW
SIDE = WH * WW
WIN = WT * SIDE
PAIR = 2
PADDED = -(-WIN // 16) * 16
ROWS = PAIR * PADDED
HEAD = 32
GROUP = 128
HEADS_IN = GROUP // HEAD
SPAN_T, SPAN_H, SPAN_W = 2 * WT - 1, 2 * WH - 1, 2 * WW - 1
PLANE = SPAN_H * SPAN_W
TABLE = SPAN_T * PLANE
TABLE_PAD = -(-TABLE // 128) * 128
LANES = 64
DIAG_PAD = (SPAN_T + 1) * LANES
KEYS = -(-SIDE // 8) * 8
ALL_KEYS, ALL_QUERIES = WT * KEYS, WT * LANES
CORNER = PLANE // 2
LOG2E = 1.4426950408889634
SCALE = HEAD ** (-0.5)
FAR = -(2.0**100)
f32 = jnp.float32
bf16 = jnp.bfloat16


def room(mib):
    return pltpu.CompilerParams(vmem_limit_bytes=mib * 1024 * 1024)


def cost(micros):
    return pl.CostEstimate(flops=int(micros * 1.1e9), bytes_accessed=1 << 20, transcendentals=0)


def dot(a, b):
    return lax.dot_general(a, b, (((1,), (0,)), ((), ())), preferred_element_type=f32)


def dot_t(a, b):
    return lax.dot_general(a, b, (((1,), (1,)), ((), ())), preferred_element_type=f32)


def moments(rows):
    centered = rows - jnp.mean(rows, axis=-1, keepdims=True)
    inverse = lax.rsqrt(jnp.mean(centered * centered, axis=-1, keepdims=True) + 1e-05)
    return centered * inverse, inverse


def norm_back(grad, unit, inverse, gain):
    scaled = grad * gain
    shared = jnp.mean(scaled, axis=-1, keepdims=True)
    along = jnp.mean(scaled * unit, axis=-1, keepdims=True)
    return inverse * (scaled - shared - unit * along)


def read_rows(target, ref, frames):
    if not frames:
        target[...] = ref[...].astype(f32)
        return
    count, _, size, _ = ref.shape
    for window in range(PAIR):
        for i in range(count):
            start = window * PADDED + i * frames * SIDE
            target[pl.ds(start, size), :] = ref[i, window].astype(f32)
        start = window * PADDED + WIN
        target[pl.ds(start, PADDED - WIN), :] = jnp.zeros((PADDED - WIN, target.shape[1]), f32)


def write_rows(ref, source, frames):
    if not frames:
        ref[...] = source[...].astype(bf16)
        return
    count, _, size, _ = ref.shape
    for window in range(PAIR):
        for i in range(count):
            start = window * PADDED + i * frames * SIDE
            ref[i, window] = source[pl.ds(start, size), :].astype(bf16)


def cells_kernel(facts_ref, tokens_ref, order_ref, out_ref):
    size, block = out_ref.shape[2], order_ref.shape[0] // 4
    rows = dot(order_ref[...], tokens_ref[0])
    for i in range(4):
        out_ref[i // 2, i % 2] = rows[i * block : i * block + size].astype(bf16)


def home_kernel(count, facts_ref, *refs):
    order_ref = refs[count]
    out_ref, rows = refs[-2:]
    step = pl.program_id(0)
    size, block = refs[0].shape[2], rows.shape[0] // 4

    @pl.when(step == 0)
    def _():
        rows[...] = jnp.zeros_like(rows)

    for clip in range(out_ref.shape[0]):
        for device in range(count):

            @pl.when(step == device)
            def _():
                for i in range(4):
                    piece = refs[device][2 * clip + i // 2, i % 2]
                    rows[i * block : i * block + size, :] = piece.astype(f32)

        out_ref[clip] = dot(order_ref[...], rows[...].astype(bf16)).astype(out_ref.dtype)


SPANS = []
for _lane in range(0, DIAG_PAD, 256):
    _low = _lane // LANES * PLANE // 128 * 128
    _high = min((_lane + 255) // LANES + 1, SPAN_T) * PLANE
    SPANS.append((_lane, _low, -(-_high // 128) * 128))
PICK_ROWS = sum(high - low for _, low, high in SPANS)


def bias_kernel(table_ref, pick_ref, bias_ref, sheared):
    heads = bias_ref.shape[0]
    tables = table_ref[0].astype(f32)
    for head in range(heads):
        flat = jnp.broadcast_to(tables[head : head + 1], (8, TABLE_PAD))
        stairs = pltpu.roll(flat, 0, 1, stride=1, stride_axis=0)
        for row in range(WH):
            shift = (row * SPAN_W - CORNER) % TABLE_PAD
            sheared[head, pl.ds(row * WW, 8), :] = pltpu.roll(stairs, shift, 1)
        sheared[head, SIDE:KEYS, :] = jnp.zeros((KEYS - SIDE, TABLE_PAD), f32)
    everything = sheared[...].reshape(heads * KEYS, TABLE_PAD).astype(bf16)
    start = 0
    for lane, low, high in SPANS:
        part = dot(everything[:, low:high], pick_ref[start : start + high - low]) * LOG2E
        bias_ref[:, :, lane : lane + 256] = part.reshape(heads, KEYS, 256)
        start += high - low


def table_kernel(sums_ref, pick_ref, grad_ref, sheared):
    heads = sums_ref.shape[0]
    everything = sums_ref[...].reshape(heads * KEYS, DIAG_PAD).astype(bf16)
    done = 0
    start = 0
    for lane, low, high in SPANS:
        part = dot_t(everything[:, lane : lane + 256], pick_ref[start : start + high - low])
        part = part.reshape(heads, KEYS, high - low)
        if done > low:
            sheared[:, :, low:done] += part[:, :, : done - low]
            sheared[:, :, done:high] = part[:, :, done - low :]
        else:
            sheared[:, :, low:high] = part
        done = high
        start += high - low
    row_in = lax.broadcasted_iota(jnp.int32, (8, TABLE_PAD), 0)
    for head in range(heads):
        stairs = jnp.zeros((8, TABLE_PAD), f32)
        for row in range(WH):
            shift = (CORNER - row * SPAN_W) % TABLE_PAD
            stairs = stairs + pltpu.roll(sheared[head, pl.ds(row * WW, 8), :], shift, 1)
        flat = jnp.where(row_in == 0, stairs, 0.0)
        for step in range(1, WW):
            moved = pltpu.roll(stairs, TABLE_PAD - step, 1)
            flat = flat + jnp.where(row_in == step, moved, 0.0)
        grad_ref[head] = jnp.sum(flat, axis=0, keepdims=True)


def spread_frames(source, window, columns, stride):
    place = lax.broadcasted_iota(jnp.int32, (KEYS, GROUP), 0)
    parts = []
    for frame in range(WT):
        rows = source[pl.ds(window * PADDED + frame * SIDE, KEYS), columns]
        parts.append(jnp.where(place < SIDE, rows, 0.0))
        if stride > KEYS:
            parts.append(jnp.zeros((stride - KEYS, GROUP), f32))
    return jnp.concatenate(parts, axis=0)


def close_frames(target, window, columns, rows, stride):
    for frame in range(WT):
        place = pl.ds(window * PADDED + frame * SIDE, KEYS)
        target[place, columns] = rows[frame * stride : frame * stride + KEYS]
    place = slice(window * PADDED + WIN, (window + 1) * PADDED)
    target[place, columns] = jnp.zeros((PADDED - WIN, GROUP), f32)


def turn_bias(target, bias_ref):
    for head in range(bias_ref.shape[0]):
        target[head, 0] = bias_ref[head]
        target[head, 1] = pltpu.roll(bias_ref[head], DIAG_PAD - LANES, 1)


def frame_bias(head, frame, lanes):
    start = (WT - 1 - frame) * LANES
    copy = start // LANES % 2
    start = start - copy * LANES + lanes
    return (head, copy, slice(None), slice(start, start + 256))


def by_tile(rows, how):
    return how(rows.reshape(rows.shape[0] // 8, 8, rows.shape[1]), axis=0)


def mask_heads(target, rows, lane):
    for head in range(HEADS_IN):
        masked = jnp.where(lane == head, rows, jnp.zeros_like(rows))
        target[head * ALL_KEYS : (head + 1) * ALL_KEYS, 0:GROUP] = masked


def attention_kernel(first, frames, *refs):
    step = pl.program_id(0)
    refs = refs[1:]
    if first:
        got_ref, gain_ref, shift_ref, w0_ref, w1_ref, wb_ref, bias_ref, qf_ref, kf_ref = refs[:9]
        x_ref, a1_ref, a1_t_ref, q_ref, k_ref, v_ref, o_ref, lse_ref = refs[9:17]
        w_ref, wide, keys, logits, probs, rows_o, bias, rows_in = refs[17:]

        @pl.when(step == 0)
        def _():
            read_rows(rows_in, got_ref, frames)
            x_ref[...] = rows_in[...].astype(bf16)
            unit, _ = moments(rows_in[...])
            low = unit * gain_ref[...] + shift_ref[...]
            a1_ref[...] = low.astype(bf16)
            a1_t_ref[...] = a1_ref[...].T
    else:
        a1_ref, w0_ref, w1_ref, wb_ref, bias_ref, qf_ref, kf_ref = refs[:7]
        q_ref, k_ref, v_ref, o_ref, lse_ref = refs[7:12]
        w_ref, wide, keys, logits, probs, rows_o, bias = refs[12:]

    @pl.when(step == 0)
    def _():
        w_ref[...] = w0_ref[...]

    @pl.when(step == 1)
    def _():
        w_ref[...] = w1_ref[...]

    turn_bias(bias, bias_ref)
    shift = wb_ref[0].astype(f32)[HEADS_IN : HEADS_IN + 1]
    nothing = jnp.zeros((1, GROUP), f32)
    shift = jnp.concatenate([shift[:, :GROUP], nothing, shift[:, GROUP : 2 * GROUP]], axis=1)
    wide[...] = dot(a1_ref[...], w_ref[...]) + shift
    lane = lax.broadcasted_iota(jnp.int32, (ALL_KEYS, GROUP), 1) // HEAD
    for window in range(PAIR):
        query = spread_frames(wide, window, slice(0, GROUP), LANES).astype(bf16)
        key = spread_frames(wide, window, slice(GROUP, 2 * GROUP), KEYS).astype(bf16)
        value = spread_frames(wide, window, slice(2 * GROUP, 3 * GROUP), KEYS)
        q_ref[0, window] = query
        k_ref[0, window] = key
        v_ref[0, window] = value.astype(bf16)
        value_t = value.T.astype(bf16)
        mask_heads(keys, key, lane)
        for head in range(HEADS_IN):
            keys[head * ALL_KEYS : (head + 1) * ALL_KEYS, GROUP : 2 * GROUP] = kf_ref[0, window]
        logits[...] = dot_t(keys[...], jnp.concatenate([query, qf_ref[0, window]], axis=1))
        parts = []
        for head in range(HEADS_IN):
            tops, totals = [], []
            for lanes in range(0, ALL_QUERIES, 256):
                across = slice(lanes, lanes + 256)
                top = jnp.full((8, 256), -jnp.inf, f32)
                for frame in range(WT):
                    at = head * ALL_KEYS + frame * KEYS
                    block = logits[at : at + KEYS, across] * (SCALE * LOG2E)
                    block = block + bias[frame_bias(head, frame, lanes)]
                    logits[at : at + KEYS, across] = block
                    top = jnp.maximum(top, by_tile(block, jnp.max))
                top = jnp.max(top, axis=0, keepdims=True)
                total = jnp.zeros((8, 256), f32)
                for pair in range(0, ALL_KEYS, 2 * KEYS):
                    at = head * ALL_KEYS + pair
                    block = jnp.exp2(logits[at : at + 2 * KEYS, across] - top)
                    total = total + by_tile(block, jnp.sum)
                    probs[pair : pair + 2 * KEYS, across] = block.astype(bf16)
                tops.append(top)
                totals.append(jnp.sum(total, axis=0, keepdims=True))
            total = jnp.concatenate(totals, axis=1)
            lse = jnp.concatenate(tops, axis=1) + jnp.log2(total)
            lse_ref[0, pl.ds(window * HEADS_IN + head, 1), :] = lse
            mixed = dot(value_t[head * HEAD : (head + 1) * HEAD], probs[...])
            parts.append(mixed / total)
        mixed = jnp.concatenate(parts, axis=0).T
        close_frames(rows_o, window, slice(None), mixed, LANES)
    o_ref[...] = rows_o[...].astype(bf16)


def mlp_kernel(frames, facts_ref, *refs):
    got_ref, x_ref, oa_ref, ob_ref = refs[:4]
    weights, home_ref, away_ref = refs[4:8], refs[8], refs[9]
    pb_ref, gain_ref, shift_ref, near_ref, far_ref, out_shift_ref = refs[10:16]
    out_ref, refs = refs[16], refs[17:]
    dh_ref, dow_ref, gwi_keep, gwi_send, gwo_keep, gwo_send, gwp_keep, gwp_send = refs[:8]
    gib_ref, vec_ref = refs[8:10]
    hidden, a2, a2_t, g_ref, g_t, unit_s, inv_s, acc_out, acc_in, o_all, wp = refs[10:21]
    wi, wo, ib_ref, u_s, back_s, act, du, grad_out_w, grad_in_w = refs[21:]
    step = pl.program_id(0)
    width = x_ref.shape[1]
    units = gib_ref.shape[2]

    @pl.when(step == 0)
    def _():
        o_all[:, 0 : 2 * GROUP] = oa_ref[...]
        o_all[:, 2 * GROUP : 4 * GROUP] = ob_ref[...]
        for i, ref in enumerate(weights):
            wp[:, i * GROUP : (i + 1) * GROUP] = ref[:, units : units + GROUP]
        branch = dot_t(o_all[...], wp[...])
        hidden[...] = x_ref[...].astype(f32) + branch + pb_ref[...]
        unit, inverse = moments(hidden[...])
        unit_s[...] = unit
        inv_s[...] = inverse
        low = unit * gain_ref[...] + shift_ref[...]
        a2[...] = low.astype(bf16)
        a2_t[...] = a2[...].T
        read_rows(acc_out, got_ref, frames)
        g_ref[...] = acc_out[...].astype(bf16)
        g_t[...] = g_ref[...].T
        acc_out[...] = jnp.zeros_like(acc_out)
        acc_in[...] = jnp.zeros_like(acc_in)

    for i, slot in enumerate((1, 3, 0, 2)):

        @pl.when(step == i)
        def _():
            wi[...] = weights[slot][:, 0:units]
            wo[...] = (away_ref if slot % 2 else home_ref)[0]
            shifts = (near_ref if slot < 2 else far_ref)[slot % 2].astype(f32)
            ib_ref[...] = shifts[HEADS_IN + 1 : HEADS_IN + 2, 0:units]

    for first in range(0, units, 256):
        some = slice(first, first + 256)
        u_s[...] = dot(a2[...], wi[:, some])
        back_s[...] = dot(g_ref[...], wo[:, some])
        sums = jnp.zeros((8, 256), f32)
        for row in range(0, ROWS, 80):
            rows = slice(row, row + 80)
            u = u_s[rows] + ib_ref[:, some]
            half = 0.5 * (1.0 + lax.erf(u * (0.5**0.5)))
            act[rows, some] = (u * half).astype(bf16)
            slope = half + u * jnp.exp(-0.5 * u * u) * 0.3989422804014327
            low = (back_s[rows] * slope).astype(bf16)
            du[rows, some] = low
            sums = sums + by_tile(low.astype(f32), jnp.sum)
        gib_ref[0, :, some] = jnp.sum(sums, axis=0, keepdims=True)
        grad_out_w[:, some] = dot(g_t[...], act[:, some]).astype(bf16)
        grad_in_w[:, some] = dot(a2_t[...], du[:, some]).astype(bf16)
    acc_out[...] += dot_t(act[...], wo[...])
    acc_in[...] += dot_t(du[...], wi[...])

    @pl.when(step < 2)
    def _():
        gwo_send[0] = grad_out_w[...]
        gwi_send[0] = grad_in_w[...]

    @pl.when(step >= 2)
    def _():
        gwo_keep[0] = grad_out_w[...]
        gwi_keep[0] = grad_in_w[...]

    @pl.when(step == pl.num_programs(0) - 1)
    def _():
        acc_out[...] += hidden[...] + out_shift_ref[...]
        write_rows(out_ref, acc_out, frames)
        upstream = g_ref[...].astype(f32)
        grad = acc_in[...]
        unit = unit_s[...]
        dh = upstream + norm_back(grad, unit, inv_s[...], gain_ref[...])
        dh_ref[...] = dh
        dz = dh.astype(bf16)
        dow_ref[...] = dot(dz, wp[...]).astype(bf16)
        grad_wp = dot(dz.T, o_all[...])
        for i in range(2):
            gwp_keep[i] = grad_wp[:, 2 * i * GROUP : (2 * i + 1) * GROUP].astype(bf16)
            gwp_send[i] = grad_wp[:, (2 * i + 1) * GROUP : (2 * i + 2) * GROUP].astype(bf16)
        vec_ref[...] = jnp.concatenate(
            [
                jnp.sum(grad * unit, axis=0, keepdims=True),
                jnp.sum(grad, axis=0, keepdims=True),
                jnp.sum(dz.astype(f32), axis=0, keepdims=True),
                jnp.sum(upstream, axis=0, keepdims=True),
            ],
            axis=0,
        )


def attention_back_kernel(last, frames, facts_ref, *refs):
    a1_t_ref, w0_ref, w1_ref, q_ref, k_ref, v_ref, dow_ref, lse_ref, bias_ref, qf_ref, kf_ref = refs[:11]
    refs = refs[11:]
    if last:
        sum_ref, x_ref, gain_ref, dh_ref, gx_ref, vec_ref = refs[:6]
        refs = refs[6:]
    else:
        sum_ref, refs = refs[0], refs[1:]
    keep_ref, send_ref, gb_ref, sums_ref, acc, dqkv, w_ref = refs[:7]
    rows_in, keys, values, probs_f, dp, probs, ds, shifted, bias = refs[7:]
    step = pl.program_id(0)

    @pl.when(step == 0)
    def _():
        w_ref[...] = w0_ref[...]

    @pl.when(step == 1)
    def _():
        w_ref[...] = w1_ref[...]

    shifted[...] = jnp.zeros_like(shifted)
    turn_bias(bias, bias_ref)
    rows_in[...] = dow_ref[...].astype(f32)
    lane = lax.broadcasted_iota(jnp.int32, (ALL_KEYS, GROUP), 1) // HEAD
    for window in range(PAIR):
        query, key, value = q_ref[0, window], k_ref[0, window], v_ref[0, window]
        dow = spread_frames(rows_in, window, slice(None), LANES).astype(bf16)
        key_t = key.astype(f32).T.astype(bf16)
        mask_heads(keys, key, lane)
        mask_heads(values, value, lane)
        for head in range(HEADS_IN):
            keys[head * ALL_KEYS : (head + 1) * ALL_KEYS, GROUP : 2 * GROUP] = kf_ref[0, window]
        probs_f[...] = dot_t(keys[...], jnp.concatenate([query, qf_ref[0, window]], axis=1))
        dp[...] = dot_t(values[...], dow)
        for head in range(HEADS_IN):
            lse = lse_ref[0, pl.ds(window * HEADS_IN + head, 1), :]
            for lanes in range(0, ALL_QUERIES, 256):
                across = slice(lanes, lanes + 256)
                dots = jnp.zeros((8, 256), f32)
                for pair in range(0, WT, 2):
                    blocks = []
                    for frame in (pair, pair + 1):
                        at = head * ALL_KEYS + frame * KEYS
                        block = probs_f[at : at + KEYS, across] * (SCALE * LOG2E)
                        block = block + bias[frame_bias(head, frame, lanes)]
                        blocks.append(block)
                    at = head * ALL_KEYS + pair * KEYS
                    block = jnp.exp2(jnp.concatenate(blocks, axis=0) - lse[:, across])
                    probs_f[at : at + 2 * KEYS, across] = block
                    probs[at : at + 2 * KEYS, across] = block.astype(bf16)
                    dots = dots + by_tile(block * dp[at : at + 2 * KEYS, across], jnp.sum)
                dots = jnp.sum(dots, axis=0, keepdims=True)
                for pair in range(0, WT, 2):
                    at = head * ALL_KEYS + pair * KEYS
                    block = probs_f[at : at + 2 * KEYS, across]
                    block = block * (dp[at : at + 2 * KEYS, across] - dots)
                    ds[at : at + 2 * KEYS, across] = block.astype(bf16)
                    for i in range(2):
                        place = frame_bias(head, pair + i, lanes)
                        shifted[place] += block[i * KEYS : (i + 1) * KEYS]
        dv_all = dot(probs[...], dow)
        dk_all = dot(ds[...], query)
        none = jnp.zeros((ALL_KEYS, GROUP), f32)
        dk, dv, dq_t = none, none, []
        for head in range(HEADS_IN):
            part = slice(head * ALL_KEYS, (head + 1) * ALL_KEYS)
            dv = jnp.where(lane == head, dv_all[part], dv)
            dk = jnp.where(lane == head, dk_all[part], dk)
            dq_t.append(dot(key_t[head * HEAD : (head + 1) * HEAD], ds[part]))
        dq = jnp.concatenate(dq_t, axis=0).T
        close_frames(dqkv, window, slice(0, GROUP), dq * SCALE, LANES)
        close_frames(dqkv, window, slice(GROUP, 2 * GROUP), dk * SCALE, KEYS)
        close_frames(dqkv, window, slice(2 * GROUP, 3 * GROUP), dv, KEYS)
    for head in range(HEADS_IN):
        sums_ref[head] = shifted[head, 0] + pltpu.roll(shifted[head, 1], LANES, 1)
    low = dqkv[...].astype(bf16)
    grad = dot_t(low, w_ref[...])
    grad_w = dot(a1_t_ref[...], low)
    gb_ref[0] = jnp.sum(low.astype(f32), axis=0, keepdims=True)

    @pl.when(step == 0)
    def _():
        acc[...] = grad + sum_ref[...] if last else grad
        keep_ref[...] = grad_w.astype(bf16)

    @pl.when(step == 1)
    def _():
        send_ref[...] = grad_w.astype(bf16)
        total = acc[...] + grad
        if last:
            unit, inverse = moments(x_ref[...].astype(f32))
            acc[...] = dh_ref[...] + norm_back(total, unit, inverse, gain_ref[...])
            write_rows(gx_ref, acc, frames)
            vec_ref[...] = jnp.concatenate(
                [jnp.sum(total * unit, axis=0, keepdims=True), jnp.sum(total, axis=0, keepdims=True)],
                axis=0,
            )
        else:
            sum_ref[...] = total


def whole(shape):
    return pl.BlockSpec(shape, lambda *i: (0,) * len(shape))


def shaped(shape, kind=f32):
    return jax.ShapeDtypeStruct(shape, kind)


def chunk(shape):
    return pl.BlockSpec((1,) + shape, lambda i, *_: (i,) + (0,) * len(shape))


def pick_matrix():
    place = np.arange(TABLE_PAD)
    row, column = place % PLANE // SPAN_W, place % PLANE % SPAN_W
    target = place // PLANE * LANES + row * WW + column
    good = (place < TABLE) & (row < WH) & (column < WW)
    target = np.where(good, target, -1)
    target = np.concatenate([target[low:high] - lane for lane, low, high in SPANS])
    return jnp.asarray(np.arange(256) == target[:, None], bf16)


def region_features():
    lane = np.arange(GROUP)

    def codes(stride, is_late, is_low, is_right):
        frame, cell = np.divmod(np.arange(WT * stride), stride)
        code = (
            (is_late * (frame >= WT - ST)) * 4
            + (is_low * (cell // WW >= WH - SH)) * 2
            + is_right * (cell % WW >= WW - SW)
        )
        return (cell < SIDE)[:, None], code[:, None]

    ours, theirs = [], []
    for is_late in range(2):
        for is_low in range(2):
            for is_right in range(PAIR):
                real, code = codes(LANES, is_late, is_low, is_right)
                ours.append((real & (lane == code)) | (lane == 8))
                real, code = codes(KEYS, is_late, is_low, is_right)
                other = np.where(real, (lane < 8) & (lane != code), lane == 8)
                theirs.append(np.where(other, FAR, 0.0))
    ours = jnp.asarray(np.reshape(ours, (4, PAIR, ALL_QUERIES, GROUP)), bf16)
    return ours, jnp.asarray(np.reshape(theirs, (4, PAIR, ALL_KEYS, GROUP)), bf16)


def cell_order(frames):
    size = frames * SIDE
    step = -(-size // 16) * 16
    matrix = np.zeros((4 * step, frames * FRAME), bool)
    for low in range(2):
        for right in range(2):
            for cell in range(size):
                frame, row, column = cell // SIDE, cell // WW % WH, cell % WW
                row = (low * WH + row + SH) % CH
                column = (right * WW + column + SW) % CW
                place = frame * FRAME + row * CW + column
                matrix[(low * 2 + right) * step + cell, place] = True
    return matrix


class Windows:
    def __init__(self, clips, local, groups, shares):
        self.share = clips // shares
        self.local = local
        self.half = groups // 2
        first = ST * FRAME // local
        order = [(first + i) % groups for i in range(groups)]
        self.groups = [order[: self.half], order[self.half :]]
        self.frames = local // FRAME if local % FRAME == 0 else 0
        slot = (lax.axis_index("grp") - first) % groups
        self.low = slot % 2
        me = lax.axis_index("tp")
        order = [me * self.share, slot // self.half * 2 + self.low]
        order += [me ^ i for i in range(shares)]
        self.facts = lax.optimization_barrier(jnp.stack(order).astype(jnp.int32))

    def exchange(self, rows):
        return lax.all_to_all(
            rows, "grp", split_axis=0, concat_axis=0, tiled=True, axis_index_groups=self.groups
        )

    def shape(self, width):
        if not self.frames:
            return (ROWS, width)
        return (self.half, 2, -(-self.frames * SIDE // 8) * 8, width)

    def before(self, field):
        width = field.shape[-1]
        place = lax.axis_index("tp") * self.share
        if not self.frames:
            own = lax.dynamic_slice_in_dim(field, place, self.share, 0)
            return jnp.repeat(own, 2, axis=0)
        order = jnp.asarray(cell_order(self.frames), bf16)
        shape = self.shape(width)
        return pl.pallas_call(
            cells_kernel,
            grid_spec=pltpu.PrefetchScalarGridSpec(
                num_scalar_prefetch=1,
                grid=(self.share,),
                in_specs=[
                    pl.BlockSpec((1, self.local, width), lambda i, facts: (facts[0] + i, 0, 0)),
                    whole(order.shape),
                ],
                out_specs=pl.BlockSpec((2,) + shape[1:], lambda i, facts: (i, 0, 0, 0)),
            ),
            out_shape=shaped(shape, bf16),
            compiler_params=room(60),
            cost_estimate=cost(3),
            name="cells",
        )(self.facts, field, order)

    def home(self, parts, first, into, kind, micros):
        width = parts[0].shape[-1]
        size = lax.axis_size("tp")
        clips = size * self.share
        if not self.frames:
            if into is None:
                into = jnp.zeros((clips, self.local, width), kind)
            for i, part in enumerate(parts):
                part = part.reshape(self.share, 2, self.local, width)
                part = (part[:, 0] + part[:, 1]).astype(kind)
                start = (lax.axis_index("tp") ^ (first + i)) * self.share
                into = lax.dynamic_update_slice_in_dim(into, part, start, 0)
            return into
        order = jnp.asarray(cell_order(self.frames).T, bf16)
        extra = [] if into is None else [into]

        def place(step, facts):
            return (facts[2 + first + step], 0, 0)

        return pl.pallas_call(
            functools.partial(home_kernel, len(parts)),
            grid_spec=pltpu.PrefetchScalarGridSpec(
                num_scalar_prefetch=1,
                grid=(len(parts),),
                in_specs=[whole(parts[0].shape)] * len(parts)
                + [whole(order.shape)]
                + [pl.BlockSpec(memory_space=pl.ANY)] * len(extra),
                out_specs=pl.BlockSpec((self.share, self.local, width), place),
                scratch_shapes=[pltpu.VMEM((order.shape[1], width), f32)],
            ),
            out_shape=shaped((clips, self.local, width), kind),
            input_output_aliases={len(parts) + 2: 0} if extra else {},
            compiler_params=room(60),
            cost_estimate=cost(micros),
            name="home",
        )(self.facts, *parts, order, *extra)

    def arrange(self, cells):
        if self.frames:
            return cells
        width = cells.shape[-1]
        cells = cells.reshape(WT, CH, CW, width)
        cells = jnp.roll(cells, (-SH, -SW), axis=(1, 2))
        cells = lax.dynamic_slice_in_dim(cells, self.low * WH, WH, 1)
        cells = cells.reshape(WT, WH, 2, WW, width).transpose(2, 0, 1, 3, 4)
        cells = cells.reshape(PAIR, WIN, width)
        cells = jnp.pad(cells, ((0, 0), (0, PADDED - WIN), (0, 0)))
        return cells.reshape(ROWS, width)

    def leave(self, rows):
        if self.frames:
            return rows
        width = rows.shape[-1]
        cells = rows.reshape(PAIR, PADDED, width)[:, :WIN]
        cells = cells.reshape(2, WT, WH, WW, width).transpose(1, 2, 0, 3, 4)
        cells = cells.reshape(WT, WH, CW, width)
        blank = jnp.zeros((WT, CH, CW, width), cells.dtype)
        cells = lax.dynamic_update_slice_in_dim(blank, cells, self.low * WH, 1)
        cells = jnp.roll(cells, (SH, SW), axis=(1, 2))
        return cells.reshape(self.half, self.local, width)


def swap(field, axis, bit):
    size = lax.axis_size(axis)
    return lax.ppermute(field, axis, [(i, i ^ bit) for i in range(size)])


def bits_of(axis):
    size = lax.axis_size(axis)
    return [1 << i for i in reversed(range(size.bit_length() - 1))]


def flag_of(axis, bit):
    return lax.axis_index(axis) // bit % 2


def after(value, *others):
    return lax.optimization_barrier((value, others))[0]


def join(mine, other, bit, axis, place):
    second = flag_of(axis, bit) == 1
    return jnp.concatenate(
        [jnp.where(second, other, mine), jnp.where(second, mine, other)], axis=place
    )


class Gather:
    def __init__(self, part):
        self.bits = bits_of("grp")
        self.shape = part.shape
        self.field = part.reshape((1,) * len(self.bits) + part.shape)
        self.coming = ()
        self.done = 0

    def send(self, *others, double=False):
        self.field = after(self.field, *others)
        bit = self.bits[self.done]
        which = [bit, bit // 2, bit + bit // 2] if double else [bit]
        self.coming = [swap(self.field, "grp", i) for i in which]
        return self.field

    def take(self):
        bit, place = self.bits[self.done], self.done
        if len(self.coming) == 1:
            self.field = join(self.field, self.coming[0], bit, "grp", place)
            self.done += 1
            return
        one, two, both = self.coming
        near = join(self.field, two, bit // 2, "grp", place + 1)
        far = join(one, both, bit // 2, "grp", place + 1)
        self.field = join(near, far, bit, "grp", place)
        self.done += 2

    def result(self):
        return self.field.reshape((self.shape[0] << len(self.bits),) + self.shape[1:])


def plus(one, other):
    return (one.astype(f32) + other.astype(f32)).astype(bf16)


def split_rows(field, lead):
    bits = bits_of("grp")
    shape = field.shape
    rows = shape[lead] >> len(bits)
    return field.reshape(shape[:lead] + (2,) * len(bits) + (rows,) + shape[lead + 1 :])


def halves(field, lead, bit):
    place = lead + bits_of("grp").index(bit)
    mine = flag_of("grp", bit)
    keep = lax.dynamic_index_in_dim(field, mine, place, keepdims=True)
    send = lax.dynamic_index_in_dim(field, 1 - mine, place, keepdims=True)
    return keep, send


def per_device(
    tokens, grad_out, ln1_gain, ln1_shift, w_qkv, qkv_bias, rel_table, w_proj, proj_bias,
    ln2_gain, ln2_shift, w_in, in_bias, w_out, out_bias,
):
    groups, shares = lax.axis_size("grp"), lax.axis_size("tp")
    clips, local, width = tokens.shape
    move = Windows(clips, local, groups, shares)
    depth = w_qkv.shape[0]
    hidden = w_in.shape[1]
    heads = rel_table.shape[1]
    half = shares // 2

    later = Gather(jnp.concatenate([w_in, w_out, w_proj], axis=1))
    later_bits = later.bits
    vectors = jnp.stack([ln1_gain, ln1_shift, proj_bias, ln2_gain, ln2_shift, out_bias])
    first = jnp.concatenate(
        [w_qkv.reshape(depth, 3 * GROUP), jnp.pad(vectors.T, ((0, 0), (0, GROUP - 6)))], axis=1
    )
    first = Gather(first)
    for _ in range(len(first.bits) - 3):
        for chain in (first, later):
            chain.send()
            chain.take()
    split = jnp.concatenate(
        [
            jnp.pad(rel_table.T, ((0, 0), (0, TABLE_PAD - TABLE))),
            jnp.pad(qkv_bias.reshape(1, -1), ((0, 0), (0, TABLE_PAD - qkv_bias.size))),
            jnp.pad(in_bias[None], ((0, 3 - heads % 2), (0, TABLE_PAD - hidden))),
        ]
    )
    split = jnp.stack([split, swap(split, "tp", 1)])
    other_split = swap(split, "tp", 2)

    pick = pick_matrix()
    ours, theirs = region_features()

    def bias_of(half_split):
        return pl.pallas_call(
            bias_kernel,
            grid=(2,),
            in_specs=[chunk(half_split.shape[1:]), whole((PICK_ROWS, 256))],
            out_specs=pl.BlockSpec((heads, KEYS, DIAG_PAD), lambda i: (i, 0, 0)),
            out_shape=shaped((2 * heads, KEYS, DIAG_PAD)),
            scratch_shapes=[pltpu.VMEM((heads, KEYS, TABLE_PAD), f32)],
            compiler_params=room(60),
            cost_estimate=cost(6),
            name="bias",
        )(half_split, pick)

    sent = first.send(double=True)
    sent = sent, later.send(sent)
    x_send = move.before(after(tokens, sent))
    first.take()
    later.take()
    sent = first.send(x_send), later.send(x_send)
    x_got = move.exchange(after(x_send, sent))
    bias_a = bias_of(after(split, sent))
    first.take()
    later.take()
    first, later = after((first.result(), later.field), bias_a)
    bit, at = later_bits[-1], len(later_bits) - 1
    ins = jnp.concatenate([later[..., :hidden], later[..., 2 * hidden :]], axis=-1)
    outs = later[..., hidden : 2 * hidden]
    ins_got = swap(ins, "grp", bit)
    outs_got = swap(outs, "tp", 2)
    vectors = first[:, 3 * GROUP : 3 * GROUP + 6].T.astype(f32)
    gain_one, shift_one, proj_shift, gain_two, shift_two, out_shift = (
        vectors[i : i + 1] for i in range(6)
    )
    own = first[:, : 3 * GROUP]
    place = move.facts
    across = swap(own, "tp", 2)
    w_a = (own, swap(own, "tp", 1))
    x_got = move.arrange(x_got)


    rows, row = whole((ROWS, width)), whole((1, width))
    features = [
        pl.BlockSpec((1, PAIR, size, GROUP), lambda i, facts: (facts[1], 0, 0, 0))
        for size in (ALL_QUERIES, ALL_KEYS)
    ]
    bias_block = pl.BlockSpec((heads, KEYS, DIAG_PAD), lambda i, *_: (i, 0, 0))
    bias_scratch = pltpu.VMEM((heads, 2, KEYS, DIAG_PAD), f32)
    pair_columns = pl.BlockSpec((ROWS, GROUP), lambda i, *_: (0, i))
    query_block, key_block = chunk((PAIR, ALL_QUERIES, GROUP)), chunk((PAIR, ALL_KEYS, GROUP))
    lse_block = chunk((PAIR * heads, ALL_QUERIES))
    pair_specs = [query_block, key_block, key_block, pair_columns, lse_block]
    pair_shapes = [
        shaped((2, PAIR, ALL_QUERIES, GROUP), bf16),
        shaped((2, PAIR, ALL_KEYS, GROUP), bf16),
        shaped((2, PAIR, ALL_KEYS, GROUP), bf16),
        shaped((ROWS, 2 * GROUP), bf16),
        shaped((2, PAIR * heads, ALL_QUERIES)),
    ]
    w_block = whole((width, 3 * GROUP))
    w_specs = [w_block, w_block, chunk(split.shape[1:]), bias_block, *features]
    w_scratch = pltpu.VMEM((width, 3 * GROUP), bf16)
    attention_scratch = [
        w_scratch,
        pltpu.VMEM((ROWS, 3 * GROUP), f32),
        pltpu.VMEM((heads * ALL_KEYS, 2 * GROUP), bf16),
        pltpu.VMEM((heads * ALL_KEYS, ALL_QUERIES), f32),
        pltpu.VMEM((ALL_KEYS, ALL_QUERIES), bf16),
        pltpu.VMEM((ROWS, GROUP), f32),
        bias_scratch,
    ]
    x_rows, a1, a1_t, q_a, k_a, v_a, o_a, lse_a = pl.pallas_call(
        functools.partial(attention_kernel, True, move.frames),
        grid_spec=pltpu.PrefetchScalarGridSpec(
            num_scalar_prefetch=1,
            grid=(2,),
            in_specs=[whole(x_got.shape), row, row, *w_specs],
            out_specs=[rows, rows, whole((width, ROWS)), *pair_specs],
            scratch_shapes=[
                *attention_scratch, pltpu.VMEM((ROWS, width), f32),
            ],
        ),
        out_shape=[
            shaped((ROWS, width), bf16),
            shaped((ROWS, width), bf16),
            shaped((width, ROWS), bf16),
            *pair_shapes,
        ],
        compiler_params=room(60),
        cost_estimate=cost(12),
        name="attention",
    )(place, x_got, gain_one, shift_one, *after(w_a, ins, outs), split, bias_a, ours, theirs)
    ins_got, outs_got, across = after((ins_got, outs_got, across), a1)
    ins = join(ins, ins_got, bit, "grp", at).reshape(width, hidden + GROUP)
    outs = jnp.stack([outs, outs_got])
    far_ins = swap(ins, "tp", 2)
    outs_got = swap(outs, "grp", bit)
    g_send = move.before(after(grad_out, ins, outs, across))
    g_got = move.exchange(g_send)
    bias_b = bias_of(after(other_split, g_send))
    far_ins, outs_got = after((far_ins, outs_got), bias_b)
    outs = join(outs, outs_got, bit, "grp", at + 1).reshape(half, width, hidden)
    near_ins, last_ins = swap(ins, "tp", 1), swap(far_ins, "tp", 1)
    away_outs = swap(outs, "tp", 1)
    w_b = (across, swap(across, "tp", 1))
    q_b, k_b, v_b, o_b, lse_b = pl.pallas_call(
        functools.partial(attention_kernel, False, 0),
        grid_spec=pltpu.PrefetchScalarGridSpec(
            num_scalar_prefetch=1,
            grid=(2,),
            in_specs=[rows, *w_specs],
            out_specs=pair_specs,
            scratch_shapes=attention_scratch,
        ),
        out_shape=pair_shapes,
        compiler_params=room(60),
        cost_estimate=cost(11),
        name="attention",
    )(place, a1, *after(w_b, ins, far_ins, outs), other_split, bias_b, ours, theirs)

    g_got = move.arrange(g_got)
    both = whole((ROWS, 2 * GROUP))
    proj_block = whole((half, width, GROUP))
    keep_spec = pl.BlockSpec((1, width, hidden), lambda i, *_: (jnp.maximum(i - half, 0), 0, 0))
    send_spec = pl.BlockSpec((1, width, hidden), lambda i, *_: (jnp.minimum(i, half - 1), 0, 0))
    unit_spec = pl.BlockSpec(
        (1, 1, hidden), lambda i, *_: (jnp.where(i < half, 2 * i + 1, 2 * i - shares), 0, 0)
    )
    made = pl.pallas_call(
        functools.partial(mlp_kernel, move.frames),
        grid_spec=pltpu.PrefetchScalarGridSpec(
            num_scalar_prefetch=1,
            grid=(shares,),
            in_specs=[
                whole(g_got.shape), rows, both, both,
                *[whole((width, hidden + GROUP))] * shares,
                pl.BlockSpec((1, width, hidden), lambda i, *_: (jnp.maximum(i - half, 0), 0, 0)),
                pl.BlockSpec((1, width, hidden), lambda i, *_: (jnp.minimum(i, half - 1), 0, 0)),
                row, row, row, whole(split.shape), whole(split.shape), row,
            ],
            out_specs=[
                whole(move.shape(width)), rows, rows,
                keep_spec, send_spec, keep_spec, send_spec, proj_block,
                proj_block, unit_spec, whole((4, width)),
            ],
            scratch_shapes=[
                pltpu.VMEM((ROWS, width), f32),
                pltpu.VMEM((ROWS, width), bf16),
                pltpu.VMEM((width, ROWS), bf16),
                pltpu.VMEM((ROWS, width), bf16),
                pltpu.VMEM((width, ROWS), bf16),
                pltpu.VMEM((ROWS, width), f32),
                pltpu.VMEM((ROWS, 1), f32),
                pltpu.VMEM((ROWS, width), f32),
                pltpu.VMEM((ROWS, width), f32),
                pltpu.VMEM((ROWS, width), bf16),
                pltpu.VMEM((width, width), bf16),
                pltpu.VMEM((width, hidden), bf16),
                pltpu.VMEM((width, hidden), bf16),
                pltpu.VMEM((1, hidden), f32),
                pltpu.VMEM((ROWS, 256), f32),
                pltpu.VMEM((ROWS, 256), f32),
                pltpu.VMEM((ROWS, hidden), bf16),
                pltpu.VMEM((ROWS, hidden), bf16),
                pltpu.VMEM((width, hidden), bf16),
                pltpu.VMEM((width, hidden), bf16),
            ],
        ),
        out_shape=[
            shaped(move.shape(width), bf16),
            shaped((ROWS, width)),
            shaped((ROWS, width), bf16),
            shaped((half, width, hidden), bf16),
            shaped((half, width, hidden), bf16),
            shaped((half, width, hidden), bf16),
            shaped((half, width, hidden), bf16),
            shaped((half, width, GROUP), bf16),
            shaped((half, width, GROUP), bf16),
            shaped((shares, 1, hidden)),
            shaped((4, width)),
        ],
        compiler_params=room(60),
        cost_estimate=cost(22),
        name="mlp",
    )(
        place, g_got, x_rows, o_a, o_b, ins, near_ins, far_ins, last_ins, outs, away_outs,
        proj_shift, gain_two, shift_two, split, other_split, out_shift,
    )
    out_rows, dh, dow, in_keep, in_send, out_keep, out_send, proj_keep, proj_send, *made = made
    grad_in_shift, vec_two = made

    mine = jnp.concatenate(
        [
            plus(in_keep, swap(in_send, "tp", 1)),
            plus(out_keep, swap(out_send, "tp", 1)),
            plus(proj_keep, swap(proj_send, "tp", 1)),
        ],
        axis=-1,
    )
    far = mine[1]
    out_cells = move.leave(out_rows)
    out_got = move.exchange(out_cells)
    far_got = swap(far, "tp", 2)

    def back(pair, weights, given, extra, last):
        specs = [
            whole((width, ROWS)), w_block, w_block, query_block, key_block, key_block,
            pl.BlockSpec((ROWS, GROUP), lambda i, *_: (0, 2 * pair + i)),
            lse_block, bias_block, *features,
        ]
        specs += [whole(v.shape) for v in extra]
        made = [shaped((ROWS, width))]
        if last:
            made = [shaped(move.shape(width), bf16), shaped((2, width))]
        made_specs = [whole(v.shape) for v in made]
        made += [
            shaped((width, 3 * GROUP), bf16),
            shaped((width, 3 * GROUP), bf16),
            shaped((2, 1, 3 * GROUP)),
            shaped((2 * heads, KEYS, DIAG_PAD)),
        ]
        made_specs += [
            whole((width, 3 * GROUP)), whole((width, 3 * GROUP)), chunk((1, 3 * GROUP)), bias_block,
        ]
        scratch = [
            pltpu.VMEM((ROWS, width), f32),
            pltpu.VMEM((ROWS, 3 * GROUP), f32),
            w_scratch,
            pltpu.VMEM((ROWS, GROUP), f32),
            pltpu.VMEM((heads * ALL_KEYS, 2 * GROUP), bf16),
            pltpu.VMEM((heads * ALL_KEYS, GROUP), bf16),
            pltpu.VMEM((heads * ALL_KEYS, ALL_QUERIES), f32),
            pltpu.VMEM((heads * ALL_KEYS, ALL_QUERIES), f32),
            pltpu.VMEM((heads * ALL_KEYS, ALL_QUERIES), bf16),
            pltpu.VMEM((heads * ALL_KEYS, ALL_QUERIES), bf16),
            bias_scratch,
            bias_scratch,
        ]
        return pl.pallas_call(
            functools.partial(attention_back_kernel, last, move.frames),
            grid_spec=pltpu.PrefetchScalarGridSpec(
                num_scalar_prefetch=1,
                grid=(2,),
                in_specs=specs,
                out_specs=made_specs,
                scratch_shapes=scratch,
            ),
            out_shape=made,
            compiler_params=room(60),
            cost_estimate=cost(19),
            name="attention_back",
        )(place, a1_t, *weights, *given, ours, theirs, *extra)

    dow_b = after(dow, far, out_cells)
    running, keep_b, send_b, shift_b, sums_b = back(1, w_b, (q_b, k_b, v_b, dow_b, lse_b, bias_b), (), False)

    mine = plus(mine[0], after(far_got, keep_b))
    mine = split_rows(mine, 0)
    steps = list(reversed(bits_of("grp")))
    near_b = swap(send_b, "tp", 1)
    keep, send = halves(mine, 0, steps[0])
    got_first = swap(send, "grp", steps[0])
    out_part = after(out_got, keep_b)
    out_far = swap(out_part, "tp", 2)
    out_near = swap(out_part, "tp", 1)
    far_b = plus(keep_b, near_b)
    far_got_b = swap(far_b, "tp", 2)
    running = after(running, far_b, out_part, send)
    made = back(0, w_a, (q_a, k_a, v_a, dow, lse_a, bias_a), (running, x_rows, gain_one, dh), True)
    gx, vec_one, keep_a, send_a, shift_a, sums_a = made

    gx_cells = move.leave(after(gx, got_first, far_got_b))
    gx_got = move.exchange(gx_cells)
    out_far = after(out_far, gx_cells)
    near_a = swap(after(send_a, gx_cells), "tp", 1)

    def table_of(pair_sums):
        return pl.pallas_call(
            table_kernel,
            grid=(2,),
            in_specs=[bias_block, whole((PICK_ROWS, 256))],
            out_specs=pl.BlockSpec((heads, 1, TABLE_PAD), lambda i: (i, 0, 0)),
            out_shape=shaped((2 * heads, 1, TABLE_PAD)),
            scratch_shapes=[pltpu.VMEM((heads, KEYS, TABLE_PAD), f32)],
            compiler_params=room(60),
            cost_estimate=cost(6),
            name="table",
        )(pair_sums, pick)

    def rows_of(*parts):
        return jnp.concatenate([part.reshape(-1) for part in parts]).reshape(-1, 3 * GROUP)

    def slot(tables, shifts, which, in_slot):
        return (tables[which * heads : (which + 1) * heads], shifts[which], grad_in_shift[in_slot])

    tables_b = table_of(after(sums_b, gx_cells))
    tables_a = table_of(after(sums_a, tables_b))
    gx_part = after(gx_got, tables_a)
    gx_far = swap(gx_part, "tp", 2)
    gx_near = swap(gx_part, "tp", 1)
    keep, send = halves(plus(after(keep, gx_part), got_first), 0, steps[1])
    got_second = swap(send, "grp", steps[1])
    got_a = plus(plus(keep_a, near_a), far_got_b)
    got_a = split_rows(got_a, 0)
    vec = rows_of(vec_one, vec_two)
    small = rows_of(vec, *slot(tables_a, shift_a, 0, 0), *slot(tables_b, shift_b, 0, 2))
    sent = rows_of(vec, *slot(tables_a, shift_a, 1, 1), *slot(tables_b, shift_b, 1, 3))
    small = small + swap(sent, "tp", 1)
    lead = vec.shape[0]
    cut = lead + (small.shape[0] - lead) // 2
    small = small[:cut] + swap(jnp.concatenate([small[:lead], small[cut:]]), "tp", 2)
    tail = small
    output = (out_part, out_near, out_far, swap(after(out_far, tail), "tp", 1))
    output = move.home(output, 0, None, bf16, 3)
    grad_tokens = move.home((gx_part, after(gx_near, tail)), 0, None, f32, 0.1)
    mine = plus(keep, after(got_second, output))
    for bit in steps[2:]:
        keep, send = halves(mine, 0, bit)
        mine = plus(keep, swap(send, "grp", bit))
    mine = mine.reshape(depth, 2 * hidden + GROUP).astype(f32)

    last = swap(after(gx_far, grad_tokens), "tp", 1)
    final = move.home((gx_far, last), 2, grad_tokens, f32, 0.1)

    for i, bit in enumerate(steps):
        keep, send = halves(got_a, 0, bit)
        high = lax.reduce_precision(small, 8, 7)
        low = (small - high).astype(bf16)
        size = send.size // (3 * GROUP)
        sent = jnp.concatenate([send.reshape(size, 3 * GROUP), high.astype(bf16), low])
        if i == 0:
            sent = after(sent, gx_far, grad_tokens)
        got = swap(sent, "grp", bit)
        if i == len(steps) - 1:
            got = after(got, final)
        got_a = plus(keep, got[:size].reshape(keep.shape))
        got = got[size:].astype(f32)
        small = small + got[:cut] + got[cut:]
    got_a = got_a.reshape(depth, 3, GROUP).astype(f32)
    vec = small[:lead].reshape(6, width)
    vec = lax.dynamic_slice_in_dim(vec, lax.axis_index("grp") * depth, depth, 1)
    small = small[lead:].reshape(-1)
    got_table = small[: heads * TABLE_PAD].reshape(heads, TABLE_PAD)[:, :TABLE].T
    got_shift = small[heads * TABLE_PAD :][: 3 * GROUP].reshape(3, GROUP)
    got_in_shift = small[heads * TABLE_PAD + 3 * GROUP :]

    return (
        output,
        final,
        vec[0],
        vec[1],
        got_a,
        jnp.stack([got_shift[0], got_shift[2]]),
        got_table,
        mine[:, 2 * hidden :],
        vec[4],
        vec[2],
        vec[3],
        mine[:, :hidden],
        got_in_shift,
        mine[:, hidden : 2 * hidden],
        vec[5],
    )


def solution(mesh):
    shard = P("grp")
    tokens = P(None, "grp", None)
    placed = (
        tokens, tokens, shard, shard, P("grp", None, "tp"), P(None, "tp"), P(None, "tp"),
        P("grp", "tp"), shard, shard, shard, P("grp", "tp"), P("tp"), P("grp", "tp"), shard,
    )
    return jax.shard_map(
        per_device, mesh=mesh, in_specs=placed, out_specs=placed, check_vma=False
    )
```
